32 devices in a mesh: seq: 4 (over z), shard: 8 (over y, x, core).
Axes of the slice: x: 2, y: 2, z: 4, core: 2. Of those that a mesh axis runs over, the one named last changes fastest.
Arguments:
- tokens: bfloat16 [2, 8, 1024, 768], P(None, 'shard', 'seq'), may hold values from -6 to 6
- segments: int32 [2, 8, 1024], P(None, 'shard', 'seq'), may hold values from 0 to 3, never falling along the last dimension, each value on 1 to 512 neighbouring positions
- w_qkv: bfloat16 [768, 2304], P('shard'), may hold values from -0.21875 to 0.21875
- w_out: bfloat16 [768, 768], P('shard'), may hold values from -2.5 to 2.5
- w_up: bfloat16 [768, 3072], P('shard'), may hold values from -0.21875 to 0.21875
- w_down: bfloat16 [3072, 768], P('shard'), may hold values from -0.109375 to 0.109375
- gain_one: bfloat16 [768], P('shard'), may hold values from 0.5 to 1.5
- gain_two: bfloat16 [768], P('shard'), may hold values from 0.5 to 1.5
- cotangent: bfloat16 [2, 8, 1024, 768], P(None, 'shard', 'seq'), may hold values from -6 to 6
Outputs:
- mixed: bfloat16 [2, 8, 1024, 768], P(None, 'shard', 'seq')
- grad_tokens: float32 [2, 8, 1024, 768], P(None, 'shard', 'seq')
- grad_qkv: float32 [768, 2304], P('shard')
- grad_out: float32 [768, 768], P('shard')
- grad_up: float32 [768, 3072], P('shard')
- grad_down: float32 [3072, 768], P('shard')
- grad_gain_one: float32 [768], P('shard')
- grad_gain_two: float32 [768], P('shard')
The draws below stay inside these ranges and needn't reach their ends.
Inputs may be any that keep to these rules, and one draw needn't show every extreme that they name: `segments`: within a sequence the ids never decrease; a document spans at most half of 1024 tokens.
All inputs are finite; a program needn't handle non-finite values.
Results may differ from the reference program's by a relative error of at most 0.012.
The reference program's roundings to bfloat16 on the way count: a program that leaves them out, or rounds other values in their place, can miss the bound.
Values may be sent and summed in bfloat16 or wider, within the bound.
A program may use at most 192 MiB of HBM per device.

```python
import math
import jax
import jax.numpy as jnp
import numpy as np
from jax import lax

D = 768
HEADS = 12
HEAD_DIM = 64
FF = 3072
MICRO = 2
SEGMENTS = 4
LENGTH = 1024
SEQS = 8


def with_spikes(drawn, stream_key, source, target, parts, factor):
    owner, partner = [(jnp.arange(drawn.shape[position]) // (drawn.shape[position] // parts)).reshape([-1 if axis == position else 1 for axis in range(drawn.ndim)]) for position in (source, target)]
    chosen = jax.random.permutation(stream_key, parts)[partner]
    strong = (owner == chosen) | (owner == (partner + parts // 2) % parts)
    return jnp.where(strong, factor * drawn, drawn)


def levels(stream_key, shape, split, smallest, largest):
    factor_of = 1.0
    for position, blocks in split:
        heights = jax.random.uniform(jax.random.fold_in(jax.random.fold_in(stream_key, 6), position), (blocks,), jnp.float32, smallest / len(split), largest / len(split))
        factor_of = factor_of * jnp.repeat(jnp.exp(heights), shape[position] // blocks).reshape((-1,) + (1,) * (len(shape) - 1 - position))
    return factor_of


def profile(count, total, reach, slope):
    portions = [(1 << 20) // math.isqrt(standing ** slope) + 1 for standing in range(2, count + 1)]
    spare, counts = total - reach - (count - 1), [1] * (count - 1)
    while spare > 0:
        movable = [i for i in range(count - 1) if counts[i] < reach]
        pool, left = sum([portions[i] for i in movable]), spare
        for i in movable:
            addition = min(reach - counts[i], max(1, left * portions[i] // pool), spare)
            counts[i] = counts[i] + addition
            spare = spare - addition
    return np.array([reach] + counts)


def uneven(own_key, number_of, total, limit, skew):
    if number_of == 2:
        one = jax.random.randint(own_key, (), max(1, total - limit), min(limit, total - 1) + 1)
        return jnp.stack([one, total - one])
    lengths = jnp.asarray(profile(number_of, total, limit, skew), jnp.int32)
    twos = (number_of - 1) // 2
    giver, sink = lengths[1:1 + 2 * twos:2], lengths[2:2 + 2 * twos:2]
    room = jnp.minimum(giver - 1, limit - sink)
    passed = jax.random.randint(jax.random.fold_in(own_key, 1), (twos,), 0, 1 << 20) % (room + 1)
    lengths = lengths.at[1:1 + 2 * twos:2].set(giver - passed).at[2:2 + 2 * twos:2].set(sink + passed)
    return lengths[jax.random.permutation(jax.random.fold_in(own_key, 2), number_of)]


def normal_values(own_key, shape, width, limit, shards=(), kind=jnp.bfloat16):
    drawn = jax.random.normal(own_key, shape, jnp.float32) * width
    if len(shards) > 0:
        drawn = levels(own_key, shape, shards, -0.22, 0.18) * drawn
    return jnp.clip(drawn, min=-limit, max=limit).astype(kind)


def heavy_noise(rng, extent, deviation, limit, pieces, heavy, kind=jnp.bfloat16):
    values = deviation * jax.random.normal(rng, extent, jnp.float32)
    if pieces:
        values = values * levels(rng, extent, pieces, -0.22, 0.18)
    return jnp.clip(with_spikes(values, jax.random.fold_in(rng, 3), *heavy), -limit, limit).astype(kind)


def setup_inputs(seed: int = 0) -> dict:
    key_list = jax.random.split(jax.random.key(seed), 10)
    tokens = heavy_noise(key_list[0], (MICRO, SEQS, LENGTH, D), 1.0, 6.0, ((1, 8), (2, 4)), (1, 3, 8, 2.0))
    segments = jax.vmap(lambda own: jnp.searchsorted(jnp.cumsum(uneven(own, SEGMENTS, LENGTH, LENGTH // 2, 2)), jnp.arange(LENGTH), side="right"))(jax.random.split(key_list[1], MICRO * SEQS)).reshape((MICRO, SEQS, LENGTH)).astype(jnp.int32)
    w_qkv = normal_values(key_list[2], (D, 3 * D), D ** -0.5, 0.21875, ((0, 8),))
    w_out = normal_values(key_list[3], (D, D), (max(D // 128, 1)) ** -0.5, 2.5, ((0, 8),))
    w_up = normal_values(key_list[4], (D, FF), D ** -0.5, 0.21875, ((0, 8),))
    w_down = normal_values(key_list[5], (FF, D), FF ** -0.5, 0.109375, ((0, 8),))
    gain_one = jnp.clip(1.0 + 0.1 * jax.random.normal(key_list[6], (D,), jnp.float32), 0.5, 1.5).astype(jnp.bfloat16)
    gain_two = jnp.clip(1.0 + 0.1 * jax.random.normal(key_list[7], (D,), jnp.float32), 0.5, 1.5).astype(jnp.bfloat16)
    cotangent = normal_values(key_list[8], (MICRO, SEQS, LENGTH, D), 1.0, 6.0, ((1, 8), (2, 4)))
    return {"tokens": tokens, "segments": segments, "w_qkv": w_qkv, "w_out": w_out, "w_up": w_up, "w_down": w_down, "gain_one": gain_one, "gain_two": gain_two, "cotangent": cotangent}


@jax.custom_vjp
def low(v):
    return lax.optimization_barrier(v.astype(jnp.bfloat16)).astype(jnp.float32)

@jax.custom_vjp
def low_back(v):
    return v

def low_keep(v):
    return (low(v), None)

def low_pass(kept, grad):
    return (grad,)

def back_keep(v):
    return (v, None)

def back_low(kept, grad):
    return (low(grad),)
low.defvjp(low_keep, low_pass)
low_back.defvjp(back_keep, back_low)
epsilon = 1e-05
far_below = -1e+30
highest = lax.Precision.HIGHEST

def norm_rows(values, gain):
    row_mean = lax.optimization_barrier(jnp.mean(values, axis=-1, keepdims=True))
    centred = values - row_mean
    spread = lax.optimization_barrier(jnp.mean(centred * centred, axis=-1, keepdims=True))
    return centred * lax.rsqrt(spread + epsilon) * gain

def matrix(left, right):
    return jnp.dot(left, right, precision=highest)

def layer(params, tokens_f, seg_ids):
    w_qkv, w_out, w_up, w_down, gain_one, gain_two = params
    length = tokens_f.shape[0]
    score_scale = HEAD_DIM ** (-0.5)
    normed = low(norm_rows(tokens_f, gain_one))
    packed = low(low_back(matrix(normed, w_qkv)))
    queries = packed[:, :D].reshape(length, HEADS, HEAD_DIM)
    keys = packed[:, D:2 * D].reshape(length, HEADS, HEAD_DIM)
    values = packed[:, 2 * D:].reshape(length, HEADS, HEAD_DIM)
    scores = low_back(jnp.einsum('qhd,khd->hqk', queries, keys, precision=highest) * score_scale)
    positions = jnp.arange(length, dtype=jnp.int32)
    allowed = (positions[None, :] <= positions[:, None]) & (seg_ids[None, :] == seg_ids[:, None])
    allowed = allowed[None]
    magnitude = jnp.abs(scores)
    row_top = lax.optimization_barrier(jnp.max(jnp.where(allowed, magnitude, far_below), axis=-1, keepdims=True))
    exp_raw = jnp.where(allowed, jnp.exp(magnitude - row_top), 0.0)
    total = lax.optimization_barrier(jnp.sum(exp_raw, axis=-1, keepdims=True))
    floor_term = jnp.where(allowed, jnp.exp(-row_top), 0.0)
    signed = low(jnp.sign(scores) * (exp_raw - floor_term) / total)
    heads_out = jnp.einsum('hqk,khd->qhd', signed, values, precision=highest).reshape(length, D)
    attended = low_back(low(heads_out))
    branch = low_back(matrix(attended, w_out))
    middle = tokens_f + branch
    normed_two = low(norm_rows(middle, gain_two))
    up_pre = low_back(matrix(normed_two, w_up))
    active = low(jax.nn.gelu(up_pre, approximate=True))
    down = low_back(matrix(active, w_down))
    return middle + down

def reference(tokens, segments, w_qkv, w_out, w_up, w_down, gain_one, gain_two, cotangent):
    params = (w_qkv.astype(jnp.float32), w_out.astype(jnp.float32), w_up.astype(jnp.float32), w_down.astype(jnp.float32), gain_one.astype(jnp.float32), gain_two.astype(jnp.float32))
    number = MICRO * SEQS
    flat_tokens = tokens.astype(jnp.float32).reshape(number, LENGTH, D)
    flat_segments = segments.reshape(number, LENGTH)
    flat_cot = cotangent.astype(jnp.float32).reshape(number, LENGTH, D)

    def one_step(totals, item):
        tokens_f, seg_ids, cot_f = item

        def forward(weights, inputs):
            return layer(weights, inputs, seg_ids)
        result, pull = jax.vjp(forward, params, tokens_f)
        grad_params, grad_inputs = pull(cot_f)
        totals = tuple((left_term + right_term for left_term, right_term in zip(totals, grad_params)))
        return (totals, (result.astype(jnp.bfloat16), grad_inputs))
    zeros = tuple((jnp.zeros(weight.shape, jnp.float32) for weight in params))
    totals, outputs = lax.scan(one_step, zeros, (flat_tokens, flat_segments, flat_cot))
    results, grads = outputs
    return (results.reshape(tokens.shape), grads.reshape(tokens.shape), totals[0], totals[1], totals[2], totals[3], totals[4], totals[5])
```

```python
import functools
import math

import jax
import jax.numpy as jnp
from jax import lax
from jax.experimental import pallas as pl
from jax.experimental.pallas import tpu as pltpu
from jax.sharding import PartitionSpec as P


HEADS = 12
HEAD_DIM = 64


epsilon = 1e-05
far_below = -1e30


def norm_rows(values, gain):
    row_mean = jnp.mean(values, axis=-1, keepdims=True)
    centred = values - row_mean
    spread = jnp.mean(centred * centred, axis=-1, keepdims=True)
    return centred * lax.rsqrt(spread + epsilon) * gain


def gelu_tanh(values):
    return jax.nn.gelu(values, approximate=True)


def product(left, right):
    return jnp.dot(left, right, preferred_element_type=jnp.float32)


def product_left_t(left, right):
    return lax.dot_general(
        left, right, (((0,), (0,)), ((), ())), preferred_element_type=jnp.float32
    )


def product_right_t(left, right):
    return lax.dot_general(
        left, right, (((1,), (1,)), ((), ())), preferred_element_type=jnp.float32
    )


def block_scores(query_block, keys, seg_rows, seg_cols, row_first, score_scale):
    rows_count = query_block.shape[0]
    cols_count = keys.shape[0]
    scores = (
        jnp.einsum("qhd,khd->hqk", query_block, keys, preferred_element_type=jnp.float32)
        * score_scale
    )
    row_pos = row_first + lax.broadcasted_iota(jnp.int32, (rows_count, cols_count), 0)
    col_pos = lax.broadcasted_iota(jnp.int32, (rows_count, cols_count), 1)
    allowed = (col_pos <= row_pos) & (seg_rows[:, None] == seg_cols[None, :])
    return (scores, allowed[None])


def attend_forward(queries, keys, values, seg_all, rows_block, score_scale):
    length = queries.shape[0]
    out_parts = []
    level_parts = []
    for row_first in range(0, length, rows_block):
        query_block = queries[row_first : row_first + rows_block]
        scores, allowed = block_scores(
            query_block,
            keys,
            seg_all[row_first : row_first + rows_block],
            seg_all,
            row_first,
            score_scale,
        )
        magnitude = jnp.abs(scores)
        row_top = jnp.max(jnp.where(allowed, magnitude, far_below), axis=-1, keepdims=True)
        exp_raw = jnp.where(allowed, jnp.exp(magnitude - row_top), 0.0)
        total = jnp.sum(exp_raw, axis=-1, keepdims=True)
        floor_term = jnp.where(allowed, jnp.exp(-row_top), 0.0)
        signed = (jnp.sign(scores) * (exp_raw - floor_term) / total).astype(jnp.bfloat16)
        out_parts.append(
            jnp.einsum("hqk,khd->qhd", signed, values, preferred_element_type=jnp.float32)
        )
        level_parts.append(row_top + jnp.log(total))
    return (jnp.concatenate(out_parts, axis=0), jnp.concatenate(level_parts, axis=1))


def attend_backward(queries, keys, values, seg_all, levels, d_heads, rows_block, score_scale):
    length = queries.shape[0]
    grad_keys = jnp.zeros(keys.shape, jnp.float32)
    grad_values = jnp.zeros(values.shape, jnp.float32)
    query_parts = []
    for row_first in range(0, length, rows_block):
        query_block = queries[row_first : row_first + rows_block]
        d_block = d_heads[row_first : row_first + rows_block]
        scores, allowed = block_scores(
            query_block,
            keys,
            seg_all[row_first : row_first + rows_block],
            seg_all,
            row_first,
            score_scale,
        )
        level_block = levels[:, row_first : row_first + rows_block]
        sign_part = jnp.sign(scores)
        prob = jnp.where(allowed, jnp.exp(jnp.abs(scores) - level_block), 0.0)
        weight = sign_part * jnp.where(allowed, prob - jnp.exp(-level_block), 0.0)
        d_signed = jnp.einsum("qhd,khd->hqk", d_block, values, preferred_element_type=jnp.float32)
        delta = jnp.sum(weight * d_signed, axis=-1, keepdims=True)
        d_score = (prob * (d_signed - sign_part * delta)).astype(jnp.bfloat16)
        query_parts.append(
            jnp.einsum("hqk,khd->qhd", d_score, keys, preferred_element_type=jnp.float32)
            * score_scale
        )
        grad_keys = (
            grad_keys
            + jnp.einsum("hqk,qhd->khd", d_score, query_block, preferred_element_type=jnp.float32)
            * score_scale
        )
        grad_values = grad_values + jnp.einsum(
            "hqk,qhd->khd", weight.astype(jnp.bfloat16), d_block, preferred_element_type=jnp.float32
        )
    grad_queries = jnp.concatenate(query_parts, axis=0)
    stacked = jnp.stack([grad_queries, grad_keys, grad_values], axis=1)
    heads_dev = queries.shape[1]
    return stacked.astype(jnp.bfloat16).reshape(length, 3, 1, heads_dev * queries.shape[2])


def per_device(tokens, segments, w_qkv, w_out, w_up, w_down, gain_one, gain_two, cotangent):
    micro_count = tokens.shape[0]
    tok_rows = tokens.shape[2]
    width = tokens.shape[3]
    groups = lax.axis_size("seq")
    heads_dev = HEADS // groups
    head_cols = heads_dev * HEAD_DIM
    length = tok_rows * groups
    rows_block = min(512, length)
    score_scale = HEAD_DIM ** (-0.5)
    totals = None
    shares = None
    results = []
    grad_rows = []
    for micro_idx in range(micro_count):
        whole = (
            lax.all_gather(w_qkv, "shard", axis=0, tiled=True),
            lax.all_gather(w_out, "shard", axis=0, tiled=True),
            lax.all_gather(w_up, "shard", axis=0, tiled=True),
            lax.all_gather(w_down, "shard", axis=0, tiled=True),
            lax.all_gather(gain_one, "shard", axis=0, tiled=True),
            lax.all_gather(gain_two, "shard", axis=0, tiled=True),
        )
        full_qkv, full_out, full_up, full_down = (whole[0], whole[1], whole[2], whole[3])
        gain_first = whole[4].astype(jnp.float32)
        gain_second = whole[5].astype(jnp.float32)
        tokens_f = tokens[micro_idx, 0].astype(jnp.float32)
        seg_local = segments[micro_idx, 0].astype(jnp.bfloat16)
        normed = norm_rows(tokens_f, gain_first).astype(jnp.bfloat16)
        packed = (
            product(normed, full_qkv).astype(jnp.bfloat16).reshape(tok_rows, 3, groups, head_cols)
        )
        seg_tile = jnp.broadcast_to(seg_local[:, None, None, None], (tok_rows, 1, groups, 1))
        received, seg_recv = (
            lax.all_to_all(packed, "seq", split_axis=2, concat_axis=0, tiled=True),
            lax.all_to_all(seg_tile, "seq", split_axis=2, concat_axis=0, tiled=True),
        )
        queries = received[:, 0, 0].reshape(length, heads_dev, HEAD_DIM)
        keys = received[:, 1, 0].reshape(length, heads_dev, HEAD_DIM)
        values = received[:, 2, 0].reshape(length, heads_dev, HEAD_DIM)
        seg_all = seg_recv[:, 0, 0, 0]
        heads_out, levels = attend_forward(queries, keys, values, seg_all, rows_block, score_scale)
        heads_low = heads_out.astype(jnp.bfloat16).reshape(length, 1, head_cols)
        attended = lax.all_to_all(
            heads_low, "seq", split_axis=0, concat_axis=1, tiled=True
        ).reshape(tok_rows, width)
        middle = tokens_f + product(attended, full_out)
        normed_two = norm_rows(middle, gain_second).astype(jnp.bfloat16)
        up_pre = product(normed_two, full_up)
        active = gelu_tanh(up_pre).astype(jnp.bfloat16)
        results.append((middle + product(active, full_down)).astype(jnp.bfloat16))
        again = (
            lax.all_gather(w_qkv, "shard", axis=0, tiled=True),
            lax.all_gather(w_out, "shard", axis=0, tiled=True),
            lax.all_gather(w_up, "shard", axis=0, tiled=True),
            lax.all_gather(w_down, "shard", axis=0, tiled=True),
            lax.all_gather(gain_one, "shard", axis=0, tiled=True),
            lax.all_gather(gain_two, "shard", axis=0, tiled=True),
        )
        back_qkv, back_out, back_up, back_down = (again[0], again[1], again[2], again[3])
        cot_low = cotangent[micro_idx, 0]
        grad_down_term = product_left_t(active, cot_low)
        d_active = product_right_t(cot_low, back_down)
        unused_gelu, gelu_pull = jax.vjp(gelu_tanh, up_pre)
        d_up = gelu_pull(d_active)[0].astype(jnp.bfloat16)
        grad_up_term = product_left_t(normed_two, d_up)
        d_norm_two = product_right_t(d_up, back_up)
        unused_second, second_pull = jax.vjp(norm_rows, middle, gain_second)
        d_middle_norm, grad_gain_two_term = second_pull(d_norm_two)
        d_middle = cot_low.astype(jnp.float32) + d_middle_norm
        d_branch = d_middle.astype(jnp.bfloat16)
        grad_out_term = product_left_t(attended, d_branch)
        d_attended = (
            product_right_t(d_branch, back_out)
            .astype(jnp.bfloat16)
            .reshape(tok_rows, groups, head_cols)
        )
        d_heads = lax.all_to_all(d_attended, "seq", split_axis=1, concat_axis=0, tiled=True)
        d_heads = d_heads[:, 0].reshape(length, heads_dev, HEAD_DIM)
        grad_heads = attend_backward(
            queries, keys, values, seg_all, levels, d_heads, rows_block, score_scale
        )
        d_packed = lax.all_to_all(
            grad_heads, "seq", split_axis=0, concat_axis=2, tiled=True
        ).reshape(tok_rows, 3 * width)
        grad_qkv_term = product_left_t(normed, d_packed)
        d_normed = product_right_t(d_packed, back_qkv)
        unused_first, first_pull = jax.vjp(norm_rows, tokens_f, gain_first)
        d_tokens_norm, grad_gain_one_term = first_pull(d_normed)
        grad_rows.append(d_middle + d_tokens_norm)
        terms = (
            grad_qkv_term,
            grad_out_term,
            grad_up_term,
            grad_down_term,
            grad_gain_one_term,
            grad_gain_two_term,
        )
        if totals is None:
            totals = terms
        else:
            totals = tuple((left_term + right_term for left_term, right_term in zip(totals, terms)))
    shares = (
        lax.psum_scatter(totals[0], "shard", scatter_dimension=0, tiled=True),
        lax.psum_scatter(totals[1], "shard", scatter_dimension=0, tiled=True),
        lax.psum_scatter(totals[2], "shard", scatter_dimension=0, tiled=True),
        lax.psum_scatter(totals[3], "shard", scatter_dimension=0, tiled=True),
        lax.psum_scatter(totals[4], "shard", scatter_dimension=0, tiled=True),
        lax.psum_scatter(totals[5], "shard", scatter_dimension=0, tiled=True),
    )
    replicas = lax.psum((shares[0], shares[1], shares[2], shares[3], shares[4], shares[5]), "seq")
    mixed = jnp.stack(results, axis=0)[:, None]
    grad_tokens = jnp.stack(grad_rows, axis=0)[:, None]
    return (
        mixed,
        grad_tokens,
        replicas[0],
        replicas[1],
        replicas[2],
        replicas[3],
        replicas[4],
        replicas[5],
    )


BF = jnp.bfloat16
F32 = jnp.float32
MESH = pl.DeviceIdType.MESH
N_SEMS = 192
HUGE = 3.0e38
GELU_K = math.sqrt(2.0 / math.pi)
GELU_C = 0.044715
LANES = 128


def nt(left, right, precision=None):
    return lax.dot_general(
        left, right, (((1,), (1,)), ((), ())), preferred_element_type=F32, precision=precision
    )


def tn(left, right):
    return lax.dot_general(left, right, (((0,), (0,)), ((), ())), preferred_element_type=F32)


def nn(left, right, precision=None):
    return jnp.dot(left, right, preferred_element_type=F32, precision=precision)


def row_stats(v):
    mean = jnp.mean(v, axis=-1, keepdims=True)
    cen = v - mean
    var = jnp.mean(cen * cen, axis=-1, keepdims=True)
    return cen, lax.rsqrt(var + epsilon)


def norm_back(dn, n, rstd, gain):
    e = dn * gain
    return (e - jnp.mean(e, axis=-1, keepdims=True) - n * jnp.mean(e * n, axis=-1, keepdims=True)) * rstd


def layer_kernel(names, *refs):
    r = dict(zip(names, refs))
    tok, seg, wqkv, wout, wup, wdn, gpl, cot = (
        r[k] for k in ("tok", "seg", "wqkv", "wout", "wup", "wdn", "gpl", "cot")
    )
    ssem, rsem = r["ssem"], r["rsem"]
    width = tok.shape[2]
    quarter = tok.shape[1]
    half = 2 * quarter
    length = 4 * quarter
    rows_dev = wqkv.shape[0]
    rows_chip = 2 * rows_dev
    hcols = width // 2
    pairs = hcols // LANES
    pcols = 3 * LANES
    ffh = wup.shape[1] // 2
    ffb = wdn.shape[0]

    z = lax.axis_index("seq")
    s = lax.axis_index("shard")
    c = lax.rem(s, 2)
    q = lax.div(s, 2)
    x = lax.rem(q, 2)
    y = lax.div(q, 2)
    part = (z, s + 1 - 2 * c)
    nx = (z, s + 2 - 4 * x)
    ny = (z, s + 4 - 8 * y)
    zp = (z + 1 - 2 * lax.rem(z, 2), s)
    zm = (3 - z, s)
    edge = lax.rem(z, 3) == 0
    mid = lax.rem(z, 3) != 0
    qx = q + 1 - 2 * x
    qy = q + 2 - 4 * y
    zh = lax.div(z, 2)
    zk = lax.rem(z, 2)
    own0 = pl.multiple_of(half * c, half)
    oth0 = pl.multiple_of(half * (1 - c), half)

    used = [0]
    ends = []

    def sems(n=1):
        first = used[0]
        used[0] += n
        return first

    def remote(src, dst, i, dev, j=None):
        return pltpu.make_async_remote_copy(
            src_ref=src,
            dst_ref=dst,
            send_sem=ssem.at[i if j is None else j],
            recv_sem=rsem.at[i],
            device_id=dev,
            device_id_type=MESH,
        )

    def send(src, dst, dev):
        copy = remote(src, dst, sems(), dev)
        copy.start()
        ends.append(copy.wait_send)
        return copy

    def wait_in(ref, i):
        pltpu.make_async_copy(ref, ref, rsem.at[i]).wait()

    def rows(ref, start, n, align=16):
        return ref.at[pl.ds(pl.multiple_of(start, align), n), :]

    peers = [part, nx, ny]
    for dz in range(1, 4):
        zz = lax.rem(z + dz, 4)
        peers += [(zz, s), (zz, s + 1 - 2 * c)]
    bar = pltpu.get_barrier_semaphore()
    for dev in peers:
        pl.semaphore_signal(bar, inc=1, device_id=dev, device_id_type=MESH)
    pl.semaphore_wait(bar, len(peers))

    seg_i = sems(4)
    x_i = sems(2)
    c_i = sems(2)

    def to_chip(src, dst, i_recv, i_send, zd, core):
        is_self = (zd == z) & (core == c)
        dev = (zd, s - c + core)

        @pl.when(is_self)
        def _():
            pltpu.make_async_copy(src, dst, rsem.at[i_recv]).start()

        @pl.when(jnp.logical_not(is_self))
        def _():
            remote(src, dst, i_recv, dev, i_send).start()

        def end():
            @pl.when(jnp.logical_not(is_self))
            def _():
                remote(src, dst, i_recv, dev, i_send).wait_send()

        ends.append(end)

    for m in range(2):
        for core in range(2):
            to_chip(seg.at[m], r["segs"].at[z], seg_i + z, seg_i + 2 * m + core, 2 * m + c, core)
    for m in range(2):
        to_chip(tok.at[m], rows(r["xb"], quarter * zk, quarter), x_i + zk, x_i + m, 2 * m + c, zh)

    my = pl.multiple_of(rows_dev * s, 32)
    local_q, local_o, local_u, local_d = sems(), sems(), sems(), sems()
    flip_q, flip_o, flip_u = sems(), sems(), sems()
    W = {"q": r["w_q"], "o": r["w_o"], "u": r["w_u"], "d": r["w_d"]}

    def dcol(start, n):
        return pl.ds(pl.multiple_of(start, LANES), n)

    def pieces_q(core):
        for t in range(3):
            for p in range(pairs):
                yield wqkv.at[:, dcol(t * width + core * hcols + p * LANES, LANES)], W["q"].at[
                    pl.ds(my, rows_dev), pl.ds(p * pcols + t * LANES, LANES)
                ]

    def pieces_o(core):
        yield wout.at[:, dcol(core * hcols, hcols)], W["o"].at[
            pl.ds(my, rows_dev), dcol(core * hcols, hcols)
        ]

    def pieces_u(core):
        for j in range(4):
            yield wup.at[:, dcol((2 * j + core) * ffb, ffb)], W["u"].at[
                pl.ds(my, rows_dev), pl.ds(j * ffb, ffb)
            ]

    for pieces, i_local, i_flip in (
        (pieces_q, local_q, flip_q),
        (pieces_o, local_o, flip_o),
        (pieces_u, local_u, flip_u),
    ):
        for src, dst in pieces(1 - c):
            remote(src, dst, i_flip, part).start()
        for src, dst in pieces(c):
            pltpu.make_async_copy(src, dst, rsem.at[i_local]).start()
    pltpu.make_async_copy(wdn, rows(W["d"], ffb * q, ffb), rsem.at[local_d]).start()
    gains = r["gains"]
    g_core = send(gpl, gains.at[0], part)
    for m in range(2):
        to_chip(cot.at[m], rows(r["cb"], quarter * z, quarter), c_i + zk, c_i + m, 2 * m + c, zh)

    partner_rows = pl.ds(pl.multiple_of(part[1] * rows_dev, 32), rows_dev)
    my_rows = pl.ds(my, rows_dev)

    def whole(name):
        if name == "o":
            return (my_rows, dcol(c * hcols, hcols)), (partner_rows, dcol(c * hcols, hcols))
        return (my_rows, slice(None)), (partner_rows, slice(None))

    def flip_done(name, i_local, i_flip):
        mine, his = whole(name)
        wait_in(W[name].at[mine], i_local)
        wait_in(W[name].at[his], i_flip)

        def end():
            copy = remote(W[name].at[mine], W[name].at[mine], i_flip, part)
            copy.wait_send()

        ends.append(end)

    def cols_of(name):
        return dcol(c * hcols, hcols) if name == "o" else slice(None)

    def block(name, first, n):
        return W[name].at[pl.ds(pl.multiple_of(first, 32), n), cols_of(name)]

    ag = {}

    def ag_first(name):
        n = ffb if name == "d" else rows_chip
        dst = block(name, n * q, n)
        src = wdn if name == "d" else dst
        ag[name] = (send(src, dst, nx), send(src, dst, ny))

    def ag_second(name):
        n = (ffb if name == "d" else rows_chip) // 2
        cx, cy = ag[name]
        cx.wait_recv()
        bx = block(name, 2 * n * qx, n)
        by = block(name, 2 * n * qy + n, n)
        fy = send(bx, bx, ny)
        cy.wait_recv()
        fx = send(by, by, nx)
        ag[name] = (fx, fy)

    def ag_last(name):
        for copy in ag[name]:
            copy.wait_recv()

    flip_done("q", local_q, flip_q)
    ag_first("q")
    g_core.wait_recv()
    gains[1] = gpl[...] + gains[0]
    g_x = send(gains.at[1], gains.at[2], nx)
    flip_done("o", local_o, flip_o)
    flip_done("u", local_u, flip_u)
    g_x.wait_recv()
    gains[3] = gains[1] + gains[2]
    g_y = send(gains.at[3], gains.at[4], ny)
    ag_second("q")
    ag_first("o")
    ag_first("u")
    g_y.wait_recv()
    gains[5] = gains[3] + gains[4]
    gain_one = gains[5][:, :width]
    gain_two = gains[5][:, width:]

    xb, normed = r["xb"], r["normed"]
    for k in range(2):
        wait_in(rows(xb, quarter * k, quarter), x_i + k)
        cen, rstd = row_stats(xb[pl.ds(quarter * k, quarter), :].astype(F32))
        normed[pl.ds(own0 + quarter * k, quarter), :] = (cen * rstd * gain_one).astype(BF)
    n_copy = send(rows(normed, own0, half), rows(normed, own0, half), part)

    segs, segc, mask = r["segs"], r["segc"], r["mask"]
    for b in range(4):
        wait_in(segs.at[b], seg_i + b)
    for b in range(4):
        tile = jnp.broadcast_to(segs[b].astype(F32), (LANES, quarter))
        segc[pl.ds(quarter * b, quarter), :] = jnp.transpose(tile)
    base = []
    at = 0
    for b in range(4):
        k0 = max(0, b - 2)
        base.append((at, k0, (b - k0 + 1) * quarter))
        for kb in range(k0, b + 1):
            col = segc[pl.ds(quarter * kb, quarter), :]
            same = jnp.concatenate([col] * (quarter // LANES), axis=1) == segs[b].astype(F32)
            if kb == b:
                shape = (quarter, quarter)
                same = same & (
                    lax.broadcasted_iota(jnp.int32, shape, 0)
                    <= lax.broadcasted_iota(jnp.int32, shape, 1)
                )
            mask[pl.ds(at, quarter), :] = jnp.where(same, 1.0, 0.0)
            at += quarter

    ag_last("q")
    ag_second("o")
    qkv = r["qkv"]

    def qkv_rows(first):
        def step(p, _):
            cols = dcol(p * pcols, pcols)
            out = nn(normed[pl.ds(first, half), :], W["q"][:, cols])
            qkv[pl.ds(first, half), cols] = out.astype(BF)
            return 0

        lax.fori_loop(0, pairs, step, 0)

    qkv_rows(own0)
    n_copy.wait_recv()
    qkv_rows(oth0)

    attended, lev = r["attended"], r["lev"]
    lane = lax.broadcasted_iota(jnp.int32, (1, LANES), 1)
    head_lane = [jnp.where(lane < LANES // 2, 1.0, 0.0), jnp.where(lane < LANES // 2, 0.0, 1.0)]
    head_bf = [v.astype(BF) for v in head_lane]
    scale = HEAD_DIM ** (-0.5)

    def attend(p):
        for b in range(4):
            at, k0, n = base[b]
            qs = pl.ds(quarter * b, quarter)
            ks = pl.ds(quarter * k0, n)
            query = qkv[qs, dcol(p * pcols, LANES)] * jnp.asarray(scale, BF)
            key = qkv[ks, dcol(p * pcols + LANES, LANES)]
            value = qkv[ks, dcol(p * pcols + 2 * LANES, LANES)]
            allowed = mask[pl.ds(at, n), :]
            total_out = None
            for h in range(2):
                sm = nt(key, query * head_bf[h]) * allowed
                mag = jnp.abs(sm)
                top = jnp.max(mag, axis=0, keepdims=True)
                raw = jnp.exp(mag - top)
                low = jnp.exp(-top)
                total = jnp.sum(raw * allowed, axis=0, keepdims=True)
                sign = jnp.clip(sm * HUGE, -1.0, 1.0)
                signed = (sign * (raw - low) * (1.0 / total)).astype(BF)
                lev[2 * p + h, :, qs] = top + jnp.log(total)
                out = tn(signed, value * head_bf[h])
                total_out = out if total_out is None else total_out + out
            attended[qs, dcol(c * hcols + p * LANES, LANES)] = total_out.astype(BF)

    att_i = sems(pairs)

    def att_copy(p):
        cols = attended.at[:, dcol(c * hcols + p * LANES, LANES)]
        return remote(cols, cols, att_i + p, part)

    for p in range(pairs):
        attend(p)
        att_copy(p).start()
        ends.append(att_copy(p).wait_send)
        if p == 0:
            ag_second("u")
            ag_first("d")
            ag_last("o")
            half_o = W["o"].at[:, dcol(c * hcols, hcols)]
            o_copy = send(half_o, half_o, part)
    o_copy.wait_recv()
    for p in range(pairs):
        att_copy(p).wait_recv()

    middle, n2 = r["middle"], r["n2"]
    for k in range(2):
        ts = pl.ds(own0 + quarter * k, quarter)
        ls = pl.ds(quarter * k, quarter)
        mid_v = xb[ls, :].astype(F32) + nn(attended[ts, :], W["o"][...])
        middle[ls, :] = mid_v
        cen, rstd = row_stats(mid_v)
        n2[ts, :] = (cen * rstd * gain_two).astype(BF)
    n2_copy = send(rows(n2, own0, half), rows(n2, own0, half), part)

    ag_last("u")
    active, du = r["active"], r["du"]
    ft = 512
    nft = ffh // ft

    def up_rows(first):
        def step(i, _):
            ts = pl.ds(first + quarter * lax.div(i, nft), quarter)
            cols = dcol(ft * lax.rem(i, nft), ft)
            u = nn(n2[ts, :], W["u"][:, cols])
            u2 = u * u
            t = jnp.tanh(GELU_K * (u + GELU_C * u * u2))
            active[ts, cols] = (0.5 * u * (1.0 + t)).astype(BF)
            slope = 0.5 * (1.0 + t) + 0.5 * u * (1.0 - t * t) * (
                GELU_K * (1.0 + 3.0 * GELU_C * u2)
            )
            du[ts, cols] = slope.astype(BF)
            return 0

        lax.fori_loop(0, 2 * nft, step, 0)

    up_rows(own0)
    n2_copy.wait_recv()
    up_rows(oth0)
    ag_second("d")

    cb = r["cb"]
    for k in range(2):
        wait_in(rows(cb, own0 + quarter * k, quarter), c_i + k)
    c_copy = send(rows(cb, own0, half), rows(cb, own0, half), part)
    c_copy.wait_recv()

    def reduce_piece(name, ref, blk, cols, place):
        h2 = blk // 2
        r1a, r1b, r2a, r2b, r3, r4, fin = (
            r[name + k] for k in ("1a", "1b", "2a", "2b", "3", "4", "f")
        )
        i3, i4, i5 = sems(), sems(), sems()
        state = {}

        def part_rows(qq, upper):
            return pl.ds(pl.multiple_of(qq * blk + upper * h2, 32), h2)

        q_of = lambda yy, xx: 2 * yy + xx

        def first():
            state["a"] = [
                send(ref.at[part_rows(q_of(yy, 1 - x), 0), :], r1a.at[yy], nx) for yy in range(2)
            ]
            state["b"] = [
                send(ref.at[part_rows(q_of(1 - y, xx), 1), :], r1b.at[xx], ny) for xx in range(2)
            ]

        def second():
            for copy in state["a"]:
                copy.wait_recv()
            ra = part_rows(q_of(1 - y, x), 0)
            ref[ra, :] = (ref[ra, :].astype(F32) + r1a[1 - y].astype(F32)).astype(BF)
            state["a2"] = send(ref.at[ra, :], r2a, ny)
            for copy in state["b"]:
                copy.wait_recv()
            rb = part_rows(q_of(y, 1 - x), 1)
            ref[rb, :] = (ref[rb, :].astype(F32) + r1b[1 - x].astype(F32)).astype(BF)
            state["b2"] = send(ref.at[rb, :], r2b, nx)

        own = pl.ds(pl.multiple_of(q * blk, 32), blk)

        def along_z(src, dst, i, dev):
            return remote(src, dst, i, dev)

        def third():
            state["a2"].wait_recv()
            ra = part_rows(q, 0)
            ref[ra, :] = (
                ref[ra, :].astype(F32) + r1a[y].astype(F32) + r2a[...].astype(F32)
            ).astype(BF)
            state["b2"].wait_recv()
            rb = part_rows(q, 1)
            ref[rb, :] = (
                ref[rb, :].astype(F32) + r1b[x].astype(F32) + r2b[...].astype(F32)
            ).astype(BF)

            @pl.when(edge)
            def _():
                along_z(ref.at[own, :], r3, i3, zp).start()

        def fourth():
            @pl.when(mid)
            def _():
                along_z(ref.at[own, :], r3, i3, zp).wait_recv()
                ref[own, :] = (ref[own, :].astype(F32) + r3[...].astype(F32)).astype(BF)
                along_z(ref.at[own, :], r4, i4, zm).start()

        def fifth():
            @pl.when(mid)
            def _():
                along_z(ref.at[own, :], r4, i4, zm).wait_recv()
                fin[...] = (ref[own, :].astype(F32) + r4[...].astype(F32)).astype(BF)
                along_z(fin, fin, i5, zp).start()

        def last():
            @pl.when(edge)
            def _():
                along_z(fin, fin, i5, zp).wait_recv()

            place(fin)

        def end():
            @pl.when(edge)
            def _():
                along_z(ref.at[own, :], r3, i3, zp).wait_send()

            @pl.when(mid)
            def _():
                along_z(ref.at[own, :], r4, i4, zm).wait_send()
                along_z(fin, fin, i5, zp).wait_send()

        ends.append(end)
        return first, second, third, fourth, fifth, last

    waits = []

    def put(src, dst):
        i = sems()
        copy = pltpu.make_async_copy(src, dst, rsem.at[i])
        copy.start()
        waits.append(copy.wait)

    def put_partner(src, dst):
        copy = send(src, dst, part)
        waits.append(copy.wait_recv)

    def by_core(fin, cuts, out):
        mine = pl.ds(pl.multiple_of(c * rows_dev, 32), rows_dev)
        his = pl.ds(pl.multiple_of((1 - c) * rows_dev, 32), rows_dev)
        for src_col, dst_col, n in cuts:
            put_partner(fin.at[his, pl.ds(src_col, n)], out.at[:, dcol(dst_col, n)])
            put(fin.at[mine, pl.ds(src_col, n)], out.at[:, dcol(dst_col, n)])

    def place_d(fin):
        put(fin, r["o_down"])

    def place_u(fin):
        by_core(fin, [(j * ffb, (2 * j + c) * ffb, ffb) for j in range(4)], r["o_up"])

    def place_o(fin):
        by_core(fin, [(0, c * hcols, hcols)], r["o_out"])

    def place_q(p):
        def place(fin):
            by_core(
                fin,
                [
                    (t * LANES, t * width + c * hcols + p * LANES, LANES)
                    for t in range(3)
                ],
                r["o_qkv"],
            )

        return place

    red = {
        "d": reduce_piece("rd", r["g_d"], ffb, width, place_d),
        "u": reduce_piece("ru", r["g_u"], rows_chip, ffh, place_u),
        "o": reduce_piece("ro", r["g_o"], rows_chip, hcols, place_o),
    }
    for p in range(pairs):
        red[p] = reduce_piece("rq%d" % p, r["g_q"].at[p], rows_chip, pcols, place_q(p))

    gt = 256

    def grad_down_step(i, _):
        cols = dcol(gt * i, gt)
        r["g_d"][pl.ds(pl.multiple_of(gt * i, gt), gt), :] = tn(active[:, cols], cb[...]).astype(BF)
        return 0

    lax.fori_loop(0, ffh // gt, grad_down_step, 0)
    red["d"][0]()

    ag_last("d")
    wait_in(rows(W["d"], ffb * q, ffb), local_d)
    xs, xr = r["xs"], r["xr"]

    def exchange(n, product_of):
        copies = []
        for k in range(2):
            ls = pl.ds(quarter * k, quarter)
            xs[ls, :] = product_of(pl.ds(oth0 + quarter * k, quarter))
            copies.append(send(xs.at[ls, :], xr.at[n, ls, :], part))
        return copies

    mix_copies = exchange(0, lambda ts: nn(active[ts, :], W["d"][...]))
    red["d"][1]()
    mixb = r["mixb"]
    for k in range(2):
        ls = pl.ds(quarter * k, quarter)
        mixb_f = middle[ls, :] + nn(active[pl.ds(own0 + quarter * k, quarter), :], W["d"][...])
        mix_copies[k].wait_recv()
        mixb[ls, :] = (mixb_f + xr[0, ls, :]).astype(BF)

    def from_chip(buf, out, i0):
        for k in range(2):
            zd = 2 * c + k
            src = buf.at[pl.ds(quarter * k, quarter), :]
            is_self = (zd == z) & (zk == c)
            dev = (zd, s - c + zk)
            dst = out.at[zh]

            @pl.when(is_self)
            def _():
                pltpu.make_async_copy(src, dst, rsem.at[i0 + zh]).start()

            @pl.when(jnp.logical_not(is_self))
            def _():
                remote(src, dst, i0 + zh, dev, i0 + k).start()

            def end(src=src, dst=dst, dev=dev, is_self=is_self, k=k):
                @pl.when(jnp.logical_not(is_self))
                def _():
                    remote(src, dst, i0 + zh, dev, i0 + k).wait_send()

            ends.append(end)
        for m in range(2):
            waits.append(functools.partial(wait_in, out.at[m], i0 + m))

    mo_i = sems(2)
    from_chip(mixb, r["o_mixed"], mo_i)

    def d_up_step(i, _):
        ts = pl.ds(pl.multiple_of(quarter * lax.div(i, nft), quarter), quarter)
        cols = dcol(ft * lax.rem(i, nft), ft)
        da = nt(cb[ts, :], W["d"][pl.ds(pl.multiple_of(ft * lax.rem(i, nft), ft), ft), :])
        du[ts, cols] = (da * du[ts, cols].astype(F32)).astype(BF)
        return 0

    lax.fori_loop(0, 4 * nft, d_up_step, 0)
    red["d"][2]()

    for copy in mix_copies:
        copy.wait_send()
        ends.remove(copy.wait_send)
    dn2_copies = exchange(1, lambda ts: nt(du[ts, :], W["u"][...]))

    def grad_up_step(i, _):
        cols = dcol(gt * lax.div(i, nft), gt)
        fcols = dcol(ft * lax.rem(i, nft), ft)
        out = tn(n2[:, cols], du[:, fcols]).astype(BF)
        r["g_u"][pl.ds(pl.multiple_of(gt * lax.div(i, nft), gt), gt), fcols] = out
        return 0

    lax.fori_loop(0, (width // gt) * nft, grad_up_step, 0)
    red["u"][0]()
    red["d"][3]()

    dbr, gsum = r["dbr"], r["gsum"]
    gain_acc = jnp.zeros((1, width), F32)
    for k in range(2):
        ts = pl.ds(own0 + quarter * k, quarter)
        ls = pl.ds(quarter * k, quarter)
        dn = nt(du[ts, :], W["u"][...])
        dn2_copies[k].wait_recv()
        dn = dn + xr[1, ls, :]
        cen, rstd = row_stats(middle[ls, :])
        n = cen * rstd
        gain_acc = gain_acc + jnp.sum(dn * n, axis=0, keepdims=True)
        dmid = cb[ts, :].astype(F32) + norm_back(dn, n, rstd, gain_two)
        middle[ls, :] = dmid
        dbr[ts, :] = dmid.astype(BF)
    gsum[0, :, width:] = gain_acc
    db_copy = send(rows(dbr, own0, half), rows(dbr, own0, half), part)
    red["d"][4]()
    db_copy.wait_recv()

    datt = r["datt"]

    def datt_step(k, _):
        ts = pl.ds(pl.multiple_of(quarter * k, quarter), quarter)
        w_rows = W["o"][pl.ds(pl.multiple_of(c * hcols, LANES), hcols), :]
        datt[ts, :] = nt(dbr[ts, :], w_rows).astype(BF)
        return 0

    lax.fori_loop(0, 4, datt_step, 0)

    def grad_out_step(i, _):
        cols = dcol(gt * i, gt)
        out = tn(attended[:, cols], dbr[:, dcol(c * hcols, hcols)]).astype(BF)
        r["g_o"][pl.ds(pl.multiple_of(gt * i, gt), gt), :] = out
        return 0

    lax.fori_loop(0, width // gt, grad_out_step, 0)
    red["o"][0]()
    red["u"][1]()
    red["d"][5]()

    dk, dv = r["dk"], r["dv"]
    sel = (
        lax.broadcasted_iota(jnp.int32, (8, LANES), 0)
        == lax.div(lax.broadcasted_iota(jnp.int32, (8, LANES), 1), LANES // 2)
    ).astype(F32)

    def attend_back(p):
        dk[...] = jnp.zeros_like(dk)
        dv[...] = jnp.zeros_like(dv)
        for b in range(4):
            at, k0, n = base[b]
            qs = pl.ds(quarter * b, quarter)
            ks = pl.ds(quarter * k0, n)
            query = qkv[qs, dcol(p * pcols, LANES)] * jnp.asarray(scale, BF)
            key = qkv[ks, dcol(p * pcols + LANES, LANES)]
            value = qkv[ks, dcol(p * pcols + 2 * LANES, LANES)]
            d_att = datt[qs, dcol(p * LANES, LANES)]
            att = attended[qs, dcol(c * hcols + p * LANES, LANES)]
            delta = nt(sel, d_att.astype(F32) * att.astype(F32), lax.Precision.HIGHEST)
            allowed = mask[pl.ds(at, n), :]
            d_query = None
            for h in range(2):
                q_h = query * head_bf[h]
                d_h = d_att * head_bf[h]
                sm = nt(key, q_h) * allowed
                mag = jnp.abs(sm)
                level = lev[2 * p + h, :, qs]
                prob = jnp.exp(mag - level)
                low = jnp.exp(-level)
                sign = jnp.clip(sm * HUGE, -1.0, 1.0)
                weight = (sign * (prob - low)).astype(BF)
                d_signed = nt(value, d_h)
                d_score = (prob * allowed * (d_signed - sign * delta[h : h + 1, :])).astype(BF)
                dv[ks, :] += nn(weight, d_h)
                dk[ks, :] += nn(d_score, q_h)
                out = tn(d_score, key * head_bf[h])
                d_query = out if d_query is None else d_query + out
            qkv[qs, dcol(p * pcols, LANES)] = (d_query * scale).astype(BF)
        qkv[:, dcol(p * pcols + LANES, LANES)] = dk[...].astype(BF)
        qkv[:, dcol(p * pcols + 2 * LANES, LANES)] = dv[...].astype(BF)

    def grad_qkv(p):
        def step(i, _):
            cols = dcol(gt * i, gt)
            out = tn(normed[:, cols], qkv[:, dcol(p * pcols, pcols)]).astype(BF)
            r["g_q"][p, pl.ds(pl.multiple_of(gt * i, gt), gt), :] = out
            return 0

        lax.fori_loop(0, width // gt, step, 0)

    attend_back(0)
    grad_qkv(0)
    red["o"][1]()
    red[0][0]()
    red["u"][2]()
    attend_back(1)
    grad_qkv(1)
    red["u"][3]()
    red["o"][2]()
    red[0][1]()
    red[1][0]()
    attend_back(2)
    red["u"][4]()
    red["o"][3]()
    grad_qkv(2)
    red[2][0]()

    for copy in dn2_copies:
        copy.wait_send()
        ends.remove(copy.wait_send)
    dn1_copies = exchange(2, lambda ts: nt(qkv[ts, :], W["q"][...]))
    red[0][2]()
    red[1][1]()
    gtb = r["gtb"]
    gain_acc = jnp.zeros((1, width), F32)
    for k in range(2):
        ts = pl.ds(own0 + quarter * k, quarter)
        ls = pl.ds(quarter * k, quarter)
        dn = nt(qkv[ts, :], W["q"][...])
        dn1_copies[k].wait_recv()
        dn = dn + xr[2, ls, :]
        cen, rstd = row_stats(xb[ls, :].astype(F32))
        n = cen * rstd
        gain_acc = gain_acc + jnp.sum(dn * n, axis=0, keepdims=True)
        gtb[ls, :] = (middle[ls, :] + norm_back(dn, n, rstd, gain_one)).astype(BF)
    gsum[0, :, :width] = gain_acc
    to_i = sems(2)
    from_chip(gtb, r["o_gt"], to_i)

    g_copy = send(gsum.at[0], gsum.at[1], part)
    red[2][1]()
    red["u"][5]()
    red["o"][4]()
    red[0][3]()
    red[1][2]()
    g_copy.wait_recv()
    gsum[2] = gsum[0] + gsum[1]
    g_copy = send(gsum.at[2], gsum.at[3], nx)
    red[1][3]()
    red[2][2]()
    red[0][4]()
    red["o"][5]()
    g_copy.wait_recv()
    gsum[4] = gsum[2] + gsum[3]
    g_copy = send(gsum.at[4], gsum.at[5], ny)
    red[2][3]()
    red[1][4]()
    red[0][5]()
    g_copy.wait_recv()
    gsum[6] = gsum[4] + gsum[5]
    g3, g4, g5 = sems(), sems(), sems()

    @pl.when(edge)
    def _():
        remote(gsum.at[6], gsum.at[7], g3, zp).start()

    @pl.when(mid)
    def _():
        remote(gsum.at[6], gsum.at[7], g3, zp).wait_recv()
        gsum[8] = gsum[6] + gsum[7]
        remote(gsum.at[8], gsum.at[9], g4, zm).start()

    red[2][4]()
    red[1][5]()

    @pl.when(mid)
    def _():
        remote(gsum.at[8], gsum.at[9], g4, zm).wait_recv()
        gsum[10] = gsum[8] + gsum[9]
        remote(gsum.at[10], gsum.at[10], g5, zp).start()
        remote(gsum.at[8], gsum.at[9], g4, zm).wait_send()
        remote(gsum.at[10], gsum.at[10], g5, zp).wait_send()

    @pl.when(edge)
    def _():
        remote(gsum.at[10], gsum.at[10], g5, zp).wait_recv()
        remote(gsum.at[6], gsum.at[7], g3, zp).wait_send()

    red[2][5]()
    pick = (
        lax.broadcasted_iota(jnp.int32, (width, LANES), 0)
        == lax.broadcasted_iota(jnp.int32, (width, LANES), 1) + rows_dev * s
    ).astype(F32)
    for k in range(2):
        vec = jnp.broadcast_to(gsum[10][:, width * k : width * (k + 1)], (8, width))
        r["o_gains"][k : k + 1, :] = nn(vec, pick, lax.Precision.HIGHEST)[0:1, :rows_dev]
    for wait in waits:
        wait()
    for end in ends:
        end()
    assert used[0] <= N_SEMS, used[0]


def per_device_fast(tokens, segments, w_qkv, w_out, w_up, w_down, gain_one, gain_two, cotangent):
    micro, _, quarter, width = tokens.shape
    rows_dev = w_qkv.shape[0]
    ff = w_up.shape[1]
    ffb = w_down.shape[0]
    half, length = 2 * quarter, 4 * quarter
    hcols, ffh, rows_chip = width // 2, ff // 2, 2 * rows_dev
    pairs = hcols // LANES
    pcols = 3 * LANES
    shard = lax.axis_index("shard")
    mine = lax.div(jnp.arange(width), rows_dev) == shard

    def spread(gain):
        return jnp.where(mine, jnp.tile(gain.astype(F32), width // rows_dev), 0.0)

    placed = jnp.concatenate([spread(gain_one), spread(gain_two)])[None]
    scratch = {}

    def vm(name, shape, dtype=BF):
        scratch[name] = pltpu.VMEM(shape, dtype)

    vm("w_q", (width, pairs * pcols))
    vm("w_o", (width, width))
    vm("w_u", (width, ffh))
    vm("w_d", (ffh, width))
    vm("segs", (4, 1, quarter), jnp.int32)
    vm("segc", (length, LANES), F32)
    vm("mask", (9 * quarter, quarter), F32)
    vm("xb", (half, width))
    vm("cb", (length, width))
    vm("gains", (6, 1, 2 * width), F32)
    vm("gsum", (11, 1, 2 * width), F32)
    vm("normed", (length, width))
    vm("qkv", (length, pairs * pcols))
    vm("lev", (2 * pairs, 1, length), F32)
    vm("attended", (length, width))
    vm("middle", (half, width), F32)
    vm("n2", (length, width))
    vm("active", (length, ffh))
    vm("du", (length, ffh))
    vm("xs", (half, width), F32)
    vm("xr", (3, half, width), F32)
    vm("mixb", (half, width))
    vm("gtb", (half, width))
    vm("dbr", (length, width))
    vm("datt", (length, hcols))
    vm("dk", (length, LANES), F32)
    vm("dv", (length, LANES), F32)
    vm("g_d", (ffh, width))
    vm("g_u", (width, ffh))
    vm("g_o", (width, hcols))
    vm("g_q", (pairs, width, pcols))
    pieces = [("rd", ffb, width), ("ru", rows_chip, ffh), ("ro", rows_chip, hcols)]
    pieces += [("rq%d" % p, rows_chip, pcols) for p in range(pairs)]
    for name, blk, cols in pieces:
        vm(name + "1a", (2, blk // 2, cols))
        vm(name + "1b", (2, blk // 2, cols))
        vm(name + "2a", (blk // 2, cols))
        vm(name + "2b", (blk // 2, cols))
        vm(name + "3", (blk, cols))
        vm(name + "4", (blk, cols))
        vm(name + "f", (blk, cols))
    scratch["ssem"] = pltpu.SemaphoreType.DMA((N_SEMS,))
    scratch["rsem"] = pltpu.SemaphoreType.DMA((N_SEMS,))
    outs = {
        "o_mixed": ((micro, quarter, width), BF),
        "o_gt": ((micro, quarter, width), BF),
        "o_qkv": ((rows_dev, 3 * width), BF),
        "o_out": ((rows_dev, width), BF),
        "o_up": ((rows_dev, ff), BF),
        "o_down": ((ffb, width), BF),
        "o_gains": ((2, rows_dev), F32),
    }
    ins = ["tok", "seg", "wqkv", "wout", "wup", "wdn", "gpl", "cot"]
    names = ins + list(outs) + list(scratch)
    hbm = pl.BlockSpec(memory_space=pl.ANY)
    vmem = pl.BlockSpec(memory_space=pltpu.VMEM)
    tokens_all = 2 * half
    flops = 6 * half * (width * (4 * width + 2 * ff)) + 14 * 9 * 6 * quarter * quarter * 128
    got = pl.pallas_call(
        functools.partial(layer_kernel, names),
        out_shape=[jax.ShapeDtypeStruct(*v) for v in outs.values()],
        in_specs=[vmem if k == "gpl" else hbm for k in ins],
        out_specs=[vmem if k == "o_gains" else hbm for k in outs],
        scratch_shapes=list(scratch.values()),
        compiler_params=pltpu.CompilerParams(
            collective_id=0, has_side_effects=True, vmem_limit_bytes=VMEM_LIMIT
        ),
        cost_estimate=pl.CostEstimate(
            flops=flops, bytes_accessed=20 * tokens_all * width, transcendentals=0
        ),
    )(
        tokens[:, 0],
        segments.reshape(micro, 1, quarter),
        w_qkv,
        w_out,
        w_up,
        w_down,
        placed,
        cotangent[:, 0],
    )
    mixed, grad_tokens, g_qkv, g_out, g_up, g_down, g_gains = got
    return (
        mixed[:, None],
        grad_tokens.astype(F32)[:, None],
        g_qkv.astype(F32),
        g_out.astype(F32),
        g_up.astype(F32),
        g_down.astype(F32),
        g_gains[0],
        g_gains[1],
    )


VMEM_LIMIT = 62 * 1024 * 1024


def solution(mesh):
    placed = (
        P(None, "shard", "seq", None),
        P(None, "shard", "seq"),
        P("shard", None),
        P("shard", None),
        P("shard", None),
        P("shard", None),
        P("shard"),
        P("shard"),
        P(None, "shard", "seq", None),
    )
    chip_sized = mesh.shape["seq"] == 4 and mesh.shape["shard"] == 8
    return jax.shard_map(
        per_device_fast if chip_sized else per_device,
        mesh=mesh,
        in_specs=placed,
        out_specs=(
            P(None, "shard", "seq", None),
            P(None, "shard", "seq", None),
            P("shard", None),
            P("shard", None),
            P("shard", None),
            P("shard", None),
            P("shard"),
            P("shard"),
        ),
        check_vma=False,
    )
```

```python
import functools
import math

import jax
import jax.numpy as jnp
from jax import lax
from jax.experimental import pallas as pl
from jax.experimental.pallas import tpu as pltpu
from jax.sharding import PartitionSpec as P


HEADS = 12
HEAD_DIM = 64


epsilon = 1e-05
far_below = -1e30


def norm_rows(values, gain):
    row_mean = jnp.mean(values, axis=-1, keepdims=True)
    centred = values - row_mean
    spread = jnp.mean(centred * centred, axis=-1, keepdims=True)
    return centred * lax.rsqrt(spread + epsilon) * gain


def gelu_tanh(values):
    return jax.nn.gelu(values, approximate=True)


def product(left, right):
    return jnp.dot(left, right, preferred_element_type=jnp.float32)


def product_left_t(left, right):
    return lax.dot_general(
        left, right, (((0,), (0,)), ((), ())), preferred_element_type=jnp.float32
    )


def product_right_t(left, right):
    return lax.dot_general(
        left, right, (((1,), (1,)), ((), ())), preferred_element_type=jnp.float32
    )


def block_scores(query_block, keys, seg_rows, seg_cols, row_first, score_scale):
    rows_count = query_block.shape[0]
    cols_count = keys.shape[0]
    scores = (
        jnp.einsum("qhd,khd->hqk", query_block, keys, preferred_element_type=jnp.float32)
        * score_scale
    )
    row_pos = row_first + lax.broadcasted_iota(jnp.int32, (rows_count, cols_count), 0)
    col_pos = lax.broadcasted_iota(jnp.int32, (rows_count, cols_count), 1)
    allowed = (col_pos <= row_pos) & (seg_rows[:, None] == seg_cols[None, :])
    return (scores, allowed[None])


def attend_forward(queries, keys, values, seg_all, rows_block, score_scale):
    length = queries.shape[0]
    out_parts = []
    level_parts = []
    for row_first in range(0, length, rows_block):
        query_block = queries[row_first : row_first + rows_block]
        scores, allowed = block_scores(
            query_block,
            keys,
            seg_all[row_first : row_first + rows_block],
            seg_all,
            row_first,
            score_scale,
        )
        magnitude = jnp.abs(scores)
        row_top = jnp.max(jnp.where(allowed, magnitude, far_below), axis=-1, keepdims=True)
        exp_raw = jnp.where(allowed, jnp.exp(magnitude - row_top), 0.0)
        total = jnp.sum(exp_raw, axis=-1, keepdims=True)
        floor_term = jnp.where(allowed, jnp.exp(-row_top), 0.0)
        signed = (jnp.sign(scores) * (exp_raw - floor_term) / total).astype(jnp.bfloat16)
        out_parts.append(
            jnp.einsum("hqk,khd->qhd", signed, values, preferred_element_type=jnp.float32)
        )
        level_parts.append(row_top + jnp.log(total))
    return (jnp.concatenate(out_parts, axis=0), jnp.concatenate(level_parts, axis=1))


def attend_backward(queries, keys, values, seg_all, levels, d_heads, rows_block, score_scale):
    length = queries.shape[0]
    grad_keys = jnp.zeros(keys.shape, jnp.float32)
    grad_values = jnp.zeros(values.shape, jnp.float32)
    query_parts = []
    for row_first in range(0, length, rows_block):
        query_block = queries[row_first : row_first + rows_block]
        d_block = d_heads[row_first : row_first + rows_block]
        scores, allowed = block_scores(
            query_block,
            keys,
            seg_all[row_first : row_first + rows_block],
            seg_all,
            row_first,
            score_scale,
        )
        level_block = levels[:, row_first : row_first + rows_block]
        sign_part = jnp.sign(scores)
        prob = jnp.where(allowed, jnp.exp(jnp.abs(scores) - level_block), 0.0)
        weight = sign_part * jnp.where(allowed, prob - jnp.exp(-level_block), 0.0)
        d_signed = jnp.einsum("qhd,khd->hqk", d_block, values, preferred_element_type=jnp.float32)
        delta = jnp.sum(weight * d_signed, axis=-1, keepdims=True)
        d_score = (prob * (d_signed - sign_part * delta)).astype(jnp.bfloat16)
        query_parts.append(
            jnp.einsum("hqk,khd->qhd", d_score, keys, preferred_element_type=jnp.float32)
            * score_scale
        )
        grad_keys = (
            grad_keys
            + jnp.einsum("hqk,qhd->khd", d_score, query_block, preferred_element_type=jnp.float32)
            * score_scale
        )
        grad_values = grad_values + jnp.einsum(
            "hqk,qhd->khd", weight.astype(jnp.bfloat16), d_block, preferred_element_type=jnp.float32
        )
    grad_queries = jnp.concatenate(query_parts, axis=0)
    stacked = jnp.stack([grad_queries, grad_keys, grad_values], axis=1)
    heads_dev = queries.shape[1]
    return stacked.astype(jnp.bfloat16).reshape(length, 3, 1, heads_dev * queries.shape[2])


def per_device(tokens, segments, w_qkv, w_out, w_up, w_down, gain_one, gain_two, cotangent):
    micro_count = tokens.shape[0]
    tok_rows = tokens.shape[2]
    width = tokens.shape[3]
    groups = lax.axis_size("seq")
    heads_dev = HEADS // groups
    head_cols = heads_dev * HEAD_DIM
    length = tok_rows * groups
    rows_block = min(512, length)
    score_scale = HEAD_DIM ** (-0.5)
    totals = None
    shares = None
    results = []
    grad_rows = []
    for micro_idx in range(micro_count):
        whole = (
            lax.all_gather(w_qkv, "shard", axis=0, tiled=True),
            lax.all_gather(w_out, "shard", axis=0, tiled=True),
            lax.all_gather(w_up, "shard", axis=0, tiled=True),
            lax.all_gather(w_down, "shard", axis=0, tiled=True),
            lax.all_gather(gain_one, "shard", axis=0, tiled=True),
            lax.all_gather(gain_two, "shard", axis=0, tiled=True),
        )
        full_qkv, full_out, full_up, full_down = (whole[0], whole[1], whole[2], whole[3])
        gain_first = whole[4].astype(jnp.float32)
        gain_second = whole[5].astype(jnp.float32)
        tokens_f = tokens[micro_idx, 0].astype(jnp.float32)
        seg_local = segments[micro_idx, 0].astype(jnp.bfloat16)
        normed = norm_rows(tokens_f, gain_first).astype(jnp.bfloat16)
        packed = (
            product(normed, full_qkv).astype(jnp.bfloat16).reshape(tok_rows, 3, groups, head_cols)
        )
        seg_tile = jnp.broadcast_to(seg_local[:, None, None, None], (tok_rows, 1, groups, 1))
        received, seg_recv = (
            lax.all_to_all(packed, "seq", split_axis=2, concat_axis=0, tiled=True),
            lax.all_to_all(seg_tile, "seq", split_axis=2, concat_axis=0, tiled=True),
        )
        queries = received[:, 0, 0].reshape(length, heads_dev, HEAD_DIM)
        keys = received[:, 1, 0].reshape(length, heads_dev, HEAD_DIM)
        values = received[:, 2, 0].reshape(length, heads_dev, HEAD_DIM)
        seg_all = seg_recv[:, 0, 0, 0]
        heads_out, levels = attend_forward(queries, keys, values, seg_all, rows_block, score_scale)
        heads_low = heads_out.astype(jnp.bfloat16).reshape(length, 1, head_cols)
        attended = lax.all_to_all(
            heads_low, "seq", split_axis=0, concat_axis=1, tiled=True
        ).reshape(tok_rows, width)
        middle = tokens_f + product(attended, full_out)
        normed_two = norm_rows(middle, gain_second).astype(jnp.bfloat16)
        up_pre = product(normed_two, full_up)
        active = gelu_tanh(up_pre).astype(jnp.bfloat16)
        results.append((middle + product(active, full_down)).astype(jnp.bfloat16))
        again = (
            lax.all_gather(w_qkv, "shard", axis=0, tiled=True),
            lax.all_gather(w_out, "shard", axis=0, tiled=True),
            lax.all_gather(w_up, "shard", axis=0, tiled=True),
            lax.all_gather(w_down, "shard", axis=0, tiled=True),
            lax.all_gather(gain_one, "shard", axis=0, tiled=True),
            lax.all_gather(gain_two, "shard", axis=0, tiled=True),
        )
        back_qkv, back_out, back_up, back_down = (again[0], again[1], again[2], again[3])
        cot_low = cotangent[micro_idx, 0]
        grad_down_term = product_left_t(active, cot_low)
        d_active = product_right_t(cot_low, back_down)
        unused_gelu, gelu_pull = jax.vjp(gelu_tanh, up_pre)
        d_up = gelu_pull(d_active)[0].astype(jnp.bfloat16)
        grad_up_term = product_left_t(normed_two, d_up)
        d_norm_two = product_right_t(d_up, back_up)
        unused_second, second_pull = jax.vjp(norm_rows, middle, gain_second)
        d_middle_norm, grad_gain_two_term = second_pull(d_norm_two)
        d_middle = cot_low.astype(jnp.float32) + d_middle_norm
        d_branch = d_middle.astype(jnp.bfloat16)
        grad_out_term = product_left_t(attended, d_branch)
        d_attended = (
            product_right_t(d_branch, back_out)
            .astype(jnp.bfloat16)
            .reshape(tok_rows, groups, head_cols)
        )
        d_heads = lax.all_to_all(d_attended, "seq", split_axis=1, concat_axis=0, tiled=True)
        d_heads = d_heads[:, 0].reshape(length, heads_dev, HEAD_DIM)
        grad_heads = attend_backward(
            queries, keys, values, seg_all, levels, d_heads, rows_block, score_scale
        )
        d_packed = lax.all_to_all(
            grad_heads, "seq", split_axis=0, concat_axis=2, tiled=True
        ).reshape(tok_rows, 3 * width)
        grad_qkv_term = product_left_t(normed, d_packed)
        d_normed = product_right_t(d_packed, back_qkv)
        unused_first, first_pull = jax.vjp(norm_rows, tokens_f, gain_first)
        d_tokens_norm, grad_gain_one_term = first_pull(d_normed)
        grad_rows.append(d_middle + d_tokens_norm)
        terms = (
            grad_qkv_term,
            grad_out_term,
            grad_up_term,
            grad_down_term,
            grad_gain_one_term,
            grad_gain_two_term,
        )
        if totals is None:
            totals = terms
        else:
            totals = tuple((left_term + right_term for left_term, right_term in zip(totals, terms)))
    shares = (
        lax.psum_scatter(totals[0], "shard", scatter_dimension=0, tiled=True),
        lax.psum_scatter(totals[1], "shard", scatter_dimension=0, tiled=True),
        lax.psum_scatter(totals[2], "shard", scatter_dimension=0, tiled=True),
        lax.psum_scatter(totals[3], "shard", scatter_dimension=0, tiled=True),
        lax.psum_scatter(totals[4], "shard", scatter_dimension=0, tiled=True),
        lax.psum_scatter(totals[5], "shard", scatter_dimension=0, tiled=True),
    )
    replicas = lax.psum((shares[0], shares[1], shares[2], shares[3], shares[4], shares[5]), "seq")
    mixed = jnp.stack(results, axis=0)[:, None]
    grad_tokens = jnp.stack(grad_rows, axis=0)[:, None]
    return (
        mixed,
        grad_tokens,
        replicas[0],
        replicas[1],
        replicas[2],
        replicas[3],
        replicas[4],
        replicas[5],
    )


BF = jnp.bfloat16
F32 = jnp.float32
MESH = pl.DeviceIdType.MESH
N_SEMS = 132
SCHEDULE = (
    (0,),
    (6,),
    (),
    (12,),
    (1,),
    (),
    (7,),
    (13, 18,),
    (2,),
    (8, 24,),
    (14, 30,),
    (),
    (3, 19,),
    (),
    (9, 25,),
    (36,),
    (4,),
    (15, 31,),
    (20, 10,),
    (26, 42,),
    (16, 5,),
    (37,),
    (21, 54, 11, 32,),
    (),
    (),
    (27, 43, 60, 38, 17,),
    (33, 22,),
    (55,),
    (39, 44, 28, 48,),
    (61, 34, 23,),
    (66, 56, 49, 62,),
    (67, 29, 45, 50,),
    (40, 68, 35, 57, 41,),
    (63, 46, 51, 58,),
    (69, 47, 64, 59,),
    (52, 65, 70, 53, 71,),
)

HUGE = 3.0e38
GELU_K = math.sqrt(2.0 / math.pi)
GELU_C = 0.044715
LANES = 128


def nt(left, right, precision=None):
    return lax.dot_general(
        left, right, (((1,), (1,)), ((), ())), preferred_element_type=F32, precision=precision
    )


def tn(left, right):
    return lax.dot_general(left, right, (((0,), (0,)), ((), ())), preferred_element_type=F32)


def nn(left, right, precision=None):
    return jnp.dot(left, right, preferred_element_type=F32, precision=precision)


def row_stats(v):
    mean = jnp.mean(v, axis=-1, keepdims=True)
    cen = v - mean
    var = jnp.mean(cen * cen, axis=-1, keepdims=True)
    return cen, lax.rsqrt(var + epsilon)


def norm_back(dn, n, rstd, gain):
    e = dn * gain
    return (e - jnp.mean(e, axis=-1, keepdims=True) - n * jnp.mean(e * n, axis=-1, keepdims=True)) * rstd


def layer_kernel(names, *refs):
    r = dict(zip(names, refs))
    tok, seg, wqkv, wout, wup, wdn, cot = (
        r[k] for k in ("tok", "seg", "wqkv", "wout", "wup", "wdn", "cot")
    )
    ssem, rsem = r["ssem"], r["rsem"]
    width = tok.shape[2]
    quarter = tok.shape[1]
    half = 2 * quarter
    length = 4 * quarter
    rows_dev = wqkv.shape[0]
    rows_chip = 2 * rows_dev
    hcols = width // 2
    pairs = hcols // LANES
    pcols = 3 * LANES
    ffh = wup.shape[1] // 2
    ffb = wdn.shape[0]

    z = lax.axis_index("seq")
    s = lax.axis_index("shard")
    c = lax.rem(s, 2)
    q = lax.div(s, 2)
    x = lax.rem(q, 2)
    y = lax.div(q, 2)
    part = (z, s + 1 - 2 * c)
    nx = (z, s + 2 - 4 * x)
    ny = (z, s + 4 - 8 * y)
    zp = (z + 1 - 2 * lax.rem(z, 2), s)
    zm = (3 - z, s)
    edge = lax.rem(z, 3) == 0
    mid = lax.rem(z, 3) != 0
    qx = q + 1 - 2 * x
    qy = q + 2 - 4 * y
    zh = lax.div(z, 2)
    zk = lax.rem(z, 2)
    own0 = pl.multiple_of(half * c, half)
    oth0 = pl.multiple_of(half * (1 - c), half)

    used = [0]
    ends = []

    def sems(n=1):
        first = used[0]
        used[0] += n
        return first

    def remote(src, dst, i, dev, j=None):
        return pltpu.make_async_remote_copy(
            src_ref=src,
            dst_ref=dst,
            send_sem=ssem.at[i if j is None else j],
            recv_sem=rsem.at[i],
            device_id=dev,
            device_id_type=MESH,
        )

    def send(src, dst, dev):
        copy = remote(src, dst, sems(), dev)
        copy.start()
        ends.append(copy.wait_send)
        return copy

    def wait_in(ref, i):
        pltpu.make_async_copy(ref, ref, rsem.at[i]).wait()

    def rows(ref, start, n, align=16):
        return ref.at[pl.ds(pl.multiple_of(start, align), n), :]

    nd = (z, s + 2 - 4 * x + 4 - 8 * y)
    qd = 3 - q

    peers = [part, nx, ny, nd]
    for dz in range(1, 4):
        zz = lax.rem(z + dz, 4)
        peers += [(zz, s), (zz, s + 1 - 2 * c)]
    bar = pltpu.get_barrier_semaphore()
    for dev in peers:
        pl.semaphore_signal(bar, inc=1, device_id=dev, device_id_type=MESH)
    spread = (
        lax.broadcasted_iota(jnp.int32, (rows_dev, width), 1)
        == lax.broadcasted_iota(jnp.int32, (rows_dev, width), 0) + rows_dev * s
    ).astype(F32)
    gains = r["gains"]
    for k, g in enumerate((r["g1"], r["g2"])):
        vec = jnp.broadcast_to(g[...].astype(F32), (8, rows_dev))
        gains[0, :, k * width : (k + 1) * width] = nn(vec, spread, lax.Precision.HIGHEST)[0:1, :]
    pl.semaphore_wait(bar, len(peers))

    seg_i = sems(4)
    x_i = sems(2)
    c_i = sems(2)

    def to_chip(src, dst, i_recv, i_send, zd, core):
        is_self = (zd == z) & (core == c)
        dev = (zd, s - c + core)

        @pl.when(is_self)
        def _():
            pltpu.make_async_copy(src, dst, rsem.at[i_recv]).start()

        @pl.when(jnp.logical_not(is_self))
        def _():
            remote(src, dst, i_recv, dev, i_send).start()

        def end():
            @pl.when(jnp.logical_not(is_self))
            def _():
                remote(src, dst, i_recv, dev, i_send).wait_send()

        ends.append(end)

    for m in range(2):
        to_chip(tok.at[m], rows(r["xb"], quarter * zk, quarter), x_i + zk, x_i + m, 2 * m + c, zh)

    my = pl.multiple_of(rows_dev * s, 32)
    partner_rows = pl.ds(pl.multiple_of(part[1] * rows_dev, 32), rows_dev)
    my_rows = pl.ds(my, rows_dev)
    local_d = sems()
    local_i = {name: sems() for name in ("q", "o", "u0", "u1")}
    flip_i = {name: sems() for name in ("q", "o", "u0", "u1")}
    W = {"q": r["w_q"], "o": r["w_o"], "u": r["w_u"], "d": r["w_d"]}

    def dcol(start, n):
        return pl.ds(pl.multiple_of(start, LANES), n)

    half_u = ffh // 2

    def cols_of(name):
        return {
            "q": slice(None),
            "o": dcol(c * hcols, hcols),
            "u0": pl.ds(0, half_u),
            "u1": pl.ds(half_u, half_u),
            "d": slice(None),
        }[name]

    def pieces(name, core):
        if name == "q":
            cuts = [(wqkv, t * width + core * hcols, t * hcols, hcols) for t in range(3)]
        elif name == "o":
            cuts = [(wout, core * hcols, core * hcols, hcols)]
        else:
            js = (0, 1) if name == "u0" else (2, 3)
            cuts = [(wup, (2 * j + core) * ffb, j * ffb, ffb) for j in js]
        for src, col, at, n in cuts:
            yield src.at[:, dcol(col, n)], W[name[0]].at[my_rows, dcol(at, n)]

    def block(name, first, n):
        return W[name[0]].at[pl.ds(pl.multiple_of(first, 32), n), cols_of(name)]

    ag = {}

    def flip(name):
        for src, dst in pieces(name, 1 - c):
            remote(src, dst, flip_i[name], part).start()

        def end():
            mine = block(name, my, rows_dev)
            remote(mine, mine, flip_i[name], part).wait_send()

        ends.append(end)

    def keep(name):
        for src, dst in pieces(name, c):
            pltpu.make_async_copy(src, dst, rsem.at[local_i[name]]).start()

    def ag_wait_sent(i, n_rows, name):
        both = W[name[0]].at[pl.ds(0, 2 * n_rows), cols_of(name)]
        ends.append(lambda: remote(both, both, i, nx).wait_send())

    def ag_own(name):
        i = sems()
        ag[name] = i
        for dev in (nx, ny):
            for src, dst in pieces(name, c):
                remote(src, dst, i, dev).start()
        ag_wait_sent(i, rows_chip, name)

    def ag_partner(name):
        his = block(name, part[1] * rows_dev, rows_dev)
        wait_in(his, flip_i[name])
        for dev in (nx, ny):
            remote(his, his, ag[name], dev).start()

    def ag_first(name):
        if name == "d":
            dst = block("d", ffb * q, ffb)
            i = sems()
            ag["d"] = i
            for dev in (nx, ny):
                remote(wdn, dst, i, dev).start()
            ag_wait_sent(i, ffb, "d")
        else:
            wait_in(block(name, my, rows_dev), local_i[name])
            wait_in(block(name, part[1] * rows_dev, rows_dev), flip_i[name])
            i = sems()
            ag[name] = i
            for dev in (nx, ny):
                for first in (0, third_z):
                    rows_out = block(name, rows_chip * q + first, third)
                    remote(rows_out, rows_out, i, dev).start()
            ag_wait_sent(i, 2 * third, name)

    third = rows_chip // 3
    third_z = third * (1 + zk)

    def ag_second_u(name):
        wait_in(W["u"].at[pl.ds(0, 4 * third), cols_of(name)], ag[name])
        i, iz = sems(), sems()
        ag[name] = (i, iz)
        bx = block(name, rows_chip * qx, third)
        by = block(name, rows_chip * qy + third_z, third)
        remote(bx, bx, i, ny).start()
        remote(by, by, i, nx).start()
        ag_wait_sent(i, third, name)
        for qq in (qx, qy):
            rows_out = block(name, rows_chip * qq + third_z, third)
            remote(rows_out, rows_out, iz, zp).start()

    def ag_third_u(name):
        i, iz = ag[name]
        wait_in(W["u"].at[pl.ds(0, 2 * third), cols_of(name)], i)
        rows_out = block(name, rows_chip * qd + third_z, third)
        remote(rows_out, rows_out, iz, zp).start()
        all_three = W["u"].at[pl.ds(0, 3 * third), cols_of(name)]
        ends.append(lambda: remote(all_three, all_three, iz, zp).wait_send())

    def ag_last_u(name):
        wait_in(W["u"].at[pl.ds(0, 3 * third), cols_of(name)], ag[name][1])

    def ag_second(name):
        full = ffb if name == "d" else rows_chip
        n = full // 2
        wait_in(W[name[0]].at[pl.ds(0, 2 * full), cols_of(name)], ag[name])
        i = sems()
        ag[name] = (i,)
        bx = block(name, full * qx, n)
        by = block(name, full * qy + n, n)
        remote(bx, bx, i, ny).start()
        remote(by, by, i, nx).start()
        ag_wait_sent(i, n, name)

    def ag_last(name):
        full = ffb if name == "d" else rows_chip
        wait_in(block(name, full * qd, full), ag[name][0])
        if name != "d":
            wait_in(block(name, my, rows_dev), local_i[name])

    flip("q")
    ag_own("q")
    g_core = send(gains.at[0], gains.at[1], part)
    flip("o")
    ag_partner("q")
    ag_own("o")
    keep("q")
    keep("o")
    flip("u0")
    flip("u1")
    for m in range(2):
        for core in range(2):
            to_chip(seg.at[m], r["segs"].at[z], seg_i + z, seg_i + 2 * m + core, 2 * m + c, core)
    ag_partner("o")
    keep("u0")
    keep("u1")
    pltpu.make_async_copy(wdn, rows(W["d"], ffb * q, ffb), rsem.at[local_d]).start()

    g_core.wait_recv()
    gains[2] = gains[0] + gains[1]
    g_in = [send(gains.at[2], gains.at[3 + i], dev) for i, dev in enumerate((nx, ny, nd))]
    ag_second("q")
    ag_first("u0")
    ag_first("u1")
    for copy in g_in:
        copy.wait_recv()
    g_all = jnp.where(x == 0, gains[2], gains[3]) + jnp.where(x == 0, gains[3], gains[2])
    g_all = g_all + (gains[4] + gains[5])
    gains[6] = g_all
    gain_one = gains[6][:, :width]
    gain_two = gains[6][:, width:]

    segs, segc, mask = r["segs"], r["segc"], r["mask"]
    for b in range(4):
        wait_in(segs.at[b], seg_i + b)
    for b in range(4):
        tile = jnp.broadcast_to(segs[b].astype(F32), (LANES, quarter))
        segc[pl.ds(quarter * b, quarter), :] = jnp.transpose(tile)
    base = []
    at = 0
    for b in range(4):
        k0 = max(0, b - 2)
        base.append((at, k0, (b - k0 + 1) * quarter))
        for kb in range(k0, b + 1):
            col = segc[pl.ds(quarter * kb, quarter), :]
            same = jnp.concatenate([col] * (quarter // LANES), axis=1) == segs[b].astype(F32)
            if kb == b:
                shape = (quarter, quarter)
                same = same & (
                    lax.broadcasted_iota(jnp.int32, shape, 0)
                    <= lax.broadcasted_iota(jnp.int32, shape, 1)
                )
            mask[pl.ds(at, quarter), :] = jnp.where(same, 1.0, 0.0)
            at += quarter

    xb, normed = r["xb"], r["normed"]
    n_copies = []
    for k in range(2):
        wait_in(rows(xb, quarter * k, quarter), x_i + k)
        cen, rstd = row_stats(xb[pl.ds(quarter * k, quarter), :].astype(F32))
        normed[pl.ds(own0 + quarter * k, quarter), :] = (cen * rstd * gain_one).astype(BF)
        mine = rows(normed, own0 + quarter * k, quarter)
        n_copies.append(send(mine, mine, part))

    ag_last("q")
    qkv = r["qkv"]

    def qkv_rows(first):
        def step(k, _):
            ts = pl.ds(pl.multiple_of(first + quarter * k, quarter), quarter)
            qkv[ts, :] = nn(normed[ts, :], W["q"][...]).astype(BF)
            return 0

        lax.fori_loop(0, 2, step, 0)

    qkv_rows(own0)
    for copy in n_copies:
        copy.wait_recv()
    qkv_rows(oth0)
    ag_second("o")

    attended, lev = r["attended"], r["lev"]
    lane = lax.broadcasted_iota(jnp.int32, (1, LANES), 1)
    head_lane = [jnp.where(lane < LANES // 2, 1.0, 0.0), jnp.where(lane < LANES // 2, 0.0, 1.0)]
    head_bf = [v.astype(BF) for v in head_lane]
    scale = HEAD_DIM ** (-0.5)

    def attend(p):
        for b in range(4):
            at, k0, n = base[b]
            qs = pl.ds(quarter * b, quarter)
            ks = pl.ds(quarter * k0, n)
            query = qkv[qs, dcol(p * LANES, LANES)] * jnp.asarray(scale, BF)
            key = qkv[ks, dcol(hcols + p * LANES, LANES)]
            value = qkv[ks, dcol(2 * hcols + p * LANES, LANES)]
            allowed = mask[pl.ds(at, n), :]
            total_out = None
            for h in range(2):
                sm = nt(key, query * head_bf[h]) * allowed
                mag = jnp.abs(sm)
                top = jnp.max(mag, axis=0, keepdims=True)
                raw = jnp.exp(mag - top)
                low = jnp.exp(-top)
                total = jnp.sum(raw * allowed, axis=0, keepdims=True)
                sign = jnp.clip(sm * HUGE, -1.0, 1.0)
                signed = (sign * (raw - low) * (1.0 / total)).astype(BF)
                lev[2 * p + h, :, qs] = top + jnp.log(total)
                out = tn(signed, value * head_bf[h])
                total_out = out if total_out is None else total_out + out
            attended[qs, dcol(c * hcols + p * LANES, LANES)] = total_out.astype(BF)

    att_i = sems(pairs)

    def att_copy(p):
        cols = attended.at[:, dcol(c * hcols + p * LANES, LANES)]
        return remote(cols, cols, att_i + p, part)

    for p in range(pairs):
        attend(p)
        att_copy(p).start()
        ends.append(att_copy(p).wait_send)
        if p == 0:
            ag_second_u("u0")
            ag_last("o")
            half_o = W["o"].at[:, dcol(c * hcols, hcols)]
            o_copy = send(half_o, half_o, part)
        if p == 1:
            ag_second_u("u1")
            ag_third_u("u0")
            ag_first("d")
        if p == 2:
            ag_third_u("u1")
            for m in range(2):
                dst = rows(r["cb"], quarter * z, quarter)
                to_chip(cot.at[m], dst, c_i + zk, c_i + m, 2 * m + c, zh)
    o_copy.wait_recv()
    for p in range(pairs):
        att_copy(p).wait_recv()

    middle, n2 = r["middle"], r["n2"]
    n2_copies = []
    for k in range(2):
        ts = pl.ds(own0 + quarter * k, quarter)
        ls = pl.ds(quarter * k, quarter)
        mid_v = xb[ls, :].astype(F32) + nn(attended[ts, :], W["o"][...])
        middle[ls, :] = mid_v
        cen, rstd = row_stats(mid_v)
        n2[ts, :] = (cen * rstd * gain_two).astype(BF)
        mine = rows(n2, own0 + quarter * k, quarter)
        n2_copies.append(send(mine, mine, part))

    active, du = r["active"], r["du"]
    ft = 256
    nft = half_u // ft

    def up_rows(first, col):
        def step(i, _):
            ts = pl.ds(first + quarter * lax.div(i, nft), quarter)
            cols = dcol(col + ft * lax.rem(i, nft), ft)
            u = nn(n2[ts, :], W["u"][:, cols])
            u2 = u * u
            t = jnp.tanh(GELU_K * (u + GELU_C * u * u2))
            active[ts, cols] = (0.5 * u * (1.0 + t)).astype(BF)
            slope = 0.5 * (1.0 + t) + 0.5 * u * (1.0 - t * t) * (
                GELU_K * (1.0 + 3.0 * GELU_C * u2)
            )
            du[ts, cols] = slope.astype(BF)
            return 0

        lax.fori_loop(0, 2 * nft, step, 0)

    ag_last_u("u0")
    up_rows(own0, 0)
    for copy in n2_copies:
        copy.wait_recv()
    up_rows(oth0, 0)
    ag_last_u("u1")
    up_rows(own0, half_u)
    ag_second("d")
    wait_in(rows(W["d"], ffb * q, ffb), local_d)
    up_rows(oth0, half_u)

    def reduce_unit(name, ref, stride, off, n, cols, place):
        h2 = n // 2
        r1, r2, r3, r4 = (r[name + k] for k in ("1", "2", "3", "4"))
        fin = r3
        i1, i2, i3, i4 = sems(), sems(), sems(), sems()

        def at_rows(qq, first, count):
            return pl.ds(pl.multiple_of(qq * stride + off + first, 16), count), cols

        def q_of(yy, xx):
            return 2 * yy + xx

        def first():
            for k in range(2):
                remote(ref.at[at_rows(q_of(k, 1 - x), 0, h2)], r1.at[k], i1, nx).start()
                remote(ref.at[at_rows(q_of(1 - y, k), h2, h2)], r1.at[2 + k], i1, ny).start()
            ends.append(lambda: remote(r1, r1, i1, nx).wait_send())

        def second():
            wait_in(r1, i1)
            ra = at_rows(q_of(1 - y, x), 0, h2)
            ref[ra] = (ref[ra].astype(F32) + r1[1 - y].astype(F32)).astype(BF)
            remote(ref.at[ra], r2.at[0], i2, ny).start()
            rb = at_rows(q_of(y, 1 - x), h2, h2)
            ref[rb] = (ref[rb].astype(F32) + r1[3 - x].astype(F32)).astype(BF)
            remote(ref.at[rb], r2.at[1], i2, nx).start()
            ends.append(lambda: remote(r2, r2, i2, nx).wait_send())

        own = at_rows(q, 0, n)

        def third():
            wait_in(r2, i2)
            ra = at_rows(q, 0, h2)
            ref[ra] = (
                ref[ra].astype(F32) + r1[y].astype(F32) + r2[0].astype(F32)
            ).astype(BF)
            rb = at_rows(q, h2, h2)
            ref[rb] = (
                ref[rb].astype(F32) + r1[2 + x].astype(F32) + r2[1].astype(F32)
            ).astype(BF)

            @pl.when(edge)
            def _():
                remote(ref.at[own], r3, i3, zp).start()

        def fourth():
            @pl.when(mid)
            def _():
                wait_in(r3, i3)
                ref[own] = (ref[own].astype(F32) + r3[...].astype(F32)).astype(BF)
                remote(ref.at[own], r4, i4, zm).start()

        def fifth():
            @pl.when(mid)
            def _():
                wait_in(r4, i4)
                fin[...] = (ref[own].astype(F32) + r4[...].astype(F32)).astype(BF)
                remote(fin, fin, i3, zp).start()

        def last():
            @pl.when(edge)
            def _():
                wait_in(fin, i3)

            place(fin)

        def end():
            remote(ref.at[own], r3, i3, zp).wait_send()

            @pl.when(mid)
            def _():
                remote(ref.at[own], r4, i4, zm).wait_send()

        ends.append(end)
        return first, second, third, fourth, fifth, last

    waits = []

    def put(src, dst):
        i = sems()
        copy = pltpu.make_async_copy(src, dst, rsem.at[i])
        copy.start()
        waits.append(copy.wait)

    def by_core(fin, cuts, out):
        i_mine, i_his = sems(), sems()
        mine = pl.ds(pl.multiple_of(c * rows_dev, 32), rows_dev)
        his = pl.ds(pl.multiple_of((1 - c) * rows_dev, 32), rows_dev)
        for src_col, dst_col, n in cuts:
            src, dst = fin.at[his, pl.ds(src_col, n)], out.at[:, dcol(dst_col, n)]
            remote(src, dst, i_his, part).start()
            pltpu.make_async_copy(fin.at[mine, pl.ds(src_col, n)], dst, rsem.at[i_mine]).start()
        whole = fin.at[mine]
        waits.append(lambda: wait_in(whole, i_mine))
        waits.append(lambda: wait_in(whole, i_his))
        ends.append(lambda: remote(whole, whole, i_his, part).wait_send())

    def place_d(i, n):
        return lambda fin: put(fin, r["o_down"].at[pl.ds(n * i, n), :])

    def place_u(j):
        return lambda fin: by_core(fin, [(0, (2 * j + c) * ffb, ffb)], r["o_up"])

    def place_o(fin):
        by_core(fin, [(0, c * hcols, hcols)], r["o_out"])

    def place_q(p):
        cuts = [(t * LANES, t * width + c * hcols + p * LANES, LANES) for t in range(3)]
        return lambda fin: by_core(fin, cuts, r["o_qkv"])

    red = {}
    dn_rows = ffb // 4
    for i in range(4):
        name = "d%d" % i
        red[name] = reduce_unit(
            name, r["g_d"], ffb, dn_rows * i, dn_rows, slice(None), place_d(i, dn_rows)
        )
    for j in range(4):
        name = "u%d" % j
        red[name] = reduce_unit(
            name, r["g_u"], rows_chip, 0, rows_chip, pl.ds(ffb * j, ffb), place_u(j)
        )
    red["o"] = reduce_unit("o", r["g_o"], rows_chip, 0, rows_chip, slice(None), place_o)
    units = list(red)
    units += ["q%d" % p for p in range(pairs)]
    for p in range(pairs):
        name = "q%d" % p
        red[name] = reduce_unit(
            name, r["g_q"].at[p], rows_chip, 0, rows_chip, slice(None), place_q(p)
        )

    turn = iter(SCHEDULE)

    def stages():
        for at in next(turn):
            red[units[at // 6]][at % 6]()

    xs, xr, mixacc = r["xs"], r["xr"], r["mixacc"]

    def down(blk, first, into, fresh):
        w_rows = pl.ds(pl.multiple_of(ffb * blk, LANES), ffb)
        for k in range(2):
            ls = pl.ds(quarter * k, quarter)
            out = nn(active[pl.ds(first + quarter * k, quarter), dcol(ffb * blk, ffb)], W["d"][w_rows, :])
            into[ls, :] = out if fresh else into[ls, :] + out

    for i, blk in enumerate((q, qx, qy)):
        down(blk, oth0, xs.at[1], i == 0)
    ag_last("d")
    down(qd, oth0, xs.at[1], False)
    mix_copies = [
        send(xs.at[1, pl.ds(quarter * k, quarter), :], xr.at[1, pl.ds(quarter * k, quarter), :], part)
        for k in range(2)
    ]
    cb = r["cb"]
    c_copies = []
    for k in range(2):
        mine = rows(cb, own0 + quarter * k, quarter)
        wait_in(mine, c_i + k)
        c_copies.append(send(mine, mine, part))
    for k in range(2):
        ls = pl.ds(quarter * k, quarter)
        mixacc[ls, :] = nn(active[pl.ds(own0 + quarter * k, quarter), :], W["d"][...])

    def from_chip(buf, out, i0, k):
        zd = 2 * c + k
        src = buf.at[pl.ds(quarter * k, quarter), :]
        is_self = (zd == z) & (zk == c)
        dev = (zd, s - c + zk)
        dst = out.at[zh]

        @pl.when(is_self)
        def _():
            pltpu.make_async_copy(src, dst, rsem.at[i0 + zh]).start()

        @pl.when(jnp.logical_not(is_self))
        def _():
            remote(src, dst, i0 + zh, dev, i0 + k).start()

        def end():
            @pl.when(jnp.logical_not(is_self))
            def _():
                remote(src, dst, i0 + zh, dev, i0 + k).wait_send()

        ends.append(end)
        waits.append(functools.partial(wait_in, out.at[k], i0 + k))

    mo_i, to_i = sems(2), sems(2)
    mixb = r["mixb"]
    for k in range(2):
        ls = pl.ds(quarter * k, quarter)
        mix_copies[k].wait_recv()
        mixb[ls, :] = (middle[ls, :] + mixacc[ls, :] + xr[1, ls, :]).astype(BF)
        from_chip(mixb, r["o_mixed"], mo_i, k)

    for copy in c_copies:
        copy.wait_recv()
    gt = 256

    def grad_down_step(i, _):
        cols = dcol(gt * i, gt)
        r["g_d"][pl.ds(pl.multiple_of(gt * i, gt), gt), :] = tn(active[:, cols], cb[...]).astype(BF)
        return 0

    lax.fori_loop(0, ffh // gt, grad_down_step, 0)
    stages()

    fd = 512

    for k in range(4):

        def d_up_step(i, _):
            ts = pl.ds(quarter * k, quarter)
            cols = dcol(fd * i, fd)
            da = nt(cb[ts, :], W["d"][pl.ds(pl.multiple_of(fd * i, LANES), fd), :])
            du[ts, cols] = (da * du[ts, cols].astype(F32)).astype(BF)
            return 0

        lax.fori_loop(0, ffh // fd, d_up_step, 0)
        stages()

    def exchange(n, product_of):
        copies = []
        for k in range(2):
            ls = pl.ds(quarter * k, quarter)
            xs[n % 2, ls, :] = product_of(pl.ds(oth0 + quarter * k, quarter))
            copies.append(send(xs.at[n % 2, ls, :], xr.at[n % 2, ls, :], part))
        return copies

    dn2_copies = exchange(0, lambda ts: nt(du[ts, :], W["u"][...]))
    stages()
    dbr, gsum = r["dbr"], r["gsum"]
    gain_acc = jnp.zeros((1, width), F32)
    db_copies = []
    for k in range(2):
        ts = pl.ds(own0 + quarter * k, quarter)
        ls = pl.ds(quarter * k, quarter)
        dn = nt(du[ts, :], W["u"][...])
        dn2_copies[k].wait_recv()
        dn = dn + xr[0, ls, :]
        cen, rstd = row_stats(middle[ls, :])
        n = cen * rstd
        gain_acc = gain_acc + jnp.sum(dn * n, axis=0, keepdims=True)
        dmid = cb[ts, :].astype(F32) + norm_back(dn, n, rstd, gain_two)
        mixacc[ls, :] = dmid
        dbr[ts, :] = dmid.astype(BF)
        mine = rows(dbr, own0 + quarter * k, quarter)
        db_copies.append(send(mine, mine, part))
        stages()
    gsum[0, :, width:] = gain_acc

    for j in range(2):

        def grad_up_step(i, _):
            cols = dcol(gt * i, gt)
            out = tn(n2[:, cols], du[:, pl.ds(half_u * j, half_u)]).astype(BF)
            r["g_u"][pl.ds(pl.multiple_of(gt * i, gt), gt), pl.ds(half_u * j, half_u)] = out
            return 0

        lax.fori_loop(0, width // gt, grad_up_step, 0)
        stages()

    for copy in db_copies:
        copy.wait_recv()
    datt = r["datt"]

    def datt_step(k, _):
        ts = pl.ds(pl.multiple_of(quarter * k, quarter), quarter)
        w_rows = W["o"][pl.ds(pl.multiple_of(c * hcols, LANES), hcols), :]
        datt[ts, :] = nt(dbr[ts, :], w_rows).astype(BF)
        return 0

    lax.fori_loop(0, 4, datt_step, 0)
    stages()

    dk, dv = r["dk"], r["dv"]
    sel = (
        lax.broadcasted_iota(jnp.int32, (8, LANES), 0)
        == lax.div(lax.broadcasted_iota(jnp.int32, (8, LANES), 1), LANES // 2)
    ).astype(F32)

    def attend_back(p):
        dk[...] = jnp.zeros_like(dk)
        dv[...] = jnp.zeros_like(dv)
        for b in range(4):
            at, k0, n = base[b]
            qs = pl.ds(quarter * b, quarter)
            ks = pl.ds(quarter * k0, n)
            query = qkv[qs, dcol(p * LANES, LANES)] * jnp.asarray(scale, BF)
            key = qkv[ks, dcol(hcols + p * LANES, LANES)]
            value = qkv[ks, dcol(2 * hcols + p * LANES, LANES)]
            d_att = datt[qs, dcol(p * LANES, LANES)]
            att = attended[qs, dcol(c * hcols + p * LANES, LANES)]
            delta = nt(sel, d_att.astype(F32) * att.astype(F32), lax.Precision.HIGHEST)
            allowed = mask[pl.ds(at, n), :]
            d_query = None
            for h in range(2):
                q_h = query * head_bf[h]
                d_h = d_att * head_bf[h]
                sm = nt(key, q_h) * allowed
                mag = jnp.abs(sm)
                level = lev[2 * p + h, :, qs]
                prob = jnp.exp(mag - level)
                low = jnp.exp(-level)
                sign = jnp.clip(sm * HUGE, -1.0, 1.0)
                weight = (sign * (prob - low)).astype(BF)
                d_signed = nt(value, d_h)
                d_score = (prob * allowed * (d_signed - sign * delta[h : h + 1, :])).astype(BF)
                dv[ks, :] += nn(weight, d_h)
                dk[ks, :] += nn(d_score, q_h)
                out = tn(d_score, key * head_bf[h])
                d_query = out if d_query is None else d_query + out
            qkv[qs, dcol(p * LANES, LANES)] = (d_query * scale).astype(BF)
            stages()
        qkv[:, dcol(hcols + p * LANES, LANES)] = dk[...].astype(BF)
        qkv[:, dcol(2 * hcols + p * LANES, LANES)] = dv[...].astype(BF)

    def grad_qkv(p):
        def step(i, _):
            cols = dcol(gt * i, gt)
            d_pair = jnp.concatenate(
                [qkv[:, dcol(t * hcols + p * LANES, LANES)] for t in range(3)], axis=1
            )
            out = tn(normed[:, cols], d_pair).astype(BF)
            r["g_q"][p, pl.ds(pl.multiple_of(gt * i, gt), gt), :] = out
            return 0

        lax.fori_loop(0, width // gt, step, 0)

    def grad_out_step(i, _):
        cols = dcol(gt * i, gt)
        out = tn(attended[:, cols], dbr[:, dcol(c * hcols, hcols)]).astype(BF)
        r["g_o"][pl.ds(pl.multiple_of(gt * i, gt), gt), :] = out
        return 0

    attend_back(0)
    grad_qkv(0)
    stages()
    attend_back(1)
    grad_qkv(1)
    stages()
    lax.fori_loop(0, width // gt, grad_out_step, 0)
    stages()
    attend_back(2)
    grad_qkv(2)
    stages()

    for copy in dn2_copies:
        copy.wait_send()
        ends.remove(copy.wait_send)
    dn1_copies = exchange(2, lambda ts: nt(qkv[ts, :], W["q"][...]))
    stages()
    gtb = r["gtb"]
    gain_acc = jnp.zeros((1, width), F32)
    for k in range(2):
        ts = pl.ds(own0 + quarter * k, quarter)
        ls = pl.ds(quarter * k, quarter)
        dn = nt(qkv[ts, :], W["q"][...])
        dn1_copies[k].wait_recv()
        dn = dn + xr[0, ls, :]
        cen, rstd = row_stats(xb[ls, :].astype(F32))
        n = cen * rstd
        gain_acc = gain_acc + jnp.sum(dn * n, axis=0, keepdims=True)
        gtb[ls, :] = (mixacc[ls, :] + norm_back(dn, n, rstd, gain_one)).astype(BF)
        from_chip(gtb, r["o_gt"], to_i, k)
        stages()
    gsum[0, :, :width] = gain_acc

    g3, g4, g5 = sems(), sems(), sems()
    g_copy = send(gsum.at[0], gsum.at[1], part)
    stages()

    g_copy.wait_recv()
    gsum[2] = gsum[0] + gsum[1]
    g_copy = send(gsum.at[2], gsum.at[3], nx)
    stages()
    g_copy.wait_recv()
    gsum[4] = gsum[2] + gsum[3]
    g_copy = send(gsum.at[4], gsum.at[5], ny)
    stages()
    g_copy.wait_recv()
    gsum[6] = gsum[4] + gsum[5]

    @pl.when(edge)
    def _():
        remote(gsum.at[6], gsum.at[7], g3, zp).start()

    stages()

    @pl.when(mid)
    def _():
        remote(gsum.at[6], gsum.at[7], g3, zp).wait_recv()
        gsum[8] = gsum[6] + gsum[7]
        remote(gsum.at[8], gsum.at[9], g4, zm).start()

    stages()

    @pl.when(mid)
    def _():
        remote(gsum.at[8], gsum.at[9], g4, zm).wait_recv()
        gsum[10] = gsum[8] + gsum[9]
        remote(gsum.at[10], gsum.at[10], g5, zp).start()

    stages()

    @pl.when(mid)
    def _():
        remote(gsum.at[8], gsum.at[9], g4, zm).wait_send()
        remote(gsum.at[10], gsum.at[10], g5, zp).wait_send()

    @pl.when(edge)
    def _():
        remote(gsum.at[10], gsum.at[10], g5, zp).wait_recv()
        remote(gsum.at[6], gsum.at[7], g3, zp).wait_send()

    pick = (
        lax.broadcasted_iota(jnp.int32, (width, LANES), 0)
        == lax.broadcasted_iota(jnp.int32, (width, LANES), 1) + rows_dev * s
    ).astype(F32)
    for k in range(2):
        vec = jnp.broadcast_to(gsum[10][:, width * k : width * (k + 1)], (8, width))
        r["o_gains"][k : k + 1, :] = nn(vec, pick, lax.Precision.HIGHEST)[0:1, :rows_dev]
    for wait in waits:
        wait()
    for end in ends:
        end()
    assert used[0] <= N_SEMS, used[0]


def per_device_fast(tokens, segments, w_qkv, w_out, w_up, w_down, gain_one, gain_two, cotangent):
    micro, _, quarter, width = tokens.shape
    rows_dev = w_qkv.shape[0]
    ff = w_up.shape[1]
    ffb = w_down.shape[0]
    half, length = 2 * quarter, 4 * quarter
    hcols, ffh, rows_chip = width // 2, ff // 2, 2 * rows_dev
    pairs = hcols // LANES
    pcols = 3 * LANES
    scratch = {}

    def vm(name, shape, dtype=BF):
        scratch[name] = pltpu.VMEM(shape, dtype)

    vm("w_q", (width, pairs * pcols))
    vm("w_o", (width, width))
    vm("w_u", (width, ffh))
    vm("w_d", (ffh, width))
    vm("segs", (4, 1, quarter), jnp.int32)
    vm("segc", (length, LANES), F32)
    vm("mask", (9 * quarter, quarter), F32)
    vm("xb", (half, width))
    vm("cb", (length, width))
    vm("gains", (7, 1, 2 * width), F32)
    vm("gsum", (11, 1, 2 * width), F32)
    vm("normed", (length, width))
    vm("qkv", (length, pairs * pcols))
    vm("lev", (2 * pairs, 1, length), F32)
    vm("attended", (length, width))
    vm("middle", (half, width), F32)
    vm("n2", (length, width))
    vm("active", (length, ffh))
    vm("du", (length, ffh))
    vm("xs", (2, half, width), F32)
    vm("xr", (2, half, width), F32)
    vm("mixb", (half, width))
    vm("mixacc", (half, width), F32)
    vm("gtb", (half, width))
    vm("dbr", (length, width))
    vm("datt", (length, hcols))
    vm("dk", (length, LANES), F32)
    vm("dv", (length, LANES), F32)
    vm("g_d", (ffh, width))
    vm("g_u", (width, ffh))
    vm("g_o", (width, hcols))
    vm("g_q", (pairs, width, pcols))
    pieces = [("d%d" % i, ffb // 4, width) for i in range(4)]
    pieces += [("u%d" % j, rows_chip, ffb) for j in range(4)]
    pieces += [("o", rows_chip, hcols)]
    pieces += [("q%d" % p, rows_chip, pcols) for p in range(pairs)]
    for name, blk, cols in pieces:
        vm(name + "1", (4, blk // 2, cols))
        vm(name + "2", (2, blk // 2, cols))
        vm(name + "3", (blk, cols))
        vm(name + "4", (blk, cols))
    scratch["ssem"] = pltpu.SemaphoreType.DMA((N_SEMS,))
    scratch["rsem"] = pltpu.SemaphoreType.DMA((N_SEMS,))
    outs = {
        "o_mixed": ((micro, quarter, width), BF),
        "o_gt": ((micro, quarter, width), BF),
        "o_qkv": ((rows_dev, 3 * width), BF),
        "o_out": ((rows_dev, width), BF),
        "o_up": ((rows_dev, ff), BF),
        "o_down": ((ffb, width), BF),
        "o_gains": ((2, rows_dev), F32),
    }
    ins = ["tok", "seg", "wqkv", "wout", "wup", "wdn", "g1", "g2", "cot"]
    names = ins + list(outs) + list(scratch)
    hbm = pl.BlockSpec(memory_space=pl.ANY)
    vmem = pl.BlockSpec(memory_space=pltpu.VMEM)
    tokens_all = 2 * half
    flops = 6 * half * (width * (4 * width + 2 * ff)) + 14 * 9 * 6 * quarter * quarter * 128
    got = pl.pallas_call(
        functools.partial(layer_kernel, names),
        out_shape=[jax.ShapeDtypeStruct(*v) for v in outs.values()],
        in_specs=[vmem if k in ("g1", "g2") else hbm for k in ins],
        out_specs=[vmem if k == "o_gains" else hbm for k in outs],
        scratch_shapes=list(scratch.values()),
        compiler_params=pltpu.CompilerParams(
            collective_id=0, has_side_effects=True, vmem_limit_bytes=VMEM_LIMIT
        ),
        cost_estimate=pl.CostEstimate(
            flops=flops, bytes_accessed=20 * tokens_all * width, transcendentals=0
        ),
    )(
        tokens[:, 0],
        segments.reshape(micro, 1, quarter),
        w_qkv,
        w_out,
        w_up,
        w_down,
        gain_one[None],
        gain_two[None],
        cotangent[:, 0],
    )
    mixed, grad_tokens, g_qkv, g_out, g_up, g_down, g_gains = got
    return (
        mixed[:, None],
        grad_tokens.astype(F32)[:, None],
        g_qkv.astype(F32),
        g_out.astype(F32),
        g_up.astype(F32),
        g_down.astype(F32),
        g_gains[0],
        g_gains[1],
    )


VMEM_LIMIT = 62 * 1024 * 1024


def solution(mesh):
    placed = (
        P(None, "shard", "seq", None),
        P(None, "shard", "seq"),
        P("shard", None),
        P("shard", None),
        P("shard", None),
        P("shard", None),
        P("shard"),
        P("shard"),
        P(None, "shard", "seq", None),
    )
    chip_sized = mesh.shape["seq"] == 4 and mesh.shape["shard"] == 8
    return jax.shard_map(
        per_device_fast if chip_sized else per_device,
        mesh=mesh,
        in_specs=placed,
        out_specs=(
            P(None, "shard", "seq", None),
            P(None, "shard", "seq", None),
            P("shard", None),
            P("shard", None),
            P("shard", None),
            P("shard", None),
            P("shard"),
            P("shard"),
        ),
        check_vma=False,
    )
```

```python
import functools
import math

import jax
import jax.numpy as jnp
from jax import lax
from jax.experimental import pallas as pl
from jax.experimental.pallas import tpu as pltpu
from jax.sharding import PartitionSpec as P


HEADS = 12
HEAD_DIM = 64


epsilon = 1e-05
far_below = -1e30


def norm_rows(values, gain):
    row_mean = jnp.mean(values, axis=-1, keepdims=True)
    centred = values - row_mean
    spread = jnp.mean(centred * centred, axis=-1, keepdims=True)
    return centred * lax.rsqrt(spread + epsilon) * gain


def gelu_tanh(values):
    return jax.nn.gelu(values, approximate=True)


def product(left, right):
    return jnp.dot(left, right, preferred_element_type=jnp.float32)


def product_left_t(left, right):
    return lax.dot_general(
        left, right, (((0,), (0,)), ((), ())), preferred_element_type=jnp.float32
    )


def product_right_t(left, right):
    return lax.dot_general(
        left, right, (((1,), (1,)), ((), ())), preferred_element_type=jnp.float32
    )


def block_scores(query_block, keys, seg_rows, seg_cols, row_first, score_scale):
    rows_count = query_block.shape[0]
    cols_count = keys.shape[0]
    scores = (
        jnp.einsum("qhd,khd->hqk", query_block, keys, preferred_element_type=jnp.float32)
        * score_scale
    )
    row_pos = row_first + lax.broadcasted_iota(jnp.int32, (rows_count, cols_count), 0)
    col_pos = lax.broadcasted_iota(jnp.int32, (rows_count, cols_count), 1)
    allowed = (col_pos <= row_pos) & (seg_rows[:, None] == seg_cols[None, :])
    return (scores, allowed[None])


def attend_forward(queries, keys, values, seg_all, rows_block, score_scale):
    length = queries.shape[0]
    out_parts = []
    level_parts = []
    for row_first in range(0, length, rows_block):
        query_block = queries[row_first : row_first + rows_block]
        scores, allowed = block_scores(
            query_block,
            keys,
            seg_all[row_first : row_first + rows_block],
            seg_all,
            row_first,
            score_scale,
        )
        magnitude = jnp.abs(scores)
        row_top = jnp.max(jnp.where(allowed, magnitude, far_below), axis=-1, keepdims=True)
        exp_raw = jnp.where(allowed, jnp.exp(magnitude - row_top), 0.0)
        total = jnp.sum(exp_raw, axis=-1, keepdims=True)
        floor_term = jnp.where(allowed, jnp.exp(-row_top), 0.0)
        signed = (jnp.sign(scores) * (exp_raw - floor_term) / total).astype(jnp.bfloat16)
        out_parts.append(
            jnp.einsum("hqk,khd->qhd", signed, values, preferred_element_type=jnp.float32)
        )
        level_parts.append(row_top + jnp.log(total))
    return (jnp.concatenate(out_parts, axis=0), jnp.concatenate(level_parts, axis=1))


def attend_backward(queries, keys, values, seg_all, levels, d_heads, rows_block, score_scale):
    length = queries.shape[0]
    grad_keys = jnp.zeros(keys.shape, jnp.float32)
    grad_values = jnp.zeros(values.shape, jnp.float32)
    query_parts = []
    for row_first in range(0, length, rows_block):
        query_block = queries[row_first : row_first + rows_block]
        d_block = d_heads[row_first : row_first + rows_block]
        scores, allowed = block_scores(
            query_block,
            keys,
            seg_all[row_first : row_first + rows_block],
            seg_all,
            row_first,
            score_scale,
        )
        level_block = levels[:, row_first : row_first + rows_block]
        sign_part = jnp.sign(scores)
        prob = jnp.where(allowed, jnp.exp(jnp.abs(scores) - level_block), 0.0)
        weight = sign_part * jnp.where(allowed, prob - jnp.exp(-level_block), 0.0)
        d_signed = jnp.einsum("qhd,khd->hqk", d_block, values, preferred_element_type=jnp.float32)
        delta = jnp.sum(weight * d_signed, axis=-1, keepdims=True)
        d_score = (prob * (d_signed - sign_part * delta)).astype(jnp.bfloat16)
        query_parts.append(
            jnp.einsum("hqk,khd->qhd", d_score, keys, preferred_element_type=jnp.float32)
            * score_scale
        )
        grad_keys = (
            grad_keys
            + jnp.einsum("hqk,qhd->khd", d_score, query_block, preferred_element_type=jnp.float32)
            * score_scale
        )
        grad_values = grad_values + jnp.einsum(
            "hqk,qhd->khd", weight.astype(jnp.bfloat16), d_block, preferred_element_type=jnp.float32
        )
    grad_queries = jnp.concatenate(query_parts, axis=0)
    stacked = jnp.stack([grad_queries, grad_keys, grad_values], axis=1)
    heads_dev = queries.shape[1]
    return stacked.astype(jnp.bfloat16).reshape(length, 3, 1, heads_dev * queries.shape[2])


def per_device(tokens, segments, w_qkv, w_out, w_up, w_down, gain_one, gain_two, cotangent):
    micro_count = tokens.shape[0]
    tok_rows = tokens.shape[2]
    width = tokens.shape[3]
    groups = lax.axis_size("seq")
    heads_dev = HEADS // groups
    head_cols = heads_dev * HEAD_DIM
    length = tok_rows * groups
    rows_block = min(512, length)
    score_scale = HEAD_DIM ** (-0.5)
    totals = None
    shares = None
    results = []
    grad_rows = []
    for micro_idx in range(micro_count):
        whole = (
            lax.all_gather(w_qkv, "shard", axis=0, tiled=True),
            lax.all_gather(w_out, "shard", axis=0, tiled=True),
            lax.all_gather(w_up, "shard", axis=0, tiled=True),
            lax.all_gather(w_down, "shard", axis=0, tiled=True),
            lax.all_gather(gain_one, "shard", axis=0, tiled=True),
            lax.all_gather(gain_two, "shard", axis=0, tiled=True),
        )
        full_qkv, full_out, full_up, full_down = (whole[0], whole[1], whole[2], whole[3])
        gain_first = whole[4].astype(jnp.float32)
        gain_second = whole[5].astype(jnp.float32)
        tokens_f = tokens[micro_idx, 0].astype(jnp.float32)
        seg_local = segments[micro_idx, 0].astype(jnp.bfloat16)
        normed = norm_rows(tokens_f, gain_first).astype(jnp.bfloat16)
        packed = (
            product(normed, full_qkv).astype(jnp.bfloat16).reshape(tok_rows, 3, groups, head_cols)
        )
        seg_tile = jnp.broadcast_to(seg_local[:, None, None, None], (tok_rows, 1, groups, 1))
        received, seg_recv = (
            lax.all_to_all(packed, "seq", split_axis=2, concat_axis=0, tiled=True),
            lax.all_to_all(seg_tile, "seq", split_axis=2, concat_axis=0, tiled=True),
        )
        queries = received[:, 0, 0].reshape(length, heads_dev, HEAD_DIM)
        keys = received[:, 1, 0].reshape(length, heads_dev, HEAD_DIM)
        values = received[:, 2, 0].reshape(length, heads_dev, HEAD_DIM)
        seg_all = seg_recv[:, 0, 0, 0]
        heads_out, levels = attend_forward(queries, keys, values, seg_all, rows_block, score_scale)
        heads_low = heads_out.astype(jnp.bfloat16).reshape(length, 1, head_cols)
        attended = lax.all_to_all(
            heads_low, "seq", split_axis=0, concat_axis=1, tiled=True
        ).reshape(tok_rows, width)
        middle = tokens_f + product(attended, full_out)
        normed_two = norm_rows(middle, gain_second).astype(jnp.bfloat16)
        up_pre = product(normed_two, full_up)
        active = gelu_tanh(up_pre).astype(jnp.bfloat16)
        results.append((middle + product(active, full_down)).astype(jnp.bfloat16))
        again = (
            lax.all_gather(w_qkv, "shard", axis=0, tiled=True),
            lax.all_gather(w_out, "shard", axis=0, tiled=True),
            lax.all_gather(w_up, "shard", axis=0, tiled=True),
            lax.all_gather(w_down, "shard", axis=0, tiled=True),
            lax.all_gather(gain_one, "shard", axis=0, tiled=True),
            lax.all_gather(gain_two, "shard", axis=0, tiled=True),
        )
        back_qkv, back_out, back_up, back_down = (again[0], again[1], again[2], again[3])
        cot_low = cotangent[micro_idx, 0]
        grad_down_term = product_left_t(active, cot_low)
        d_active = product_right_t(cot_low, back_down)
        unused_gelu, gelu_pull = jax.vjp(gelu_tanh, up_pre)
        d_up = gelu_pull(d_active)[0].astype(jnp.bfloat16)
        grad_up_term = product_left_t(normed_two, d_up)
        d_norm_two = product_right_t(d_up, back_up)
        unused_second, second_pull = jax.vjp(norm_rows, middle, gain_second)
        d_middle_norm, grad_gain_two_term = second_pull(d_norm_two)
        d_middle = cot_low.astype(jnp.float32) + d_middle_norm
        d_branch = d_middle.astype(jnp.bfloat16)
        grad_out_term = product_left_t(attended, d_branch)
        d_attended = (
            product_right_t(d_branch, back_out)
            .astype(jnp.bfloat16)
            .reshape(tok_rows, groups, head_cols)
        )
        d_heads = lax.all_to_all(d_attended, "seq", split_axis=1, concat_axis=0, tiled=True)
        d_heads = d_heads[:, 0].reshape(length, heads_dev, HEAD_DIM)
        grad_heads = attend_backward(
            queries, keys, values, seg_all, levels, d_heads, rows_block, score_scale
        )
        d_packed = lax.all_to_all(
            grad_heads, "seq", split_axis=0, concat_axis=2, tiled=True
        ).reshape(tok_rows, 3 * width)
        grad_qkv_term = product_left_t(normed, d_packed)
        d_normed = product_right_t(d_packed, back_qkv)
        unused_first, first_pull = jax.vjp(norm_rows, tokens_f, gain_first)
        d_tokens_norm, grad_gain_one_term = first_pull(d_normed)
        grad_rows.append(d_middle + d_tokens_norm)
        terms = (
            grad_qkv_term,
            grad_out_term,
            grad_up_term,
            grad_down_term,
            grad_gain_one_term,
            grad_gain_two_term,
        )
        if totals is None:
            totals = terms
        else:
            totals = tuple((left_term + right_term for left_term, right_term in zip(totals, terms)))
    shares = (
        lax.psum_scatter(totals[0], "shard", scatter_dimension=0, tiled=True),
        lax.psum_scatter(totals[1], "shard", scatter_dimension=0, tiled=True),
        lax.psum_scatter(totals[2], "shard", scatter_dimension=0, tiled=True),
        lax.psum_scatter(totals[3], "shard", scatter_dimension=0, tiled=True),
        lax.psum_scatter(totals[4], "shard", scatter_dimension=0, tiled=True),
        lax.psum_scatter(totals[5], "shard", scatter_dimension=0, tiled=True),
    )
    replicas = lax.psum((shares[0], shares[1], shares[2], shares[3], shares[4], shares[5]), "seq")
    mixed = jnp.stack(results, axis=0)[:, None]
    grad_tokens = jnp.stack(grad_rows, axis=0)[:, None]
    return (
        mixed,
        grad_tokens,
        replicas[0],
        replicas[1],
        replicas[2],
        replicas[3],
        replicas[4],
        replicas[5],
    )


BF = jnp.bfloat16
F32 = jnp.float32
MESH = pl.DeviceIdType.MESH
N_SEMS = 132
SCHEDULE = (
    (0,),
    (6,),
    (12, 72, 73,),
    (1,),
    (18,),
    (7,),
    (),
    (13,),
    (2,),
    (19,),
    (8, 24, 30,),
    (14,),
    (20, 36,),
    (),
    (3, 25,),
    (42,),
    (9, 31,),
    (),
    (15, 4,),
    (37,),
    (21, 26, 54,),
    (10,),
    (43, 5,),
    (32, 16, 60,),
    (38,),
    (27, 22,),
    (48, 11,),
    (44, 33, 55, 17,),
    (28,),
    (39, 61, 66, 23,),
    (49, 45, 34, 74,),
    (56, 29, 75,),
    (62, 40, 35,),
    (67, 46, 50, 68,),
    (57, 41, 63,),
    (47, 51, 58, 69,),
    (64, 59, 52,),
    (65, 70, 53, 71,),
)

HUGE = 3.0e38
GELU_K = math.sqrt(2.0 / math.pi)
GELU_C = 0.044715
LANES = 128


def nt(left, right, precision=None):
    return lax.dot_general(
        left, right, (((1,), (1,)), ((), ())), preferred_element_type=F32, precision=precision
    )


def tn(left, right):
    return lax.dot_general(left, right, (((0,), (0,)), ((), ())), preferred_element_type=F32)


def nn(left, right, precision=None):
    return jnp.dot(left, right, preferred_element_type=F32, precision=precision)


def row_stats(v):
    mean = jnp.mean(v, axis=-1, keepdims=True)
    cen = v - mean
    var = jnp.mean(cen * cen, axis=-1, keepdims=True)
    return cen, lax.rsqrt(var + epsilon)


def norm_back(dn, n, rstd, gain):
    e = dn * gain
    return (e - jnp.mean(e, axis=-1, keepdims=True) - n * jnp.mean(e * n, axis=-1, keepdims=True)) * rstd


def layer_kernel(names, *refs):
    r = dict(zip(names, refs))
    tok, seg, wqkv, wout, wup, wdn, cot = (
        r[k] for k in ("tok", "seg", "wqkv", "wout", "wup", "wdn", "cot")
    )
    ssem, rsem = r["ssem"], r["rsem"]
    width = tok.shape[2]
    quarter = tok.shape[1]
    half = 2 * quarter
    length = 4 * quarter
    rows_dev = wqkv.shape[0]
    rows_chip = 2 * rows_dev
    hcols = width // 2
    pairs = hcols // LANES
    pcols = 3 * LANES
    ffh = wup.shape[1] // 2
    ffb = wdn.shape[0]

    z = lax.axis_index("seq")
    s = lax.axis_index("shard")
    c = lax.rem(s, 2)
    q = lax.div(s, 2)
    x = lax.rem(q, 2)
    y = lax.div(q, 2)
    part = (z, s + 1 - 2 * c)
    nx = (z, s + 2 - 4 * x)
    ny = (z, s + 4 - 8 * y)
    zp = (z + 1 - 2 * lax.rem(z, 2), s)
    zm = (3 - z, s)
    edge = lax.rem(z, 3) == 0
    mid = lax.rem(z, 3) != 0
    qx = q + 1 - 2 * x
    qy = q + 2 - 4 * y
    zh = lax.div(z, 2)
    zk = lax.rem(z, 2)
    own0 = pl.multiple_of(half * c, half)
    oth0 = pl.multiple_of(half * (1 - c), half)

    used = [0]
    ends = []

    def sems(n=1):
        first = used[0]
        used[0] += n
        return first

    def remote(src, dst, i, dev, j=None):
        return pltpu.make_async_remote_copy(
            src_ref=src,
            dst_ref=dst,
            send_sem=ssem.at[i if j is None else j],
            recv_sem=rsem.at[i],
            device_id=dev,
            device_id_type=MESH,
        )

    def send(src, dst, dev):
        copy = remote(src, dst, sems(), dev)
        copy.start()
        ends.append(copy.wait_send)
        return copy

    def wait_in(ref, i):
        pltpu.make_async_copy(ref, ref, rsem.at[i]).wait()

    def rows(ref, start, n, align=16):
        return ref.at[pl.ds(pl.multiple_of(start, align), n), :]

    nd = (z, s + 2 - 4 * x + 4 - 8 * y)
    qd = 3 - q

    peers = [part, nx, ny, nd]
    for dz in range(1, 4):
        zz = lax.rem(z + dz, 4)
        peers += [(zz, s), (zz, s + 1 - 2 * c)]
    bar = pltpu.get_barrier_semaphore()
    for dev in peers:
        pl.semaphore_signal(bar, inc=1, device_id=dev, device_id_type=MESH)
    spread = (
        lax.broadcasted_iota(jnp.int32, (rows_dev, width), 1)
        == lax.broadcasted_iota(jnp.int32, (rows_dev, width), 0) + rows_dev * s
    ).astype(F32)
    gains = r["gains"]
    for k, g in enumerate((r["g1"], r["g2"])):
        vec = jnp.broadcast_to(g[...].astype(F32), (8, rows_dev))
        gains[0, :, k * width : (k + 1) * width] = nn(vec, spread, lax.Precision.HIGHEST)[0:1, :]
    pl.semaphore_wait(bar, len(peers))

    seg_i = sems(4)
    x_i = sems(2)
    c_i = sems(2)

    def to_chip(src, dst, i_recv, i_send, zd, core):
        is_self = (zd == z) & (core == c)
        dev = (zd, s - c + core)

        @pl.when(is_self)
        def _():
            pltpu.make_async_copy(src, dst, rsem.at[i_recv]).start()

        @pl.when(jnp.logical_not(is_self))
        def _():
            remote(src, dst, i_recv, dev, i_send).start()

        def end():
            @pl.when(jnp.logical_not(is_self))
            def _():
                remote(src, dst, i_recv, dev, i_send).wait_send()

        ends.append(end)

    for m in range(2):
        to_chip(tok.at[m], rows(r["xb"], quarter * zk, quarter), x_i + zk, x_i + m, 2 * m + c, zh)

    my = pl.multiple_of(rows_dev * s, 32)
    partner_rows = pl.ds(pl.multiple_of(part[1] * rows_dev, 32), rows_dev)
    my_rows = pl.ds(my, rows_dev)
    local_d = sems()
    local_i = {name: sems() for name in ("q", "o", "u0", "u1")}
    flip_i = {name: sems() for name in ("q", "o", "u0", "u1")}
    W = {"q": r["w_q"], "o": r["w_o"], "u": r["w_u"], "d": r["w_d"]}

    def dcol(start, n):
        return pl.ds(pl.multiple_of(start, LANES), n)

    half_u = ffh // 2

    def cols_of(name):
        return {
            "q": slice(None),
            "o": dcol(c * hcols, hcols),
            "u0": pl.ds(0, half_u),
            "u1": pl.ds(half_u, half_u),
            "d0": slice(None),
            "d1": slice(None),
        }[name]

    def pieces(name, core):
        if name == "q":
            cuts = [(wqkv, t * width + core * hcols, t * hcols, hcols) for t in range(3)]
        elif name == "o":
            cuts = [(wout, core * hcols, core * hcols, hcols)]
        else:
            js = (0, 1) if name == "u0" else (2, 3)
            cuts = [(wup, (2 * j + core) * ffb, j * ffb, ffb) for j in js]
        for src, col, at, n in cuts:
            yield src.at[:, dcol(col, n)], W[name[0]].at[my_rows, dcol(at, n)]

    def block(name, first, n):
        return W[name[0]].at[pl.ds(pl.multiple_of(first, 32), n), cols_of(name)]

    ag = {}

    def flip(name):
        for src, dst in pieces(name, 1 - c):
            remote(src, dst, flip_i[name], part).start()

        def end():
            mine = block(name, my, rows_dev)
            remote(mine, mine, flip_i[name], part).wait_send()

        ends.append(end)

    def keep(name):
        for src, dst in pieces(name, c):
            pltpu.make_async_copy(src, dst, rsem.at[local_i[name]]).start()

    def ag_wait_sent(i, n_rows, name):
        both = W[name[0]].at[pl.ds(0, 2 * n_rows), cols_of(name)]
        ends.append(lambda: remote(both, both, i, nx).wait_send())

    def ag_own(name):
        i = sems()
        ag[name] = i
        for dev in (nx, ny):
            for src, dst in pieces(name, c):
                remote(src, dst, i, dev).start()
        ag_wait_sent(i, rows_chip, name)

    def ag_partner(name):
        his = block(name, part[1] * rows_dev, rows_dev)
        wait_in(his, flip_i[name])
        for dev in (nx, ny):
            remote(his, his, ag[name], dev).start()

    half_d = ffb // 2

    def span(name):
        return half_d if name[0] == "d" else rows_chip

    def chip_rows(name, qq, first, n):
        base = ffb * qq + half_d * int(name[1]) if name[0] == "d" else rows_chip * qq
        return block(name, base + first, n)

    def ag_first(name):
        if name[0] == "d":
            i = sems()
            ag[name] = i
            for dev in (nx, ny):
                src = wdn.at[pl.ds(half_d * int(name[1]), half_d), :]
                remote(src, chip_rows(name, q, 0, half_d), i, dev).start()
            ag_wait_sent(i, half_d, name)
        else:
            ag_own(name)
            ag_partner(name)

    def ag_second(name):
        n = span(name) // 2
        wait_in(W[name[0]].at[pl.ds(0, 4 * n), cols_of(name)], ag[name])
        i = sems()
        ag[name] = (i,)
        bx = chip_rows(name, qx, 0, n)
        by = chip_rows(name, qy, n, n)
        remote(bx, bx, i, ny).start()
        remote(by, by, i, nx).start()
        ag_wait_sent(i, n, name)

    def ag_last(name):
        wait_in(chip_rows(name, qd, 0, span(name)), ag[name][0])
        if name[0] != "d":
            wait_in(block(name, my, rows_dev), local_i[name])

    flip("q")
    ag_own("q")
    g_core = send(gains.at[0], gains.at[1], part)
    flip("o")
    ag_partner("q")
    ag_own("o")
    keep("q")
    keep("o")
    flip("u0")
    flip("u1")
    for m in range(2):
        for core in range(2):
            to_chip(seg.at[m], r["segs"].at[z], seg_i + z, seg_i + 2 * m + core, 2 * m + c, core)
    ag_partner("o")
    keep("u0")
    keep("u1")
    pltpu.make_async_copy(wdn, rows(W["d"], ffb * q, ffb), rsem.at[local_d]).start()

    g_core.wait_recv()
    gains[2] = gains[0] + gains[1]
    g_in = [send(gains.at[2], gains.at[3 + i], dev) for i, dev in enumerate((nx, ny, nd))]
    ag_second("q")
    ag_first("u0")
    ag_first("u1")
    for copy in g_in:
        copy.wait_recv()
    g_all = jnp.where(x == 0, gains[2], gains[3]) + jnp.where(x == 0, gains[3], gains[2])
    g_all = g_all + (gains[4] + gains[5])
    gains[6] = g_all
    gain_one = gains[6][:, :width]
    gain_two = gains[6][:, width:]

    segs, segc, mask = r["segs"], r["segc"], r["mask"]
    for b in range(4):
        wait_in(segs.at[b], seg_i + b)
    for b in range(4):
        tile = jnp.broadcast_to(segs[b].astype(F32), (LANES, quarter))
        segc[pl.ds(quarter * b, quarter), :] = jnp.transpose(tile)
    base = []
    at = 0
    for b in range(4):
        k0 = max(0, b - 2)
        base.append((at, k0, (b - k0 + 1) * quarter))
        for kb in range(k0, b + 1):
            col = segc[pl.ds(quarter * kb, quarter), :]
            same = jnp.concatenate([col] * (quarter // LANES), axis=1) == segs[b].astype(F32)
            if kb == b:
                shape = (quarter, quarter)
                same = same & (
                    lax.broadcasted_iota(jnp.int32, shape, 0)
                    <= lax.broadcasted_iota(jnp.int32, shape, 1)
                )
            mask[pl.ds(at, quarter), :] = jnp.where(same, 1.0, 0.0)
            at += quarter

    xb, normed = r["xb"], r["normed"]
    n_copies = []
    for k in range(2):
        wait_in(rows(xb, quarter * k, quarter), x_i + k)
        if k == 1:
            for m in range(2):
                dst = rows(r["cb"], quarter * z, quarter)
                to_chip(cot.at[m], dst, c_i + zk, c_i + m, 2 * m + c, zh)
        cen, rstd = row_stats(xb[pl.ds(quarter * k, quarter), :].astype(F32))
        normed[pl.ds(own0 + quarter * k, quarter), :] = (cen * rstd * gain_one).astype(BF)
        mine = rows(normed, own0 + quarter * k, quarter)
        n_copies.append(send(mine, mine, part))

    ag_last("q")
    qkv = r["qkv"]

    def qkv_rows(first):
        def step(k, _):
            ts = pl.ds(pl.multiple_of(first + quarter * k, quarter), quarter)
            qkv[ts, :] = nn(normed[ts, :], W["q"][...]).astype(BF)
            return 0

        lax.fori_loop(0, 2, step, 0)

    qkv_rows(own0)
    for copy in n_copies:
        copy.wait_recv()
    qkv_rows(oth0)
    ag_second("o")
    ag_second("u0")
    attended, lev = r["attended"], r["lev"]
    lane = lax.broadcasted_iota(jnp.int32, (1, LANES), 1)
    head_lane = [jnp.where(lane < LANES // 2, 1.0, 0.0), jnp.where(lane < LANES // 2, 0.0, 1.0)]
    head_bf = [v.astype(BF) for v in head_lane]
    scale = HEAD_DIM ** (-0.5)

    def attend(p):
        for b in range(4):
            at, k0, n = base[b]
            qs = pl.ds(quarter * b, quarter)
            ks = pl.ds(quarter * k0, n)
            query = qkv[qs, dcol(p * LANES, LANES)] * jnp.asarray(scale, BF)
            key = qkv[ks, dcol(hcols + p * LANES, LANES)]
            value = qkv[ks, dcol(2 * hcols + p * LANES, LANES)]
            allowed = mask[pl.ds(at, n), :]
            total_out = None
            for h in range(2):
                sm = nt(key, query * head_bf[h]) * allowed
                mag = jnp.abs(sm)
                top = jnp.max(mag, axis=0, keepdims=True)
                raw = jnp.exp(mag - top)
                low = jnp.exp(-top)
                total = jnp.sum(raw * allowed, axis=0, keepdims=True)
                sign = jnp.clip(sm * HUGE, -1.0, 1.0)
                signed = (sign * (raw - low) * (1.0 / total)).astype(BF)
                lev[2 * p + h, :, qs] = top + jnp.log(total)
                out = tn(signed, value * head_bf[h])
                total_out = out if total_out is None else total_out + out
            attended[qs, dcol(c * hcols + p * LANES, LANES)] = total_out.astype(BF)
            if p == 1 and b == 1:
                ag_second("u1")
                ag_first("d0")
                ag_first("d1")

    att_i = sems(pairs)

    def att_copy(p):
        cols = attended.at[:, dcol(c * hcols + p * LANES, LANES)]
        return remote(cols, cols, att_i + p, part)

    for p in range(pairs):
        attend(p)
        att_copy(p).start()
        ends.append(att_copy(p).wait_send)
        if p == 0:
            ag_last("o")
            half_o = W["o"].at[:, dcol(c * hcols, hcols)]
            o_copy = send(half_o, half_o, part)
    o_copy.wait_recv()
    for p in range(pairs):
        att_copy(p).wait_recv()

    middle, n2 = r["middle"], r["n2"]
    n2_copies = []
    for k in range(2):
        ts = pl.ds(own0 + quarter * k, quarter)
        ls = pl.ds(quarter * k, quarter)
        mid_v = xb[ls, :].astype(F32) + nn(attended[ts, :], W["o"][...])
        middle[ls, :] = mid_v
        cen, rstd = row_stats(mid_v)
        n2[ts, :] = (cen * rstd * gain_two).astype(BF)
        mine = rows(n2, own0 + quarter * k, quarter)
        n2_copies.append(send(mine, mine, part))

    cb = r["cb"]
    c_copies = []
    for k in range(2):
        mine = rows(cb, own0 + quarter * k, quarter)
        wait_in(mine, c_i + k)
        c_copies.append(send(mine, mine, part))

    active, du = r["active"], r["du"]
    ft = 256
    nft = half_u // ft

    def up_rows(first, col):
        def step(i, _):
            ts = pl.ds(first + quarter * lax.div(i, nft), quarter)
            cols = dcol(col + ft * lax.rem(i, nft), ft)
            u = nn(n2[ts, :], W["u"][:, cols])
            u2 = u * u
            t = jnp.tanh(GELU_K * (u + GELU_C * u * u2))
            active[ts, cols] = (0.5 * u * (1.0 + t)).astype(BF)
            slope = 0.5 * (1.0 + t) + 0.5 * u * (1.0 - t * t) * (
                GELU_K * (1.0 + 3.0 * GELU_C * u2)
            )
            du[ts, cols] = slope.astype(BF)
            return 0

        lax.fori_loop(0, 2 * nft, step, 0)

    ag_last("u0")
    up_rows(own0, 0)
    for copy in n2_copies:
        copy.wait_recv()
    ag_last("u1")
    up_rows(own0, half_u)
    ag_second("d0")
    up_rows(oth0, 0)
    up_rows(oth0, half_u)
    ag_second("d1")

    def reduce_unit(name, ref, stride, off, n, cols, place):
        h2 = n // 2
        r1, r2, r3, r4 = (r[name + k] for k in ("1", "2", "3", "4"))
        fin = r3
        i1, i2, i3, i4 = sems(), sems(), sems(), sems()

        def at_rows(qq, first, count):
            return pl.ds(pl.multiple_of(qq * stride + off + first, 16), count), cols

        def q_of(yy, xx):
            return 2 * yy + xx

        def first():
            for k in range(2):
                remote(ref.at[at_rows(q_of(k, 1 - x), 0, h2)], r1.at[k], i1, nx).start()
                remote(ref.at[at_rows(q_of(1 - y, k), h2, h2)], r1.at[2 + k], i1, ny).start()
            ends.append(lambda: remote(r1, r1, i1, nx).wait_send())

        def second():
            wait_in(r1, i1)
            ra = at_rows(q_of(1 - y, x), 0, h2)
            ref[ra] = (ref[ra].astype(F32) + r1[1 - y].astype(F32)).astype(BF)
            remote(ref.at[ra], r2.at[0], i2, ny).start()
            rb = at_rows(q_of(y, 1 - x), h2, h2)
            ref[rb] = (ref[rb].astype(F32) + r1[3 - x].astype(F32)).astype(BF)
            remote(ref.at[rb], r2.at[1], i2, nx).start()
            ends.append(lambda: remote(r2, r2, i2, nx).wait_send())

        own = at_rows(q, 0, n)

        def third():
            wait_in(r2, i2)
            ra = at_rows(q, 0, h2)
            ref[ra] = (
                ref[ra].astype(F32) + r1[y].astype(F32) + r2[0].astype(F32)
            ).astype(BF)
            rb = at_rows(q, h2, h2)
            ref[rb] = (
                ref[rb].astype(F32) + r1[2 + x].astype(F32) + r2[1].astype(F32)
            ).astype(BF)

            @pl.when(edge)
            def _():
                remote(ref.at[own], r3, i3, zp).start()

        def fourth():
            @pl.when(mid)
            def _():
                wait_in(r3, i3)
                ref[own] = (ref[own].astype(F32) + r3[...].astype(F32)).astype(BF)
                remote(ref.at[own], r4, i4, zm).start()

        def fifth():
            @pl.when(mid)
            def _():
                wait_in(r4, i4)
                fin[...] = (ref[own].astype(F32) + r4[...].astype(F32)).astype(BF)
                remote(fin, fin, i3, zp).start()

        def last():
            @pl.when(edge)
            def _():
                wait_in(fin, i3)

            place(fin)

        def end():
            remote(ref.at[own], r3, i3, zp).wait_send()

            @pl.when(mid)
            def _():
                remote(ref.at[own], r4, i4, zm).wait_send()

        ends.append(end)
        return first, second, third, fourth, fifth, last

    waits = []

    def put(src, dst):
        i = sems()
        copy = pltpu.make_async_copy(src, dst, rsem.at[i])
        copy.start()
        waits.append(copy.wait)

    def by_core(fin, cuts, out):
        i_mine, i_his = sems(), sems()
        mine = pl.ds(pl.multiple_of(c * rows_dev, 32), rows_dev)
        his = pl.ds(pl.multiple_of((1 - c) * rows_dev, 32), rows_dev)
        for src_col, dst_col, n in cuts:
            src, dst = fin.at[his, pl.ds(src_col, n)], out.at[:, dcol(dst_col, n)]
            remote(src, dst, i_his, part).start()
            pltpu.make_async_copy(fin.at[mine, pl.ds(src_col, n)], dst, rsem.at[i_mine]).start()
        whole = fin.at[mine]
        waits.append(lambda: wait_in(whole, i_mine))
        waits.append(lambda: wait_in(whole, i_his))
        ends.append(lambda: remote(whole, whole, i_his, part).wait_send())

    def place_d(i, n):
        return lambda fin: put(fin, r["o_down"].at[pl.ds(n * i, n), :])

    def place_u(j):
        return lambda fin: by_core(fin, [(0, (2 * j + c) * ffb, ffb)], r["o_up"])

    def place_o(fin):
        by_core(fin, [(0, c * hcols, hcols)], r["o_out"])

    def place_q(p):
        cuts = [(t * LANES, t * width + c * hcols + p * LANES, LANES) for t in range(3)]
        return lambda fin: by_core(fin, cuts, r["o_qkv"])

    red = {}
    dn_rows = ffb // 4
    for i in range(4):
        name = "d%d" % i
        red[name] = reduce_unit(
            name, r["g_d"], ffb, dn_rows * i, dn_rows, slice(None), place_d(i, dn_rows)
        )
    for j in range(4):
        name = "u%d" % j
        red[name] = reduce_unit(
            name, r["g_u"], rows_chip, 0, rows_chip, pl.ds(ffb * j, ffb), place_u(j)
        )
    red["o"] = reduce_unit("o", r["g_o"], rows_chip, 0, rows_chip, slice(None), place_o)
    units = list(red)
    units += ["q%d" % p for p in range(pairs)]
    for p in range(pairs):
        name = "q%d" % p
        red[name] = reduce_unit(
            name, r["g_q"].at[p], rows_chip, 0, rows_chip, slice(None), place_q(p)
        )

    turn = iter(SCHEDULE)

    def stages():
        for at in next(turn):
            if at < 6 * len(units):
                red[units[at // 6]][at % 6]()
            else:
                tokens_out(at - 6 * len(units))

    xs, xr, mixacc = r["xs"], r["xr"], r["mixacc"]

    def down(blk, first, into, fresh):
        w_rows = pl.ds(pl.multiple_of(ffb * blk, LANES), ffb)
        for k in range(2):
            ls = pl.ds(quarter * k, quarter)
            out = nn(active[pl.ds(first + quarter * k, quarter), dcol(ffb * blk, ffb)], W["d"][w_rows, :])
            into[ls, :] = out if fresh else into[ls, :] + out

    for copy in c_copies:
        copy.wait_recv()
    gt = 256

    def grad_down_step(i, _):
        cols = dcol(gt * i, gt)
        r["g_d"][pl.ds(pl.multiple_of(gt * i, gt), gt), :] = tn(active[:, cols], cb[...]).astype(BF)
        return 0

    lax.fori_loop(0, ffh // gt, grad_down_step, 0)
    wait_in(rows(W["d"], ffb * q, ffb), local_d)
    stages()

    for i, blk in enumerate((q, qx, qy)):
        down(blk, oth0, xs.at[1], i == 0)
    stages()
    ag_last("d0")
    ag_last("d1")
    down(qd, oth0, xs.at[1], False)
    mix_copies = [
        send(xs.at[1, pl.ds(quarter * k, quarter), :], xr.at[1, pl.ds(quarter * k, quarter), :], part)
        for k in range(2)
    ]
    for k in range(2):
        ls = pl.ds(quarter * k, quarter)
        mixacc[ls, :] = nn(active[pl.ds(own0 + quarter * k, quarter), :], W["d"][...])

    def from_chip(buf, out, i0, k):
        zd = 2 * c + k
        src = buf.at[pl.ds(quarter * k, quarter), :]
        is_self = (zd == z) & (zk == c)
        dev = (zd, s - c + zk)
        dst = out.at[zh]

        @pl.when(is_self)
        def _():
            pltpu.make_async_copy(src, dst, rsem.at[i0 + zh]).start()

        @pl.when(jnp.logical_not(is_self))
        def _():
            remote(src, dst, i0 + zh, dev, i0 + k).start()

        def end():
            @pl.when(jnp.logical_not(is_self))
            def _():
                remote(src, dst, i0 + zh, dev, i0 + k).wait_send()

        ends.append(end)
        waits.append(functools.partial(wait_in, out.at[k], i0 + k))

    mo_i, to_i = sems(2), sems(2)
    mixb = r["mixb"]
    for k in range(2):
        ls = pl.ds(quarter * k, quarter)
        mix_copies[k].wait_recv()
        mixb[ls, :] = (middle[ls, :] + mixacc[ls, :] + xr[1, ls, :]).astype(BF)

    def tokens_out(at):
        buf, out, i = (mixb, r["o_mixed"], mo_i) if at < 2 else (r["gtb"], r["o_gt"], to_i)
        from_chip(buf, out, i, at % 2)

    stages()

    fd = 512

    for k in range(4):

        def d_up_step(i, _):
            ts = pl.ds(quarter * k, quarter)
            cols = dcol(fd * i, fd)
            da = nt(cb[ts, :], W["d"][pl.ds(pl.multiple_of(fd * i, LANES), fd), :])
            du[ts, cols] = (da * du[ts, cols].astype(F32)).astype(BF)
            return 0

        lax.fori_loop(0, ffh // fd, d_up_step, 0)
        stages()

    def exchange(n, product_of):
        copies = []
        for k in range(2):
            ls = pl.ds(quarter * k, quarter)
            xs[n % 2, ls, :] = product_of(pl.ds(oth0 + quarter * k, quarter))
            copies.append(send(xs.at[n % 2, ls, :], xr.at[n % 2, ls, :], part))
        return copies

    dn2_copies = exchange(0, lambda ts: nt(du[ts, :], W["u"][...]))
    stages()
    dbr, gsum = r["dbr"], r["gsum"]
    gain_acc = jnp.zeros((1, width), F32)
    db_copies = []
    for k in range(2):
        ts = pl.ds(own0 + quarter * k, quarter)
        ls = pl.ds(quarter * k, quarter)
        dn = nt(du[ts, :], W["u"][...])
        dn2_copies[k].wait_recv()
        dn = dn + xr[0, ls, :]
        cen, rstd = row_stats(middle[ls, :])
        n = cen * rstd
        gain_acc = gain_acc + jnp.sum(dn * n, axis=0, keepdims=True)
        dmid = cb[ts, :].astype(F32) + norm_back(dn, n, rstd, gain_two)
        mixacc[ls, :] = dmid
        dbr[ts, :] = dmid.astype(BF)
        mine = rows(dbr, own0 + quarter * k, quarter)
        db_copies.append(send(mine, mine, part))
        stages()
    gsum[0, :, width:] = gain_acc

    for j in range(2):

        def grad_up_step(i, _):
            cols = dcol(gt * i, gt)
            out = tn(n2[:, cols], du[:, pl.ds(half_u * j, half_u)]).astype(BF)
            r["g_u"][pl.ds(pl.multiple_of(gt * i, gt), gt), pl.ds(half_u * j, half_u)] = out
            return 0

        lax.fori_loop(0, width // gt, grad_up_step, 0)
        stages()

    for copy in db_copies:
        copy.wait_recv()
    datt = r["datt"]

    def datt_step(k, _):
        ts = pl.ds(pl.multiple_of(quarter * k, quarter), quarter)
        w_rows = W["o"][pl.ds(pl.multiple_of(c * hcols, LANES), hcols), :]
        datt[ts, :] = nt(dbr[ts, :], w_rows).astype(BF)
        return 0

    lax.fori_loop(0, 4, datt_step, 0)
    stages()

    dk, dv = r["dk"], r["dv"]
    sel = (
        lax.broadcasted_iota(jnp.int32, (8, LANES), 0)
        == lax.div(lax.broadcasted_iota(jnp.int32, (8, LANES), 1), LANES // 2)
    ).astype(F32)

    def attend_back(p):
        dk[...] = jnp.zeros_like(dk)
        dv[...] = jnp.zeros_like(dv)
        for b in range(4):
            at, k0, n = base[b]
            qs = pl.ds(quarter * b, quarter)
            ks = pl.ds(quarter * k0, n)
            query = qkv[qs, dcol(p * LANES, LANES)] * jnp.asarray(scale, BF)
            key = qkv[ks, dcol(hcols + p * LANES, LANES)]
            value = qkv[ks, dcol(2 * hcols + p * LANES, LANES)]
            d_att = datt[qs, dcol(p * LANES, LANES)]
            att = attended[qs, dcol(c * hcols + p * LANES, LANES)]
            delta = nt(sel, d_att.astype(F32) * att.astype(F32), lax.Precision.HIGHEST)
            allowed = mask[pl.ds(at, n), :]
            d_query = None
            for h in range(2):
                q_h = query * head_bf[h]
                d_h = d_att * head_bf[h]
                sm = nt(key, q_h) * allowed
                mag = jnp.abs(sm)
                level = lev[2 * p + h, :, qs]
                prob = jnp.exp(mag - level)
                low = jnp.exp(-level)
                sign = jnp.clip(sm * HUGE, -1.0, 1.0)
                weight = (sign * (prob - low)).astype(BF)
                d_signed = nt(value, d_h)
                d_score = (prob * allowed * (d_signed - sign * delta[h : h + 1, :])).astype(BF)
                dv[ks, :] += nn(weight, d_h)
                dk[ks, :] += nn(d_score, q_h)
                out = tn(d_score, key * head_bf[h])
                d_query = out if d_query is None else d_query + out
            qkv[qs, dcol(p * LANES, LANES)] = (d_query * scale).astype(BF)
            stages()
        qkv[:, dcol(hcols + p * LANES, LANES)] = dk[...].astype(BF)
        qkv[:, dcol(2 * hcols + p * LANES, LANES)] = dv[...].astype(BF)

    def grad_qkv(p):
        def step(i, _):
            cols = dcol(gt * i, gt)
            d_pair = jnp.concatenate(
                [qkv[:, dcol(t * hcols + p * LANES, LANES)] for t in range(3)], axis=1
            )
            out = tn(normed[:, cols], d_pair).astype(BF)
            r["g_q"][p, pl.ds(pl.multiple_of(gt * i, gt), gt), :] = out
            return 0

        lax.fori_loop(0, width // gt, step, 0)

    def grad_out_step(i, _):
        cols = dcol(gt * i, gt)
        out = tn(attended[:, cols], dbr[:, dcol(c * hcols, hcols)]).astype(BF)
        r["g_o"][pl.ds(pl.multiple_of(gt * i, gt), gt), :] = out
        return 0

    attend_back(0)
    grad_qkv(0)
    stages()
    attend_back(1)
    grad_qkv(1)
    stages()
    lax.fori_loop(0, width // gt, grad_out_step, 0)
    stages()
    attend_back(2)

    for copy in dn2_copies:
        copy.wait_send()
        ends.remove(copy.wait_send)
    dn1_copies = exchange(2, lambda ts: nt(qkv[ts, :], W["q"][...]))
    stages()
    grad_qkv(2)
    stages()
    gtb = r["gtb"]
    gain_acc = jnp.zeros((1, width), F32)
    for k in range(2):
        ts = pl.ds(own0 + quarter * k, quarter)
        ls = pl.ds(quarter * k, quarter)
        dn = nt(qkv[ts, :], W["q"][...])
        dn1_copies[k].wait_recv()
        dn = dn + xr[0, ls, :]
        cen, rstd = row_stats(xb[ls, :].astype(F32))
        n = cen * rstd
        gain_acc = gain_acc + jnp.sum(dn * n, axis=0, keepdims=True)
        gtb[ls, :] = (mixacc[ls, :] + norm_back(dn, n, rstd, gain_one)).astype(BF)
        stages()
    gsum[0, :, :width] = gain_acc

    g3, g4, g5 = sems(), sems(), sems()
    g_copy = send(gsum.at[0], gsum.at[1], part)
    stages()

    g_copy.wait_recv()
    gsum[2] = gsum[0] + gsum[1]
    g_copy = send(gsum.at[2], gsum.at[3], nx)
    stages()
    g_copy.wait_recv()
    gsum[4] = gsum[2] + gsum[3]
    g_copy = send(gsum.at[4], gsum.at[5], ny)
    stages()
    g_copy.wait_recv()
    gsum[6] = gsum[4] + gsum[5]

    @pl.when(edge)
    def _():
        remote(gsum.at[6], gsum.at[7], g3, zp).start()

    stages()

    @pl.when(mid)
    def _():
        remote(gsum.at[6], gsum.at[7], g3, zp).wait_recv()
        gsum[8] = gsum[6] + gsum[7]
        remote(gsum.at[8], gsum.at[9], g4, zm).start()

    stages()

    @pl.when(mid)
    def _():
        remote(gsum.at[8], gsum.at[9], g4, zm).wait_recv()
        gsum[10] = gsum[8] + gsum[9]
        remote(gsum.at[10], gsum.at[10], g5, zp).start()

    stages()

    @pl.when(mid)
    def _():
        remote(gsum.at[8], gsum.at[9], g4, zm).wait_send()
        remote(gsum.at[10], gsum.at[10], g5, zp).wait_send()

    @pl.when(edge)
    def _():
        remote(gsum.at[10], gsum.at[10], g5, zp).wait_recv()
        remote(gsum.at[6], gsum.at[7], g3, zp).wait_send()

    pick = (
        lax.broadcasted_iota(jnp.int32, (width, LANES), 0)
        == lax.broadcasted_iota(jnp.int32, (width, LANES), 1) + rows_dev * s
    ).astype(F32)
    for k in range(2):
        vec = jnp.broadcast_to(gsum[10][:, width * k : width * (k + 1)], (8, width))
        r["o_gains"][k : k + 1, :] = nn(vec, pick, lax.Precision.HIGHEST)[0:1, :rows_dev]
    for wait in waits:
        wait()
    for end in ends:
        end()
    assert used[0] <= N_SEMS, used[0]


def per_device_fast(tokens, segments, w_qkv, w_out, w_up, w_down, gain_one, gain_two, cotangent):
    micro, _, quarter, width = tokens.shape
    rows_dev = w_qkv.shape[0]
    ff = w_up.shape[1]
    ffb = w_down.shape[0]
    half, length = 2 * quarter, 4 * quarter
    hcols, ffh, rows_chip = width // 2, ff // 2, 2 * rows_dev
    pairs = hcols // LANES
    pcols = 3 * LANES
    scratch = {}

    def vm(name, shape, dtype=BF):
        scratch[name] = pltpu.VMEM(shape, dtype)

    vm("w_q", (width, pairs * pcols))
    vm("w_o", (width, width))
    vm("w_u", (width, ffh))
    vm("w_d", (ffh, width))
    vm("segs", (4, 1, quarter), jnp.int32)
    vm("segc", (length, LANES), F32)
    vm("mask", (9 * quarter, quarter), F32)
    vm("xb", (half, width))
    vm("cb", (length, width))
    vm("gains", (7, 1, 2 * width), F32)
    vm("gsum", (11, 1, 2 * width), F32)
    vm("normed", (length, width))
    vm("qkv", (length, pairs * pcols))
    vm("lev", (2 * pairs, 1, length), F32)
    vm("attended", (length, width))
    vm("middle", (half, width), F32)
    vm("n2", (length, width))
    vm("active", (length, ffh))
    vm("du", (length, ffh))
    vm("xs", (2, half, width), F32)
    vm("xr", (2, half, width), F32)
    vm("mixb", (half, width))
    vm("mixacc", (half, width), F32)
    vm("gtb", (half, width))
    vm("dbr", (length, width))
    vm("datt", (length, hcols))
    vm("dk", (length, LANES), F32)
    vm("dv", (length, LANES), F32)
    vm("g_d", (ffh, width))
    vm("g_u", (width, ffh))
    vm("g_o", (width, hcols))
    vm("g_q", (pairs, width, pcols))
    pieces = [("d%d" % i, ffb // 4, width) for i in range(4)]
    pieces += [("u%d" % j, rows_chip, ffb) for j in range(4)]
    pieces += [("o", rows_chip, hcols)]
    pieces += [("q%d" % p, rows_chip, pcols) for p in range(pairs)]
    for name, blk, cols in pieces:
        vm(name + "1", (4, blk // 2, cols))
        vm(name + "2", (2, blk // 2, cols))
        vm(name + "3", (blk, cols))
        vm(name + "4", (blk, cols))
    scratch["ssem"] = pltpu.SemaphoreType.DMA((N_SEMS,))
    scratch["rsem"] = pltpu.SemaphoreType.DMA((N_SEMS,))
    outs = {
        "o_mixed": ((micro, quarter, width), BF),
        "o_gt": ((micro, quarter, width), BF),
        "o_qkv": ((rows_dev, 3 * width), BF),
        "o_out": ((rows_dev, width), BF),
        "o_up": ((rows_dev, ff), BF),
        "o_down": ((ffb, width), BF),
        "o_gains": ((2, rows_dev), F32),
    }
    ins = ["tok", "seg", "wqkv", "wout", "wup", "wdn", "g1", "g2", "cot"]
    names = ins + list(outs) + list(scratch)
    hbm = pl.BlockSpec(memory_space=pl.ANY)
    vmem = pl.BlockSpec(memory_space=pltpu.VMEM)
    tokens_all = 2 * half
    flops = 6 * half * (width * (4 * width + 2 * ff)) + 14 * 9 * 6 * quarter * quarter * 128
    got = pl.pallas_call(
        functools.partial(layer_kernel, names),
        out_shape=[jax.ShapeDtypeStruct(*v) for v in outs.values()],
        in_specs=[vmem if k in ("g1", "g2") else hbm for k in ins],
        out_specs=[vmem if k == "o_gains" else hbm for k in outs],
        scratch_shapes=list(scratch.values()),
        compiler_params=pltpu.CompilerParams(
            collective_id=0, has_side_effects=True, vmem_limit_bytes=VMEM_LIMIT
        ),
        cost_estimate=pl.CostEstimate(
            flops=flops, bytes_accessed=20 * tokens_all * width, transcendentals=0
        ),
    )(
        tokens[:, 0],
        segments.reshape(micro, 1, quarter),
        w_qkv,
        w_out,
        w_up,
        w_down,
        gain_one[None],
        gain_two[None],
        cotangent[:, 0],
    )
    mixed, grad_tokens, g_qkv, g_out, g_up, g_down, g_gains = got
    return (
        mixed[:, None],
        grad_tokens.astype(F32)[:, None],
        g_qkv.astype(F32),
        g_out.astype(F32),
        g_up.astype(F32),
        g_down.astype(F32),
        g_gains[0],
        g_gains[1],
    )


VMEM_LIMIT = 62 * 1024 * 1024


def solution(mesh):
    placed = (
        P(None, "shard", "seq", None),
        P(None, "shard", "seq"),
        P("shard", None),
        P("shard", None),
        P("shard", None),
        P("shard", None),
        P("shard"),
        P("shard"),
        P(None, "shard", "seq", None),
    )
    chip_sized = mesh.shape["seq"] == 4 and mesh.shape["shard"] == 8
    return jax.shard_map(
        per_device_fast if chip_sized else per_device,
        mesh=mesh,
        in_specs=placed,
        out_specs=(
            P(None, "shard", "seq", None),
            P(None, "shard", "seq", None),
            P("shard", None),
            P("shard", None),
            P("shard", None),
            P("shard", None),
            P("shard"),
            P("shard"),
        ),
        check_vma=False,
    )
```

```python
import functools
import math

import jax
import jax.numpy as jnp
from jax import lax
from jax.experimental import pallas as pl
from jax.experimental.pallas import tpu as pltpu
from jax.sharding import PartitionSpec as P


HEADS = 12
HEAD_DIM = 64


epsilon = 1e-05
far_below = -1e30


def norm_rows(values, gain):
    row_mean = jnp.mean(values, axis=-1, keepdims=True)
    centred = values - row_mean
    spread = jnp.mean(centred * centred, axis=-1, keepdims=True)
    return centred * lax.rsqrt(spread + epsilon) * gain


def gelu_tanh(values):
    return jax.nn.gelu(values, approximate=True)


def product(left, right):
    return jnp.dot(left, right, preferred_element_type=jnp.float32)


def product_left_t(left, right):
    return lax.dot_general(
        left, right, (((0,), (0,)), ((), ())), preferred_element_type=jnp.float32
    )


def product_right_t(left, right):
    return lax.dot_general(
        left, right, (((1,), (1,)), ((), ())), preferred_element_type=jnp.float32
    )


def block_scores(query_block, keys, seg_rows, seg_cols, row_first, score_scale):
    rows_count = query_block.shape[0]
    cols_count = keys.shape[0]
    scores = (
        jnp.einsum("qhd,khd->hqk", query_block, keys, preferred_element_type=jnp.float32)
        * score_scale
    )
    row_pos = row_first + lax.broadcasted_iota(jnp.int32, (rows_count, cols_count), 0)
    col_pos = lax.broadcasted_iota(jnp.int32, (rows_count, cols_count), 1)
    allowed = (col_pos <= row_pos) & (seg_rows[:, None] == seg_cols[None, :])
    return (scores, allowed[None])


def attend_forward(queries, keys, values, seg_all, rows_block, score_scale):
    length = queries.shape[0]
    out_parts = []
    level_parts = []
    for row_first in range(0, length, rows_block):
        query_block = queries[row_first : row_first + rows_block]
        scores, allowed = block_scores(
            query_block,
            keys,
            seg_all[row_first : row_first + rows_block],
            seg_all,
            row_first,
            score_scale,
        )
        magnitude = jnp.abs(scores)
        row_top = jnp.max(jnp.where(allowed, magnitude, far_below), axis=-1, keepdims=True)
        exp_raw = jnp.where(allowed, jnp.exp(magnitude - row_top), 0.0)
        total = jnp.sum(exp_raw, axis=-1, keepdims=True)
        floor_term = jnp.where(allowed, jnp.exp(-row_top), 0.0)
        signed = (jnp.sign(scores) * (exp_raw - floor_term) / total).astype(jnp.bfloat16)
        out_parts.append(
            jnp.einsum("hqk,khd->qhd", signed, values, preferred_element_type=jnp.float32)
        )
        level_parts.append(row_top + jnp.log(total))
    return (jnp.concatenate(out_parts, axis=0), jnp.concatenate(level_parts, axis=1))


def attend_backward(queries, keys, values, seg_all, levels, d_heads, rows_block, score_scale):
    length = queries.shape[0]
    grad_keys = jnp.zeros(keys.shape, jnp.float32)
    grad_values = jnp.zeros(values.shape, jnp.float32)
    query_parts = []
    for row_first in range(0, length, rows_block):
        query_block = queries[row_first : row_first + rows_block]
        d_block = d_heads[row_first : row_first + rows_block]
        scores, allowed = block_scores(
            query_block,
            keys,
            seg_all[row_first : row_first + rows_block],
            seg_all,
            row_first,
            score_scale,
        )
        level_block = levels[:, row_first : row_first + rows_block]
        sign_part = jnp.sign(scores)
        prob = jnp.where(allowed, jnp.exp(jnp.abs(scores) - level_block), 0.0)
        weight = sign_part * jnp.where(allowed, prob - jnp.exp(-level_block), 0.0)
        d_signed = jnp.einsum("qhd,khd->hqk", d_block, values, preferred_element_type=jnp.float32)
        delta = jnp.sum(weight * d_signed, axis=-1, keepdims=True)
        d_score = (prob * (d_signed - sign_part * delta)).astype(jnp.bfloat16)
        query_parts.append(
            jnp.einsum("hqk,khd->qhd", d_score, keys, preferred_element_type=jnp.float32)
            * score_scale
        )
        grad_keys = (
            grad_keys
            + jnp.einsum("hqk,qhd->khd", d_score, query_block, preferred_element_type=jnp.float32)
            * score_scale
        )
        grad_values = grad_values + jnp.einsum(
            "hqk,qhd->khd", weight.astype(jnp.bfloat16), d_block, preferred_element_type=jnp.float32
        )
    grad_queries = jnp.concatenate(query_parts, axis=0)
    stacked = jnp.stack([grad_queries, grad_keys, grad_values], axis=1)
    heads_dev = queries.shape[1]
    return stacked.astype(jnp.bfloat16).reshape(length, 3, 1, heads_dev * queries.shape[2])


def per_device(tokens, segments, w_qkv, w_out, w_up, w_down, gain_one, gain_two, cotangent):
    micro_count = tokens.shape[0]
    tok_rows = tokens.shape[2]
    width = tokens.shape[3]
    groups = lax.axis_size("seq")
    heads_dev = HEADS // groups
    head_cols = heads_dev * HEAD_DIM
    length = tok_rows * groups
    rows_block = min(512, length)
    score_scale = HEAD_DIM ** (-0.5)
    totals = None
    shares = None
    results = []
    grad_rows = []
    for micro_idx in range(micro_count):
        whole = (
            lax.all_gather(w_qkv, "shard", axis=0, tiled=True),
            lax.all_gather(w_out, "shard", axis=0, tiled=True),
            lax.all_gather(w_up, "shard", axis=0, tiled=True),
            lax.all_gather(w_down, "shard", axis=0, tiled=True),
            lax.all_gather(gain_one, "shard", axis=0, tiled=True),
            lax.all_gather(gain_two, "shard", axis=0, tiled=True),
        )
        full_qkv, full_out, full_up, full_down = (whole[0], whole[1], whole[2], whole[3])
        gain_first = whole[4].astype(jnp.float32)
        gain_second = whole[5].astype(jnp.float32)
        tokens_f = tokens[micro_idx, 0].astype(jnp.float32)
        seg_local = segments[micro_idx, 0].astype(jnp.bfloat16)
        normed = norm_rows(tokens_f, gain_first).astype(jnp.bfloat16)
        packed = (
            product(normed, full_qkv).astype(jnp.bfloat16).reshape(tok_rows, 3, groups, head_cols)
        )
        seg_tile = jnp.broadcast_to(seg_local[:, None, None, None], (tok_rows, 1, groups, 1))
        received, seg_recv = (
            lax.all_to_all(packed, "seq", split_axis=2, concat_axis=0, tiled=True),
            lax.all_to_all(seg_tile, "seq", split_axis=2, concat_axis=0, tiled=True),
        )
        queries = received[:, 0, 0].reshape(length, heads_dev, HEAD_DIM)
        keys = received[:, 1, 0].reshape(length, heads_dev, HEAD_DIM)
        values = received[:, 2, 0].reshape(length, heads_dev, HEAD_DIM)
        seg_all = seg_recv[:, 0, 0, 0]
        heads_out, levels = attend_forward(queries, keys, values, seg_all, rows_block, score_scale)
        heads_low = heads_out.astype(jnp.bfloat16).reshape(length, 1, head_cols)
        attended = lax.all_to_all(
            heads_low, "seq", split_axis=0, concat_axis=1, tiled=True
        ).reshape(tok_rows, width)
        middle = tokens_f + product(attended, full_out)
        normed_two = norm_rows(middle, gain_second).astype(jnp.bfloat16)
        up_pre = product(normed_two, full_up)
        active = gelu_tanh(up_pre).astype(jnp.bfloat16)
        results.append((middle + product(active, full_down)).astype(jnp.bfloat16))
        again = (
            lax.all_gather(w_qkv, "shard", axis=0, tiled=True),
            lax.all_gather(w_out, "shard", axis=0, tiled=True),
            lax.all_gather(w_up, "shard", axis=0, tiled=True),
            lax.all_gather(w_down, "shard", axis=0, tiled=True),
            lax.all_gather(gain_one, "shard", axis=0, tiled=True),
            lax.all_gather(gain_two, "shard", axis=0, tiled=True),
        )
        back_qkv, back_out, back_up, back_down = (again[0], again[1], again[2], again[3])
        cot_low = cotangent[micro_idx, 0]
        grad_down_term = product_left_t(active, cot_low)
        d_active = product_right_t(cot_low, back_down)
        unused_gelu, gelu_pull = jax.vjp(gelu_tanh, up_pre)
        d_up = gelu_pull(d_active)[0].astype(jnp.bfloat16)
        grad_up_term = product_left_t(normed_two, d_up)
        d_norm_two = product_right_t(d_up, back_up)
        unused_second, second_pull = jax.vjp(norm_rows, middle, gain_second)
        d_middle_norm, grad_gain_two_term = second_pull(d_norm_two)
        d_middle = cot_low.astype(jnp.float32) + d_middle_norm
        d_branch = d_middle.astype(jnp.bfloat16)
        grad_out_term = product_left_t(attended, d_branch)
        d_attended = (
            product_right_t(d_branch, back_out)
            .astype(jnp.bfloat16)
            .reshape(tok_rows, groups, head_cols)
        )
        d_heads = lax.all_to_all(d_attended, "seq", split_axis=1, concat_axis=0, tiled=True)
        d_heads = d_heads[:, 0].reshape(length, heads_dev, HEAD_DIM)
        grad_heads = attend_backward(
            queries, keys, values, seg_all, levels, d_heads, rows_block, score_scale
        )
        d_packed = lax.all_to_all(
            grad_heads, "seq", split_axis=0, concat_axis=2, tiled=True
        ).reshape(tok_rows, 3 * width)
        grad_qkv_term = product_left_t(normed, d_packed)
        d_normed = product_right_t(d_packed, back_qkv)
        unused_first, first_pull = jax.vjp(norm_rows, tokens_f, gain_first)
        d_tokens_norm, grad_gain_one_term = first_pull(d_normed)
        grad_rows.append(d_middle + d_tokens_norm)
        terms = (
            grad_qkv_term,
            grad_out_term,
            grad_up_term,
            grad_down_term,
            grad_gain_one_term,
            grad_gain_two_term,
        )
        if totals is None:
            totals = terms
        else:
            totals = tuple((left_term + right_term for left_term, right_term in zip(totals, terms)))
    shares = (
        lax.psum_scatter(totals[0], "shard", scatter_dimension=0, tiled=True),
        lax.psum_scatter(totals[1], "shard", scatter_dimension=0, tiled=True),
        lax.psum_scatter(totals[2], "shard", scatter_dimension=0, tiled=True),
        lax.psum_scatter(totals[3], "shard", scatter_dimension=0, tiled=True),
        lax.psum_scatter(totals[4], "shard", scatter_dimension=0, tiled=True),
        lax.psum_scatter(totals[5], "shard", scatter_dimension=0, tiled=True),
    )
    replicas = lax.psum((shares[0], shares[1], shares[2], shares[3], shares[4], shares[5]), "seq")
    mixed = jnp.stack(results, axis=0)[:, None]
    grad_tokens = jnp.stack(grad_rows, axis=0)[:, None]
    return (
        mixed,
        grad_tokens,
        replicas[0],
        replicas[1],
        replicas[2],
        replicas[3],
        replicas[4],
        replicas[5],
    )


BF = jnp.bfloat16
F32 = jnp.float32
MESH = pl.DeviceIdType.MESH
N_SEMS = 132
SCHEDULE = (
    (0,),
    (6,),
    (12, 72, 73,),
    (1,),
    (18,),
    (7,),
    (),
    (13,),
    (2,),
    (19,),
    (8, 24, 30,),
    (14,),
    (20, 36,),
    (),
    (3, 25,),
    (42,),
    (9, 31,),
    (),
    (15, 4,),
    (37,),
    (21, 26, 54,),
    (10,),
    (43, 5,),
    (32, 16, 60,),
    (38,),
    (27, 22,),
    (48, 11,),
    (44, 33, 55, 17,),
    (28,),
    (39, 61, 66, 23,),
    (49, 45, 34,),
    (56, 29,),
    (62, 40, 74, 75,),
    (35, 67, 46, 76, 50,),
    (57, 41, 68, 63, 47,),
    (58, 77, 78, 51, 64,),
    (59, 69, 52, 79, 65,),
    (80, 70, 81, 53, 71,),
)

HUGE = 3.0e38
GELU_K = math.sqrt(2.0 / math.pi)
GELU_C = 0.044715
LANES = 128


def nt(left, right, precision=None):
    return lax.dot_general(
        left, right, (((1,), (1,)), ((), ())), preferred_element_type=F32, precision=precision
    )


def tn(left, right):
    return lax.dot_general(left, right, (((0,), (0,)), ((), ())), preferred_element_type=F32)


def nn(left, right, precision=None):
    return jnp.dot(left, right, preferred_element_type=F32, precision=precision)


def row_stats(v):
    mean = jnp.mean(v, axis=-1, keepdims=True)
    cen = v - mean
    var = jnp.mean(cen * cen, axis=-1, keepdims=True)
    return cen, lax.rsqrt(var + epsilon)


def norm_back(dn, n, rstd, gain):
    e = dn * gain
    return (e - jnp.mean(e, axis=-1, keepdims=True) - n * jnp.mean(e * n, axis=-1, keepdims=True)) * rstd


def layer_kernel(names, *refs):
    r = dict(zip(names, refs))
    tok, seg, wqkv, wout, wup, wdn, cot = (
        r[k] for k in ("tok", "seg", "wqkv", "wout", "wup", "wdn", "cot")
    )
    ssem, rsem = r["ssem"], r["rsem"]
    width = tok.shape[2]
    quarter = tok.shape[1]
    half = 2 * quarter
    length = 4 * quarter
    rows_dev = wqkv.shape[0]
    rows_chip = 2 * rows_dev
    hcols = width // 2
    pairs = hcols // LANES
    pcols = 3 * LANES
    ffh = wup.shape[1] // 2
    ffb = wdn.shape[0]

    z = lax.axis_index("seq")
    s = lax.axis_index("shard")
    c = lax.rem(s, 2)
    q = lax.div(s, 2)
    x = lax.rem(q, 2)
    y = lax.div(q, 2)
    part = (z, s + 1 - 2 * c)
    nx = (z, s + 2 - 4 * x)
    ny = (z, s + 4 - 8 * y)
    zp = (z + 1 - 2 * lax.rem(z, 2), s)
    zm = (3 - z, s)
    edge = lax.rem(z, 3) == 0
    mid = lax.rem(z, 3) != 0
    qx = q + 1 - 2 * x
    qy = q + 2 - 4 * y
    zh = lax.div(z, 2)
    zk = lax.rem(z, 2)
    own0 = pl.multiple_of(half * c, half)
    oth0 = pl.multiple_of(half * (1 - c), half)

    used = [0]
    ends = []

    def sems(n=1):
        first = used[0]
        used[0] += n
        return first

    def remote(src, dst, i, dev, j=None):
        return pltpu.make_async_remote_copy(
            src_ref=src,
            dst_ref=dst,
            send_sem=ssem.at[i if j is None else j],
            recv_sem=rsem.at[i],
            device_id=dev,
            device_id_type=MESH,
        )

    def send(src, dst, dev):
        copy = remote(src, dst, sems(), dev)
        copy.start()
        ends.append(copy.wait_send)
        return copy

    def wait_in(ref, i):
        pltpu.make_async_copy(ref, ref, rsem.at[i]).wait()

    def rows(ref, start, n, align=16):
        return ref.at[pl.ds(pl.multiple_of(start, align), n), :]

    nd = (z, s + 2 - 4 * x + 4 - 8 * y)
    qd = 3 - q

    peers = [part, nx, ny, nd]
    for dz in range(1, 4):
        zz = lax.rem(z + dz, 4)
        peers += [(zz, s), (zz, s + 1 - 2 * c)]
    bar = pltpu.get_barrier_semaphore()
    for dev in peers:
        pl.semaphore_signal(bar, inc=1, device_id=dev, device_id_type=MESH)
    spread = (
        lax.broadcasted_iota(jnp.int32, (rows_dev, width), 1)
        == lax.broadcasted_iota(jnp.int32, (rows_dev, width), 0) + rows_dev * s
    ).astype(F32)
    gains = r["gains"]
    for k, g in enumerate((r["g1"], r["g2"])):
        vec = jnp.broadcast_to(g[...].astype(F32), (8, rows_dev))
        gains[0, :, k * width : (k + 1) * width] = nn(vec, spread, lax.Precision.HIGHEST)[0:1, :]
    pl.semaphore_wait(bar, len(peers))

    seg_i = sems(4)
    x_i = sems(2)
    c_i = sems(2)

    def to_chip(src, dst, i_recv, i_send, zd, core):
        is_self = (zd == z) & (core == c)
        dev = (zd, s - c + core)

        @pl.when(is_self)
        def _():
            pltpu.make_async_copy(src, dst, rsem.at[i_recv]).start()

        @pl.when(jnp.logical_not(is_self))
        def _():
            remote(src, dst, i_recv, dev, i_send).start()

        def end():
            @pl.when(jnp.logical_not(is_self))
            def _():
                remote(src, dst, i_recv, dev, i_send).wait_send()

        ends.append(end)

    for m in range(2):
        to_chip(tok.at[m], rows(r["xb"], quarter * zk, quarter), x_i + zk, x_i + m, 2 * m + c, zh)

    my = pl.multiple_of(rows_dev * s, 32)
    partner_rows = pl.ds(pl.multiple_of(part[1] * rows_dev, 32), rows_dev)
    my_rows = pl.ds(my, rows_dev)
    local_d = sems()
    local_i = {name: sems() for name in ("q", "o", "u0", "u1")}
    flip_i = {name: sems() for name in ("q", "o", "u0", "u1")}
    W = {"q": r["w_q"], "o": r["w_o"], "u": r["w_u"], "d": r["w_d"]}

    def dcol(start, n):
        return pl.ds(pl.multiple_of(start, LANES), n)

    half_u = ffh // 2

    def cols_of(name):
        return {
            "q": slice(None),
            "o": dcol(c * hcols, hcols),
            "u0": pl.ds(0, half_u),
            "u1": pl.ds(half_u, half_u),
            "d0": slice(None),
            "d1": slice(None),
        }[name]

    def pieces(name, core):
        if name == "q":
            cuts = [(wqkv, t * width + core * hcols, t * hcols, hcols) for t in range(3)]
        elif name == "o":
            cuts = [(wout, core * hcols, core * hcols, hcols)]
        else:
            js = (0, 1) if name == "u0" else (2, 3)
            cuts = [(wup, (2 * j + core) * ffb, j * ffb, ffb) for j in js]
        for src, col, at, n in cuts:
            yield src.at[:, dcol(col, n)], W[name[0]].at[my_rows, dcol(at, n)]

    def block(name, first, n):
        return W[name[0]].at[pl.ds(pl.multiple_of(first, 32), n), cols_of(name)]

    ag = {}

    def flip(name):
        for src, dst in pieces(name, 1 - c):
            remote(src, dst, flip_i[name], part).start()

        def end():
            mine = block(name, my, rows_dev)
            remote(mine, mine, flip_i[name], part).wait_send()

        ends.append(end)

    def keep(name):
        for src, dst in pieces(name, c):
            pltpu.make_async_copy(src, dst, rsem.at[local_i[name]]).start()

    def ag_wait_sent(i, n_rows, name):
        both = W[name[0]].at[pl.ds(0, 2 * n_rows), cols_of(name)]
        ends.append(lambda: remote(both, both, i, nx).wait_send())

    def ag_own(name):
        i = sems()
        ag[name] = i
        for dev in (nx, ny):
            for src, dst in pieces(name, c):
                remote(src, dst, i, dev).start()
        ag_wait_sent(i, rows_chip, name)

    def ag_partner(name):
        his = block(name, part[1] * rows_dev, rows_dev)
        wait_in(his, flip_i[name])
        for dev in (nx, ny):
            remote(his, his, ag[name], dev).start()

    half_d = ffb // 2

    def span(name):
        return half_d if name[0] == "d" else rows_chip

    def chip_rows(name, qq, first, n):
        base = ffb * qq + half_d * int(name[1]) if name[0] == "d" else rows_chip * qq
        return block(name, base + first, n)

    def ag_first(name):
        if name[0] == "d":
            i = sems()
            ag[name] = i
            for dev in (nx, ny):
                src = wdn.at[pl.ds(half_d * int(name[1]), half_d), :]
                remote(src, chip_rows(name, q, 0, half_d), i, dev).start()
            ag_wait_sent(i, half_d, name)
        else:
            ag_own(name)
            ag_partner(name)

    def ag_second(name):
        n = span(name) // 2
        wait_in(W[name[0]].at[pl.ds(0, 4 * n), cols_of(name)], ag[name])
        i = sems()
        ag[name] = (i,)
        bx = chip_rows(name, qx, 0, n)
        by = chip_rows(name, qy, n, n)
        remote(bx, bx, i, ny).start()
        remote(by, by, i, nx).start()
        ag_wait_sent(i, n, name)

    def ag_last(name):
        wait_in(chip_rows(name, qd, 0, span(name)), ag[name][0])
        if name[0] != "d":
            wait_in(block(name, my, rows_dev), local_i[name])

    flip("q")
    ag_own("q")
    g_core = send(gains.at[0], gains.at[1], part)
    flip("o")
    ag_partner("q")
    ag_own("o")
    keep("q")
    keep("o")
    flip("u0")
    flip("u1")
    for m in range(2):
        for core in range(2):
            to_chip(seg.at[m], r["segs"].at[z], seg_i + z, seg_i + 2 * m + core, 2 * m + c, core)
    ag_partner("o")
    keep("u0")
    keep("u1")
    pltpu.make_async_copy(wdn, rows(W["d"], ffb * q, ffb), rsem.at[local_d]).start()

    g_core.wait_recv()
    gains[2] = gains[0] + gains[1]
    g_in = [send(gains.at[2], gains.at[3 + i], dev) for i, dev in enumerate((nx, ny, nd))]
    ag_second("q")
    ag_first("u0")
    ag_first("u1")
    for copy in g_in:
        copy.wait_recv()
    g_all = jnp.where(x == 0, gains[2], gains[3]) + jnp.where(x == 0, gains[3], gains[2])
    g_all = g_all + (gains[4] + gains[5])
    gains[6] = g_all
    gain_one = gains[6][:, :width]
    gain_two = gains[6][:, width:]

    segs, segc, mask = r["segs"], r["segc"], r["mask"]
    for b in range(4):
        wait_in(segs.at[b], seg_i + b)
    for b in range(4):
        tile = jnp.broadcast_to(segs[b].astype(F32), (LANES, quarter))
        segc[pl.ds(quarter * b, quarter), :] = jnp.transpose(tile)
    base = []
    at = 0
    for b in range(4):
        k0 = max(0, b - 2)
        base.append((at, k0, (b - k0 + 1) * quarter))
        for kb in range(k0, b + 1):
            col = segc[pl.ds(quarter * kb, quarter), :]
            same = jnp.concatenate([col] * (quarter // LANES), axis=1) == segs[b].astype(F32)
            if kb == b:
                shape = (quarter, quarter)
                same = same & (
                    lax.broadcasted_iota(jnp.int32, shape, 0)
                    <= lax.broadcasted_iota(jnp.int32, shape, 1)
                )
            mask[pl.ds(at, quarter), :] = jnp.where(same, 1.0, 0.0)
            at += quarter

    xb, normed = r["xb"], r["normed"]
    n_copies = []
    for k in range(2):
        wait_in(rows(xb, quarter * k, quarter), x_i + k)
        if k == 1:
            for m in range(2):
                dst = rows(r["cb"], quarter * z, quarter)
                to_chip(cot.at[m], dst, c_i + zk, c_i + m, 2 * m + c, zh)
        cen, rstd = row_stats(xb[pl.ds(quarter * k, quarter), :].astype(F32))
        normed[pl.ds(own0 + quarter * k, quarter), :] = (cen * rstd * gain_one).astype(BF)
        mine = rows(normed, own0 + quarter * k, quarter)
        n_copies.append(send(mine, mine, part))

    ag_last("q")
    qkv = r["qkv"]

    def qkv_rows(first):
        def step(k, _):
            ts = pl.ds(pl.multiple_of(first + quarter * k, quarter), quarter)
            qkv[ts, :] = nn(normed[ts, :], W["q"][...]).astype(BF)
            return 0

        lax.fori_loop(0, 2, step, 0)

    qkv_rows(own0)
    for copy in n_copies:
        copy.wait_recv()
    qkv_rows(oth0)
    ag_second("o")
    ag_second("u0")
    attended, lev = r["attended"], r["lev"]
    lane = lax.broadcasted_iota(jnp.int32, (1, LANES), 1)
    head_lane = [jnp.where(lane < LANES // 2, 1.0, 0.0), jnp.where(lane < LANES // 2, 0.0, 1.0)]
    head_bf = [v.astype(BF) for v in head_lane]
    scale = HEAD_DIM ** (-0.5)

    def attend(p):
        for b in range(4):
            at, k0, n = base[b]
            qs = pl.ds(quarter * b, quarter)
            ks = pl.ds(quarter * k0, n)
            query = qkv[qs, dcol(p * LANES, LANES)] * jnp.asarray(scale, BF)
            key = qkv[ks, dcol(hcols + p * LANES, LANES)]
            value = qkv[ks, dcol(2 * hcols + p * LANES, LANES)]
            allowed = mask[pl.ds(at, n), :]
            total_out = None
            for h in range(2):
                sm = nt(key, query * head_bf[h]) * allowed
                mag = jnp.abs(sm)
                top = jnp.max(mag, axis=0, keepdims=True)
                raw = jnp.exp(mag - top)
                low = jnp.exp(-top)
                total = jnp.sum(raw * allowed, axis=0, keepdims=True)
                sign = jnp.clip(sm * HUGE, -1.0, 1.0)
                signed = (sign * (raw - low) * (1.0 / total)).astype(BF)
                lev[2 * p + h, :, qs] = top + jnp.log(total)
                out = tn(signed, value * head_bf[h])
                total_out = out if total_out is None else total_out + out
            attended[qs, dcol(c * hcols + p * LANES, LANES)] = total_out.astype(BF)
            if p == 1 and b == 1:
                ag_second("u1")
                ag_first("d0")
                ag_first("d1")

    att_i = sems(pairs)

    def att_copy(p):
        cols = attended.at[:, dcol(c * hcols + p * LANES, LANES)]
        return remote(cols, cols, att_i + p, part)

    for p in range(pairs):
        attend(p)
        att_copy(p).start()
        ends.append(att_copy(p).wait_send)
        if p == 0:
            ag_last("o")
            half_o = W["o"].at[:, dcol(c * hcols, hcols)]
            o_copy = send(half_o, half_o, part)
    o_copy.wait_recv()
    for p in range(pairs):
        att_copy(p).wait_recv()

    middle, n2 = r["middle"], r["n2"]
    n2_copies = []
    for k in range(2):
        ts = pl.ds(own0 + quarter * k, quarter)
        ls = pl.ds(quarter * k, quarter)
        mid_v = xb[ls, :].astype(F32) + nn(attended[ts, :], W["o"][...])
        middle[ls, :] = mid_v
        cen, rstd = row_stats(mid_v)
        n2[ts, :] = (cen * rstd * gain_two).astype(BF)
        mine = rows(n2, own0 + quarter * k, quarter)
        n2_copies.append(send(mine, mine, part))

    cb = r["cb"]
    c_copies = []
    for k in range(2):
        mine = rows(cb, own0 + quarter * k, quarter)
        wait_in(mine, c_i + k)
        c_copies.append(send(mine, mine, part))

    active, du = r["active"], r["du"]
    ft = 256
    nft = half_u // ft

    def up_rows(first, col):
        def step(i, _):
            ts = pl.ds(first + quarter * lax.div(i, nft), quarter)
            cols = dcol(col + ft * lax.rem(i, nft), ft)
            u = nn(n2[ts, :], W["u"][:, cols])
            u2 = u * u
            t = jnp.tanh(GELU_K * (u + GELU_C * u * u2))
            active[ts, cols] = (0.5 * u * (1.0 + t)).astype(BF)
            slope = 0.5 * (1.0 + t) + 0.5 * u * (1.0 - t * t) * (
                GELU_K * (1.0 + 3.0 * GELU_C * u2)
            )
            du[ts, cols] = slope.astype(BF)
            return 0

        lax.fori_loop(0, 2 * nft, step, 0)

    ag_last("u0")
    up_rows(own0, 0)
    for copy in n2_copies:
        copy.wait_recv()
    ag_last("u1")
    up_rows(own0, half_u)
    ag_second("d0")
    up_rows(oth0, 0)
    up_rows(oth0, half_u)
    ag_second("d1")

    def reduce_unit(name, ref, stride, off, n, cols, place):
        h2 = n // 2
        r1, r2, r3, r4 = (r[name + k] for k in ("1", "2", "3", "4"))
        fin = r3
        i1, i2, i3, i4 = sems(), sems(), sems(), sems()

        def at_rows(qq, first, count):
            return pl.ds(pl.multiple_of(qq * stride + off + first, 16), count), cols

        def q_of(yy, xx):
            return 2 * yy + xx

        def first():
            for k in range(2):
                remote(ref.at[at_rows(q_of(k, 1 - x), 0, h2)], r1.at[k], i1, nx).start()
                remote(ref.at[at_rows(q_of(1 - y, k), h2, h2)], r1.at[2 + k], i1, ny).start()
            ends.append(lambda: remote(r1, r1, i1, nx).wait_send())

        def second():
            wait_in(r1, i1)
            ra = at_rows(q_of(1 - y, x), 0, h2)
            ref[ra] = (ref[ra].astype(F32) + r1[1 - y].astype(F32)).astype(BF)
            remote(ref.at[ra], r2.at[0], i2, ny).start()
            rb = at_rows(q_of(y, 1 - x), h2, h2)
            ref[rb] = (ref[rb].astype(F32) + r1[3 - x].astype(F32)).astype(BF)
            remote(ref.at[rb], r2.at[1], i2, nx).start()
            ends.append(lambda: remote(r2, r2, i2, nx).wait_send())

        own = at_rows(q, 0, n)

        def third():
            wait_in(r2, i2)
            ra = at_rows(q, 0, h2)
            ref[ra] = (
                ref[ra].astype(F32) + r1[y].astype(F32) + r2[0].astype(F32)
            ).astype(BF)
            rb = at_rows(q, h2, h2)
            ref[rb] = (
                ref[rb].astype(F32) + r1[2 + x].astype(F32) + r2[1].astype(F32)
            ).astype(BF)

            @pl.when(edge)
            def _():
                remote(ref.at[own], r3, i3, zp).start()

        def fourth():
            @pl.when(mid)
            def _():
                wait_in(r3, i3)
                ref[own] = (ref[own].astype(F32) + r3[...].astype(F32)).astype(BF)
                remote(ref.at[own], r4, i4, zm).start()

        def fifth():
            @pl.when(mid)
            def _():
                wait_in(r4, i4)
                fin[...] = (ref[own].astype(F32) + r4[...].astype(F32)).astype(BF)
                remote(fin, fin, i3, zp).start()

        def last():
            @pl.when(edge)
            def _():
                wait_in(fin, i3)

            place(fin)

        def end():
            remote(ref.at[own], r3, i3, zp).wait_send()

            @pl.when(mid)
            def _():
                remote(ref.at[own], r4, i4, zm).wait_send()

        ends.append(end)
        return first, second, third, fourth, fifth, last

    waits = []

    def put(src, dst):
        i = sems()
        copy = pltpu.make_async_copy(src, dst, rsem.at[i])
        copy.start()
        waits.append(copy.wait)

    def by_core(fin, cuts, out):
        i_mine, i_his = sems(), sems()
        mine = pl.ds(pl.multiple_of(c * rows_dev, 32), rows_dev)
        his = pl.ds(pl.multiple_of((1 - c) * rows_dev, 32), rows_dev)
        for src_col, dst_col, n in cuts:
            src, dst = fin.at[his, pl.ds(src_col, n)], out.at[:, dcol(dst_col, n)]
            remote(src, dst, i_his, part).start()
            pltpu.make_async_copy(fin.at[mine, pl.ds(src_col, n)], dst, rsem.at[i_mine]).start()
        whole = fin.at[mine]
        waits.append(lambda: wait_in(whole, i_mine))
        waits.append(lambda: wait_in(whole, i_his))
        ends.append(lambda: remote(whole, whole, i_his, part).wait_send())

    def place_d(i, n):
        return lambda fin: put(fin, r["o_down"].at[pl.ds(n * i, n), :])

    def place_u(j):
        return lambda fin: by_core(fin, [(0, (2 * j + c) * ffb, ffb)], r["o_up"])

    def place_o(fin):
        by_core(fin, [(0, c * hcols, hcols)], r["o_out"])

    def place_q(p):
        cuts = [(t * LANES, t * width + c * hcols + p * LANES, LANES) for t in range(3)]
        return lambda fin: by_core(fin, cuts, r["o_qkv"])

    red = {}
    dn_rows = ffb // 4
    for i in range(4):
        name = "d%d" % i
        red[name] = reduce_unit(
            name, r["g_d"], ffb, dn_rows * i, dn_rows, slice(None), place_d(i, dn_rows)
        )
    for j in range(4):
        name = "u%d" % j
        red[name] = reduce_unit(
            name, r["g_u"], rows_chip, 0, rows_chip, pl.ds(ffb * j, ffb), place_u(j)
        )
    red["o"] = reduce_unit("o", r["g_o"], rows_chip, 0, rows_chip, slice(None), place_o)
    units = list(red)
    units += ["q%d" % p for p in range(pairs)]
    for p in range(pairs):
        name = "q%d" % p
        red[name] = reduce_unit(
            name, r["g_q"].at[p], rows_chip, 0, rows_chip, slice(None), place_q(p)
        )

    turn = iter(SCHEDULE)

    def stages():
        for at in next(turn):
            if at < 6 * len(units):
                red[units[at // 6]][at % 6]()
            else:
                tokens_out(at - 6 * len(units))

    xs, xr, mixacc = r["xs"], r["xr"], r["mixacc"]

    def down(blk, first, into, fresh):
        w_rows = pl.ds(pl.multiple_of(ffb * blk, LANES), ffb)
        for k in range(2):
            ls = pl.ds(quarter * k, quarter)
            out = nn(active[pl.ds(first + quarter * k, quarter), dcol(ffb * blk, ffb)], W["d"][w_rows, :])
            into[ls, :] = out if fresh else into[ls, :] + out

    for copy in c_copies:
        copy.wait_recv()
    gt = 256

    def grad_down_step(i, _):
        cols = dcol(gt * i, gt)
        r["g_d"][pl.ds(pl.multiple_of(gt * i, gt), gt), :] = tn(active[:, cols], cb[...]).astype(BF)
        return 0

    lax.fori_loop(0, ffh // gt, grad_down_step, 0)
    wait_in(rows(W["d"], ffb * q, ffb), local_d)
    stages()

    for i, blk in enumerate((q, qx, qy)):
        down(blk, oth0, xs.at[1], i == 0)
    stages()
    ag_last("d0")
    ag_last("d1")
    down(qd, oth0, xs.at[1], False)
    mix_copies = [
        send(xs.at[1, pl.ds(quarter * k, quarter), :], xr.at[1, pl.ds(quarter * k, quarter), :], part)
        for k in range(2)
    ]
    for k in range(2):
        ls = pl.ds(quarter * k, quarter)
        mixacc[ls, :] = nn(active[pl.ds(own0 + quarter * k, quarter), :], W["d"][...])

    def from_chip(buf, out, i0, k, first, n, last):
        zd = 2 * c + k
        src = buf.at[pl.ds(quarter * k + first, n), :]
        is_self = (zd == z) & (zk == c)
        dev = (zd, s - c + zk)
        dst = out.at[zh, pl.ds(first, n), :]

        @pl.when(is_self)
        def _():
            pltpu.make_async_copy(src, dst, rsem.at[i0 + zh]).start()

        @pl.when(jnp.logical_not(is_self))
        def _():
            remote(src, dst, i0 + zh, dev, i0 + k).start()

        def end():
            @pl.when(jnp.logical_not(is_self))
            def _():
                whole = buf.at[pl.ds(quarter * k, quarter), :]
                remote(whole, out.at[zh], i0 + zh, dev, i0 + k).wait_send()

        if last:
            ends.append(end)
            waits.append(functools.partial(wait_in, out.at[k], i0 + k))

    mo_i, to_i = sems(2), sems(2)
    mixb = r["mixb"]
    for k in range(2):
        ls = pl.ds(quarter * k, quarter)
        mix_copies[k].wait_recv()
        mixb[ls, :] = (middle[ls, :] + mixacc[ls, :] + xr[1, ls, :]).astype(BF)

    def tokens_out(at):
        if at < 2:
            from_chip(mixb, r["o_mixed"], mo_i, at, 0, quarter, True)
        else:
            piece, n = at - 2, quarter // 4
            from_chip(r["gtb"], r["o_gt"], to_i, piece // 4, piece % 4 * n, n, piece % 4 == 3)

    stages()

    fd = 512

    for k in range(4):

        def d_up_step(i, _):
            ts = pl.ds(quarter * k, quarter)
            cols = dcol(fd * i, fd)
            da = nt(cb[ts, :], W["d"][pl.ds(pl.multiple_of(fd * i, LANES), fd), :])
            du[ts, cols] = (da * du[ts, cols].astype(F32)).astype(BF)
            return 0

        lax.fori_loop(0, ffh // fd, d_up_step, 0)
        stages()

    def exchange(n, product_of):
        copies = []
        for k in range(2):
            ls = pl.ds(quarter * k, quarter)
            xs[n % 2, ls, :] = product_of(pl.ds(oth0 + quarter * k, quarter))
            copies.append(send(xs.at[n % 2, ls, :], xr.at[n % 2, ls, :], part))
        return copies

    dn2_copies = exchange(0, lambda ts: nt(du[ts, :], W["u"][...]))
    stages()
    dbr, gsum = r["dbr"], r["gsum"]
    gain_acc = jnp.zeros((1, width), F32)
    db_copies = []
    for k in range(2):
        ts = pl.ds(own0 + quarter * k, quarter)
        ls = pl.ds(quarter * k, quarter)
        dn = nt(du[ts, :], W["u"][...])
        dn2_copies[k].wait_recv()
        dn = dn + xr[0, ls, :]
        cen, rstd = row_stats(middle[ls, :])
        n = cen * rstd
        gain_acc = gain_acc + jnp.sum(dn * n, axis=0, keepdims=True)
        dmid = cb[ts, :].astype(F32) + norm_back(dn, n, rstd, gain_two)
        mixacc[ls, :] = dmid
        dbr[ts, :] = dmid.astype(BF)
        mine = rows(dbr, own0 + quarter * k, quarter)
        db_copies.append(send(mine, mine, part))
        stages()
    gsum[0, :, width:] = gain_acc

    for j in range(2):

        def grad_up_step(i, _):
            cols = dcol(gt * i, gt)
            out = tn(n2[:, cols], du[:, pl.ds(half_u * j, half_u)]).astype(BF)
            r["g_u"][pl.ds(pl.multiple_of(gt * i, gt), gt), pl.ds(half_u * j, half_u)] = out
            return 0

        lax.fori_loop(0, width // gt, grad_up_step, 0)
        stages()

    for copy in db_copies:
        copy.wait_recv()
    datt = r["datt"]

    def datt_step(k, _):
        ts = pl.ds(pl.multiple_of(quarter * k, quarter), quarter)
        w_rows = W["o"][pl.ds(pl.multiple_of(c * hcols, LANES), hcols), :]
        datt[ts, :] = nt(dbr[ts, :], w_rows).astype(BF)
        return 0

    lax.fori_loop(0, 4, datt_step, 0)
    stages()

    dk, dv = r["dk"], r["dv"]
    sel = (
        lax.broadcasted_iota(jnp.int32, (8, LANES), 0)
        == lax.div(lax.broadcasted_iota(jnp.int32, (8, LANES), 1), LANES // 2)
    ).astype(F32)

    def attend_back(p):
        dk[...] = jnp.zeros_like(dk)
        dv[...] = jnp.zeros_like(dv)
        for b in range(4):
            at, k0, n = base[b]
            qs = pl.ds(quarter * b, quarter)
            ks = pl.ds(quarter * k0, n)
            query = qkv[qs, dcol(p * LANES, LANES)] * jnp.asarray(scale, BF)
            key = qkv[ks, dcol(hcols + p * LANES, LANES)]
            value = qkv[ks, dcol(2 * hcols + p * LANES, LANES)]
            d_att = datt[qs, dcol(p * LANES, LANES)]
            att = attended[qs, dcol(c * hcols + p * LANES, LANES)]
            delta = nt(sel, d_att.astype(F32) * att.astype(F32), lax.Precision.HIGHEST)
            allowed = mask[pl.ds(at, n), :]
            d_query = None
            for h in range(2):
                q_h = query * head_bf[h]
                d_h = d_att * head_bf[h]
                sm = nt(key, q_h) * allowed
                mag = jnp.abs(sm)
                level = lev[2 * p + h, :, qs]
                prob = jnp.exp(mag - level)
                low = jnp.exp(-level)
                sign = jnp.clip(sm * HUGE, -1.0, 1.0)
                weight = (sign * (prob - low)).astype(BF)
                d_signed = nt(value, d_h)
                d_score = (prob * allowed * (d_signed - sign * delta[h : h + 1, :])).astype(BF)
                dv[ks, :] += nn(weight, d_h)
                dk[ks, :] += nn(d_score, q_h)
                out = tn(d_score, key * head_bf[h])
                d_query = out if d_query is None else d_query + out
            qkv[qs, dcol(p * LANES, LANES)] = (d_query * scale).astype(BF)
            stages()
        qkv[:, dcol(hcols + p * LANES, LANES)] = dk[...].astype(BF)
        qkv[:, dcol(2 * hcols + p * LANES, LANES)] = dv[...].astype(BF)

    def grad_qkv(p):
        def step(i, _):
            cols = dcol(gt * i, gt)
            d_pair = jnp.concatenate(
                [qkv[:, dcol(t * hcols + p * LANES, LANES)] for t in range(3)], axis=1
            )
            out = tn(normed[:, cols], d_pair).astype(BF)
            r["g_q"][p, pl.ds(pl.multiple_of(gt * i, gt), gt), :] = out
            return 0

        lax.fori_loop(0, width // gt, step, 0)

    def grad_out_step(i, _):
        cols = dcol(gt * i, gt)
        out = tn(attended[:, cols], dbr[:, dcol(c * hcols, hcols)]).astype(BF)
        r["g_o"][pl.ds(pl.multiple_of(gt * i, gt), gt), :] = out
        return 0

    attend_back(0)
    grad_qkv(0)
    stages()
    attend_back(1)
    grad_qkv(1)
    stages()
    lax.fori_loop(0, width // gt, grad_out_step, 0)
    stages()
    attend_back(2)

    for copy in dn2_copies:
        copy.wait_send()
        ends.remove(copy.wait_send)
    dn1_copies = exchange(2, lambda ts: nt(qkv[ts, :], W["q"][...]))
    stages()
    grad_qkv(2)
    stages()
    gtb = r["gtb"]
    gain_acc = jnp.zeros((1, width), F32)
    for k in range(2):
        ts = pl.ds(own0 + quarter * k, quarter)
        ls = pl.ds(quarter * k, quarter)
        dn = nt(qkv[ts, :], W["q"][...])
        dn1_copies[k].wait_recv()
        dn = dn + xr[0, ls, :]
        cen, rstd = row_stats(xb[ls, :].astype(F32))
        n = cen * rstd
        gain_acc = gain_acc + jnp.sum(dn * n, axis=0, keepdims=True)
        gtb[ls, :] = (mixacc[ls, :] + norm_back(dn, n, rstd, gain_one)).astype(BF)
        stages()
    gsum[0, :, :width] = gain_acc

    g3, g4, g5 = sems(), sems(), sems()
    g_copy = send(gsum.at[0], gsum.at[1], part)
    stages()

    g_copy.wait_recv()
    gsum[2] = gsum[0] + gsum[1]
    g_copy = send(gsum.at[2], gsum.at[3], nx)
    stages()
    g_copy.wait_recv()
    gsum[4] = gsum[2] + gsum[3]
    g_copy = send(gsum.at[4], gsum.at[5], ny)
    stages()
    g_copy.wait_recv()
    gsum[6] = gsum[4] + gsum[5]

    @pl.when(edge)
    def _():
        remote(gsum.at[6], gsum.at[7], g3, zp).start()

    stages()

    @pl.when(mid)
    def _():
        remote(gsum.at[6], gsum.at[7], g3, zp).wait_recv()
        gsum[8] = gsum[6] + gsum[7]
        remote(gsum.at[8], gsum.at[9], g4, zm).start()

    stages()

    @pl.when(mid)
    def _():
        remote(gsum.at[8], gsum.at[9], g4, zm).wait_recv()
        gsum[10] = gsum[8] + gsum[9]
        remote(gsum.at[10], gsum.at[10], g5, zp).start()

    stages()

    @pl.when(mid)
    def _():
        remote(gsum.at[8], gsum.at[9], g4, zm).wait_send()
        remote(gsum.at[10], gsum.at[10], g5, zp).wait_send()

    @pl.when(edge)
    def _():
        remote(gsum.at[10], gsum.at[10], g5, zp).wait_recv()
        remote(gsum.at[6], gsum.at[7], g3, zp).wait_send()

    pick = (
        lax.broadcasted_iota(jnp.int32, (width, LANES), 0)
        == lax.broadcasted_iota(jnp.int32, (width, LANES), 1) + rows_dev * s
    ).astype(F32)
    for k in range(2):
        vec = jnp.broadcast_to(gsum[10][:, width * k : width * (k + 1)], (8, width))
        r["o_gains"][k : k + 1, :] = nn(vec, pick, lax.Precision.HIGHEST)[0:1, :rows_dev]
    for wait in waits:
        wait()
    for end in ends:
        end()
    assert used[0] <= N_SEMS, used[0]


def per_device_fast(tokens, segments, w_qkv, w_out, w_up, w_down, gain_one, gain_two, cotangent):
    micro, _, quarter, width = tokens.shape
    rows_dev = w_qkv.shape[0]
    ff = w_up.shape[1]
    ffb = w_down.shape[0]
    half, length = 2 * quarter, 4 * quarter
    hcols, ffh, rows_chip = width // 2, ff // 2, 2 * rows_dev
    pairs = hcols // LANES
    pcols = 3 * LANES
    scratch = {}

    def vm(name, shape, dtype=BF):
        scratch[name] = pltpu.VMEM(shape, dtype)

    vm("w_q", (width, pairs * pcols))
    vm("w_o", (width, width))
    vm("w_u", (width, ffh))
    vm("w_d", (ffh, width))
    vm("segs", (4, 1, quarter), jnp.int32)
    vm("segc", (length, LANES), F32)
    vm("mask", (9 * quarter, quarter), F32)
    vm("xb", (half, width))
    vm("cb", (length, width))
    vm("gains", (7, 1, 2 * width), F32)
    vm("gsum", (11, 1, 2 * width), F32)
    vm("normed", (length, width))
    vm("qkv", (length, pairs * pcols))
    vm("lev", (2 * pairs, 1, length), F32)
    vm("attended", (length, width))
    vm("middle", (half, width), F32)
    vm("n2", (length, width))
    vm("active", (length, ffh))
    vm("du", (length, ffh))
    vm("xs", (2, half, width), F32)
    vm("xr", (2, half, width), F32)
    vm("mixb", (half, width))
    vm("mixacc", (half, width), F32)
    vm("gtb", (half, width))
    vm("dbr", (length, width))
    vm("datt", (length, hcols))
    vm("dk", (length, LANES), F32)
    vm("dv", (length, LANES), F32)
    vm("g_d", (ffh, width))
    vm("g_u", (width, ffh))
    vm("g_o", (width, hcols))
    vm("g_q", (pairs, width, pcols))
    pieces = [("d%d" % i, ffb // 4, width) for i in range(4)]
    pieces += [("u%d" % j, rows_chip, ffb) for j in range(4)]
    pieces += [("o", rows_chip, hcols)]
    pieces += [("q%d" % p, rows_chip, pcols) for p in range(pairs)]
    for name, blk, cols in pieces:
        vm(name + "1", (4, blk // 2, cols))
        vm(name + "2", (2, blk // 2, cols))
        vm(name + "3", (blk, cols))
        vm(name + "4", (blk, cols))
    scratch["ssem"] = pltpu.SemaphoreType.DMA((N_SEMS,))
    scratch["rsem"] = pltpu.SemaphoreType.DMA((N_SEMS,))
    outs = {
        "o_mixed": ((micro, quarter, width), BF),
        "o_gt": ((micro, quarter, width), BF),
        "o_qkv": ((rows_dev, 3 * width), BF),
        "o_out": ((rows_dev, width), BF),
        "o_up": ((rows_dev, ff), BF),
        "o_down": ((ffb, width), BF),
        "o_gains": ((2, rows_dev), F32),
    }
    ins = ["tok", "seg", "wqkv", "wout", "wup", "wdn", "g1", "g2", "cot"]
    names = ins + list(outs) + list(scratch)
    hbm = pl.BlockSpec(memory_space=pl.ANY)
    vmem = pl.BlockSpec(memory_space=pltpu.VMEM)
    tokens_all = 2 * half
    flops = 6 * half * (width * (4 * width + 2 * ff)) + 14 * 9 * 6 * quarter * quarter * 128
    got = pl.pallas_call(
        functools.partial(layer_kernel, names),
        out_shape=[jax.ShapeDtypeStruct(*v) for v in outs.values()],
        in_specs=[vmem if k in ("g1", "g2") else hbm for k in ins],
        out_specs=[vmem if k == "o_gains" else hbm for k in outs],
        scratch_shapes=list(scratch.values()),
        compiler_params=pltpu.CompilerParams(
            collective_id=0, has_side_effects=True, vmem_limit_bytes=VMEM_LIMIT
        ),
        cost_estimate=pl.CostEstimate(
            flops=flops, bytes_accessed=20 * tokens_all * width, transcendentals=0
        ),
    )(
        tokens[:, 0],
        segments.reshape(micro, 1, quarter),
        w_qkv,
        w_out,
        w_up,
        w_down,
        gain_one[None],
        gain_two[None],
        cotangent[:, 0],
    )
    mixed, grad_tokens, g_qkv, g_out, g_up, g_down, g_gains = got
    return (
        mixed[:, None],
        grad_tokens.astype(F32)[:, None],
        g_qkv.astype(F32),
        g_out.astype(F32),
        g_up.astype(F32),
        g_down.astype(F32),
        g_gains[0],
        g_gains[1],
    )


VMEM_LIMIT = 62 * 1024 * 1024


def solution(mesh):
    placed = (
        P(None, "shard", "seq", None),
        P(None, "shard", "seq"),
        P("shard", None),
        P("shard", None),
        P("shard", None),
        P("shard", None),
        P("shard"),
        P("shard"),
        P(None, "shard", "seq", None),
    )
    chip_sized = mesh.shape["seq"] == 4 and mesh.shape["shard"] == 8
    return jax.shard_map(
        per_device_fast if chip_sized else per_device,
        mesh=mesh,
        in_specs=placed,
        out_specs=(
            P(None, "shard", "seq", None),
            P(None, "shard", "seq", None),
            P("shard", None),
            P("shard", None),
            P("shard", None),
            P("shard", None),
            P("shard"),
            P("shard"),
        ),
        check_vma=False,
    )
```

```python
import functools
import math

import jax
import jax.numpy as jnp
from jax import lax
from jax.experimental import pallas as pl
from jax.experimental.pallas import tpu as pltpu
from jax.sharding import PartitionSpec as P


HEADS = 12
HEAD_DIM = 64


epsilon = 1e-05
far_below = -1e30


def norm_rows(values, gain):
    row_mean = jnp.mean(values, axis=-1, keepdims=True)
    centred = values - row_mean
    spread = jnp.mean(centred * centred, axis=-1, keepdims=True)
    return centred * lax.rsqrt(spread + epsilon) * gain


def gelu_tanh(values):
    return jax.nn.gelu(values, approximate=True)


def product(left, right):
    return jnp.dot(left, right, preferred_element_type=jnp.float32)


def product_left_t(left, right):
    return lax.dot_general(
        left, right, (((0,), (0,)), ((), ())), preferred_element_type=jnp.float32
    )


def product_right_t(left, right):
    return lax.dot_general(
        left, right, (((1,), (1,)), ((), ())), preferred_element_type=jnp.float32
    )


def block_scores(query_block, keys, seg_rows, seg_cols, row_first, score_scale):
    rows_count = query_block.shape[0]
    cols_count = keys.shape[0]
    scores = (
        jnp.einsum("qhd,khd->hqk", query_block, keys, preferred_element_type=jnp.float32)
        * score_scale
    )
    row_pos = row_first + lax.broadcasted_iota(jnp.int32, (rows_count, cols_count), 0)
    col_pos = lax.broadcasted_iota(jnp.int32, (rows_count, cols_count), 1)
    allowed = (col_pos <= row_pos) & (seg_rows[:, None] == seg_cols[None, :])
    return (scores, allowed[None])


def attend_forward(queries, keys, values, seg_all, rows_block, score_scale):
    length = queries.shape[0]
    out_parts = []
    level_parts = []
    for row_first in range(0, length, rows_block):
        query_block = queries[row_first : row_first + rows_block]
        scores, allowed = block_scores(
            query_block,
            keys,
            seg_all[row_first : row_first + rows_block],
            seg_all,
            row_first,
            score_scale,
        )
        magnitude = jnp.abs(scores)
        row_top = jnp.max(jnp.where(allowed, magnitude, far_below), axis=-1, keepdims=True)
        exp_raw = jnp.where(allowed, jnp.exp(magnitude - row_top), 0.0)
        total = jnp.sum(exp_raw, axis=-1, keepdims=True)
        floor_term = jnp.where(allowed, jnp.exp(-row_top), 0.0)
        signed = (jnp.sign(scores) * (exp_raw - floor_term) / total).astype(jnp.bfloat16)
        out_parts.append(
            jnp.einsum("hqk,khd->qhd", signed, values, preferred_element_type=jnp.float32)
        )
        level_parts.append(row_top + jnp.log(total))
    return (jnp.concatenate(out_parts, axis=0), jnp.concatenate(level_parts, axis=1))


def attend_backward(queries, keys, values, seg_all, levels, d_heads, rows_block, score_scale):
    length = queries.shape[0]
    grad_keys = jnp.zeros(keys.shape, jnp.float32)
    grad_values = jnp.zeros(values.shape, jnp.float32)
    query_parts = []
    for row_first in range(0, length, rows_block):
        query_block = queries[row_first : row_first + rows_block]
        d_block = d_heads[row_first : row_first + rows_block]
        scores, allowed = block_scores(
            query_block,
            keys,
            seg_all[row_first : row_first + rows_block],
            seg_all,
            row_first,
            score_scale,
        )
        level_block = levels[:, row_first : row_first + rows_block]
        sign_part = jnp.sign(scores)
        prob = jnp.where(allowed, jnp.exp(jnp.abs(scores) - level_block), 0.0)
        weight = sign_part * jnp.where(allowed, prob - jnp.exp(-level_block), 0.0)
        d_signed = jnp.einsum("qhd,khd->hqk", d_block, values, preferred_element_type=jnp.float32)
        delta = jnp.sum(weight * d_signed, axis=-1, keepdims=True)
        d_score = (prob * (d_signed - sign_part * delta)).astype(jnp.bfloat16)
        query_parts.append(
            jnp.einsum("hqk,khd->qhd", d_score, keys, preferred_element_type=jnp.float32)
            * score_scale
        )
        grad_keys = (
            grad_keys
            + jnp.einsum("hqk,qhd->khd", d_score, query_block, preferred_element_type=jnp.float32)
            * score_scale
        )
        grad_values = grad_values + jnp.einsum(
            "hqk,qhd->khd", weight.astype(jnp.bfloat16), d_block, preferred_element_type=jnp.float32
        )
    grad_queries = jnp.concatenate(query_parts, axis=0)
    stacked = jnp.stack([grad_queries, grad_keys, grad_values], axis=1)
    heads_dev = queries.shape[1]
    return stacked.astype(jnp.bfloat16).reshape(length, 3, 1, heads_dev * queries.shape[2])


def per_device(tokens, segments, w_qkv, w_out, w_up, w_down, gain_one, gain_two, cotangent):
    micro_count = tokens.shape[0]
    tok_rows = tokens.shape[2]
    width = tokens.shape[3]
    groups = lax.axis_size("seq")
    heads_dev = HEADS // groups
    head_cols = heads_dev * HEAD_DIM
    length = tok_rows * groups
    rows_block = min(512, length)
    score_scale = HEAD_DIM ** (-0.5)
    totals = None
    shares = None
    results = []
    grad_rows = []
    for micro_idx in range(micro_count):
        whole = (
            lax.all_gather(w_qkv, "shard", axis=0, tiled=True),
            lax.all_gather(w_out, "shard", axis=0, tiled=True),
            lax.all_gather(w_up, "shard", axis=0, tiled=True),
            lax.all_gather(w_down, "shard", axis=0, tiled=True),
            lax.all_gather(gain_one, "shard", axis=0, tiled=True),
            lax.all_gather(gain_two, "shard", axis=0, tiled=True),
        )
        full_qkv, full_out, full_up, full_down = (whole[0], whole[1], whole[2], whole[3])
        gain_first = whole[4].astype(jnp.float32)
        gain_second = whole[5].astype(jnp.float32)
        tokens_f = tokens[micro_idx, 0].astype(jnp.float32)
        seg_local = segments[micro_idx, 0].astype(jnp.bfloat16)
        normed = norm_rows(tokens_f, gain_first).astype(jnp.bfloat16)
        packed = (
            product(normed, full_qkv).astype(jnp.bfloat16).reshape(tok_rows, 3, groups, head_cols)
        )
        seg_tile = jnp.broadcast_to(seg_local[:, None, None, None], (tok_rows, 1, groups, 1))
        received, seg_recv = (
            lax.all_to_all(packed, "seq", split_axis=2, concat_axis=0, tiled=True),
            lax.all_to_all(seg_tile, "seq", split_axis=2, concat_axis=0, tiled=True),
        )
        queries = received[:, 0, 0].reshape(length, heads_dev, HEAD_DIM)
        keys = received[:, 1, 0].reshape(length, heads_dev, HEAD_DIM)
        values = received[:, 2, 0].reshape(length, heads_dev, HEAD_DIM)
        seg_all = seg_recv[:, 0, 0, 0]
        heads_out, levels = attend_forward(queries, keys, values, seg_all, rows_block, score_scale)
        heads_low = heads_out.astype(jnp.bfloat16).reshape(length, 1, head_cols)
        attended = lax.all_to_all(
            heads_low, "seq", split_axis=0, concat_axis=1, tiled=True
        ).reshape(tok_rows, width)
        middle = tokens_f + product(attended, full_out)
        normed_two = norm_rows(middle, gain_second).astype(jnp.bfloat16)
        up_pre = product(normed_two, full_up)
        active = gelu_tanh(up_pre).astype(jnp.bfloat16)
        results.append((middle + product(active, full_down)).astype(jnp.bfloat16))
        again = (
            lax.all_gather(w_qkv, "shard", axis=0, tiled=True),
            lax.all_gather(w_out, "shard", axis=0, tiled=True),
            lax.all_gather(w_up, "shard", axis=0, tiled=True),
            lax.all_gather(w_down, "shard", axis=0, tiled=True),
            lax.all_gather(gain_one, "shard", axis=0, tiled=True),
            lax.all_gather(gain_two, "shard", axis=0, tiled=True),
        )
        back_qkv, back_out, back_up, back_down = (again[0], again[1], again[2], again[3])
        cot_low = cotangent[micro_idx, 0]
        grad_down_term = product_left_t(active, cot_low)
        d_active = product_right_t(cot_low, back_down)
        unused_gelu, gelu_pull = jax.vjp(gelu_tanh, up_pre)
        d_up = gelu_pull(d_active)[0].astype(jnp.bfloat16)
        grad_up_term = product_left_t(normed_two, d_up)
        d_norm_two = product_right_t(d_up, back_up)
        unused_second, second_pull = jax.vjp(norm_rows, middle, gain_second)
        d_middle_norm, grad_gain_two_term = second_pull(d_norm_two)
        d_middle = cot_low.astype(jnp.float32) + d_middle_norm
        d_branch = d_middle.astype(jnp.bfloat16)
        grad_out_term = product_left_t(attended, d_branch)
        d_attended = (
            product_right_t(d_branch, back_out)
            .astype(jnp.bfloat16)
            .reshape(tok_rows, groups, head_cols)
        )
        d_heads = lax.all_to_all(d_attended, "seq", split_axis=1, concat_axis=0, tiled=True)
        d_heads = d_heads[:, 0].reshape(length, heads_dev, HEAD_DIM)
        grad_heads = attend_backward(
            queries, keys, values, seg_all, levels, d_heads, rows_block, score_scale
        )
        d_packed = lax.all_to_all(
            grad_heads, "seq", split_axis=0, concat_axis=2, tiled=True
        ).reshape(tok_rows, 3 * width)
        grad_qkv_term = product_left_t(normed, d_packed)
        d_normed = product_right_t(d_packed, back_qkv)
        unused_first, first_pull = jax.vjp(norm_rows, tokens_f, gain_first)
        d_tokens_norm, grad_gain_one_term = first_pull(d_normed)
        grad_rows.append(d_middle + d_tokens_norm)
        terms = (
            grad_qkv_term,
            grad_out_term,
            grad_up_term,
            grad_down_term,
            grad_gain_one_term,
            grad_gain_two_term,
        )
        if totals is None:
            totals = terms
        else:
            totals = tuple((left_term + right_term for left_term, right_term in zip(totals, terms)))
    shares = (
        lax.psum_scatter(totals[0], "shard", scatter_dimension=0, tiled=True),
        lax.psum_scatter(totals[1], "shard", scatter_dimension=0, tiled=True),
        lax.psum_scatter(totals[2], "shard", scatter_dimension=0, tiled=True),
        lax.psum_scatter(totals[3], "shard", scatter_dimension=0, tiled=True),
        lax.psum_scatter(totals[4], "shard", scatter_dimension=0, tiled=True),
        lax.psum_scatter(totals[5], "shard", scatter_dimension=0, tiled=True),
    )
    replicas = lax.psum((shares[0], shares[1], shares[2], shares[3], shares[4], shares[5]), "seq")
    mixed = jnp.stack(results, axis=0)[:, None]
    grad_tokens = jnp.stack(grad_rows, axis=0)[:, None]
    return (
        mixed,
        grad_tokens,
        replicas[0],
        replicas[1],
        replicas[2],
        replicas[3],
        replicas[4],
        replicas[5],
    )


BF = jnp.bfloat16
F32 = jnp.float32
MESH = pl.DeviceIdType.MESH
N_SEMS = 132
SCHEDULE = (
    (0,),
    (6,),
    (12, 72, 73,),
    (1,),
    (18,),
    (7,),
    (),
    (13,),
    (2,),
    (19,),
    (8, 24, 30,),
    (14,),
    (20, 36,),
    (3,),
    (25,),
    (),
    (9, 42, 31,),
    (),
    (15, 37, 4,),
    (),
    (26, 48,),
    (21, 10,),
    (43, 16, 5,),
    (32, 54,),
    (27, 38,),
    (22, 11,),
    (60,),
    (44, 33, 49, 17,),
    (28,),
    (39, 55, 66, 23,),
    (61, 45, 34,),
    (50, 29,),
    (56, 40, 74, 75,),
    (35, 67, 46, 76, 62,),
    (51, 41, 68, 57, 47,),
    (52, 77, 78, 63, 58,),
    (53, 69, 64, 79, 59,),
    (80, 70, 81, 65, 71,),
)

HUGE = 3.0e38
GELU_K = math.sqrt(2.0 / math.pi)
GELU_C = 0.044715
LANES = 128


def nt(left, right, precision=None):
    return lax.dot_general(
        left, right, (((1,), (1,)), ((), ())), preferred_element_type=F32, precision=precision
    )


def tn(left, right):
    return lax.dot_general(left, right, (((0,), (0,)), ((), ())), preferred_element_type=F32)


def nn(left, right, precision=None):
    return jnp.dot(left, right, preferred_element_type=F32, precision=precision)


def row_stats(v):
    mean = jnp.mean(v, axis=-1, keepdims=True)
    cen = v - mean
    var = jnp.mean(cen * cen, axis=-1, keepdims=True)
    return cen, lax.rsqrt(var + epsilon)


def norm_back(dn, n, rstd, gain):
    e = dn * gain
    return (e - jnp.mean(e, axis=-1, keepdims=True) - n * jnp.mean(e * n, axis=-1, keepdims=True)) * rstd


def layer_kernel(names, *refs):
    r = dict(zip(names, refs))
    tok, seg, wqkv, wout, wup, wdn, cot = (
        r[k] for k in ("tok", "seg", "wqkv", "wout", "wup", "wdn", "cot")
    )
    ssem, rsem = r["ssem"], r["rsem"]
    width = tok.shape[2]
    quarter = tok.shape[1]
    half = 2 * quarter
    length = 4 * quarter
    rows_dev = wqkv.shape[0]
    rows_chip = 2 * rows_dev
    hcols = width // 2
    pairs = hcols // LANES
    pcols = 3 * LANES
    ffh = wup.shape[1] // 2
    ffb = wdn.shape[0]

    z = lax.axis_index("seq")
    s = lax.axis_index("shard")
    c = lax.rem(s, 2)
    q = lax.div(s, 2)
    x = lax.rem(q, 2)
    y = lax.div(q, 2)
    part = (z, s + 1 - 2 * c)
    nx = (z, s + 2 - 4 * x)
    ny = (z, s + 4 - 8 * y)
    zp = (z + 1 - 2 * lax.rem(z, 2), s)
    zm = (3 - z, s)
    edge = lax.rem(z, 3) == 0
    mid = lax.rem(z, 3) != 0
    qx = q + 1 - 2 * x
    qy = q + 2 - 4 * y
    zh = lax.div(z, 2)
    zk = lax.rem(z, 2)
    own0 = pl.multiple_of(half * c, half)
    oth0 = pl.multiple_of(half * (1 - c), half)

    used = [0]
    ends = []

    def sems(n=1):
        first = used[0]
        used[0] += n
        return first

    def remote(src, dst, i, dev, j=None):
        return pltpu.make_async_remote_copy(
            src_ref=src,
            dst_ref=dst,
            send_sem=ssem.at[i if j is None else j],
            recv_sem=rsem.at[i],
            device_id=dev,
            device_id_type=MESH,
        )

    def send(src, dst, dev):
        copy = remote(src, dst, sems(), dev)
        copy.start()
        ends.append(copy.wait_send)
        return copy

    def wait_in(ref, i):
        pltpu.make_async_copy(ref, ref, rsem.at[i]).wait()

    def rows(ref, start, n, align=16):
        return ref.at[pl.ds(pl.multiple_of(start, align), n), :]

    nd = (z, s + 2 - 4 * x + 4 - 8 * y)
    qd = 3 - q

    peers = [part, nx, ny, nd]
    for dz in range(1, 4):
        zz = lax.rem(z + dz, 4)
        peers += [(zz, s), (zz, s + 1 - 2 * c)]
    bar = pltpu.get_barrier_semaphore()
    for dev in peers:
        pl.semaphore_signal(bar, inc=1, device_id=dev, device_id_type=MESH)
    spread = (
        lax.broadcasted_iota(jnp.int32, (rows_dev, width), 1)
        == lax.broadcasted_iota(jnp.int32, (rows_dev, width), 0) + rows_dev * s
    ).astype(F32)
    gains = r["gains"]
    for k, g in enumerate((r["g1"], r["g2"])):
        vec = jnp.broadcast_to(g[...].astype(F32), (8, rows_dev))
        gains[0, :, k * width : (k + 1) * width] = nn(vec, spread, lax.Precision.HIGHEST)[0:1, :]
    pl.semaphore_wait(bar, len(peers))

    seg_i = sems(4)
    x_i = sems(2)
    c_i = sems(2)

    def to_chip(src, dst, i_recv, i_send, zd, core):
        is_self = (zd == z) & (core == c)
        dev = (zd, s - c + core)

        @pl.when(is_self)
        def _():
            pltpu.make_async_copy(src, dst, rsem.at[i_recv]).start()

        @pl.when(jnp.logical_not(is_self))
        def _():
            remote(src, dst, i_recv, dev, i_send).start()

        def end():
            @pl.when(jnp.logical_not(is_self))
            def _():
                remote(src, dst, i_recv, dev, i_send).wait_send()

        ends.append(end)

    for m in range(2):
        to_chip(tok.at[m], rows(r["xb"], quarter * zk, quarter), x_i + zk, x_i + m, 2 * m + c, zh)

    my = pl.multiple_of(rows_dev * s, 32)
    partner_rows = pl.ds(pl.multiple_of(part[1] * rows_dev, 32), rows_dev)
    my_rows = pl.ds(my, rows_dev)
    local_d = sems()
    local_i = {name: sems() for name in ("q", "o", "u0", "u1")}
    flip_i = {name: sems() for name in ("q", "o", "u0", "u1")}
    W = {"q": r["w_q"], "o": r["w_o"], "u": r["w_u"], "d": r["w_d"]}

    def dcol(start, n):
        return pl.ds(pl.multiple_of(start, LANES), n)

    half_u = ffh // 2

    def cols_of(name):
        return {
            "q": slice(None),
            "o": dcol(c * hcols, hcols),
            "u0": pl.ds(0, half_u),
            "u1": pl.ds(half_u, half_u),
            "d0": slice(None),
            "d1": slice(None),
        }[name]

    def pieces(name, core):
        if name == "q":
            cuts = [(wqkv, t * width + core * hcols, t * hcols, hcols) for t in range(3)]
        elif name == "o":
            cuts = [(wout, core * hcols, core * hcols, hcols)]
        else:
            js = (0, 1) if name == "u0" else (2, 3)
            cuts = [(wup, (2 * j + core) * ffb, j * ffb, ffb) for j in js]
        for src, col, at, n in cuts:
            yield src.at[:, dcol(col, n)], W[name[0]].at[my_rows, dcol(at, n)]

    def block(name, first, n):
        return W[name[0]].at[pl.ds(pl.multiple_of(first, 32), n), cols_of(name)]

    ag = {}

    def flip(name):
        for src, dst in pieces(name, 1 - c):
            remote(src, dst, flip_i[name], part).start()

        def end():
            mine = block(name, my, rows_dev)
            remote(mine, mine, flip_i[name], part).wait_send()

        ends.append(end)

    def keep(name):
        for src, dst in pieces(name, c):
            pltpu.make_async_copy(src, dst, rsem.at[local_i[name]]).start()

    def ag_wait_sent(i, n_rows, name):
        both = W[name[0]].at[pl.ds(0, 2 * n_rows), cols_of(name)]
        ends.append(lambda: remote(both, both, i, nx).wait_send())

    def ag_own(name):
        i = sems()
        ag[name] = i
        for dev in (nx, ny):
            for src, dst in pieces(name, c):
                remote(src, dst, i, dev).start()
        ag_wait_sent(i, rows_chip, name)

    def ag_partner(name):
        his = block(name, part[1] * rows_dev, rows_dev)
        wait_in(his, flip_i[name])
        for dev in (nx, ny):
            remote(his, his, ag[name], dev).start()

    half_d = ffb // 2

    def span(name):
        return half_d if name[0] == "d" else rows_chip

    def chip_rows(name, qq, first, n):
        base = ffb * qq + half_d * int(name[1]) if name[0] == "d" else rows_chip * qq
        return block(name, base + first, n)

    def ag_first(name):
        if name[0] == "d":
            i = sems()
            ag[name] = i
            for dev in (nx, ny):
                src = wdn.at[pl.ds(half_d * int(name[1]), half_d), :]
                remote(src, chip_rows(name, q, 0, half_d), i, dev).start()
            ag_wait_sent(i, half_d, name)
        else:
            ag_own(name)
            ag_partner(name)

    def ag_second(name):
        n = span(name) // 2
        wait_in(W[name[0]].at[pl.ds(0, 4 * n), cols_of(name)], ag[name])
        i = sems()
        ag[name] = (i,)
        bx = chip_rows(name, qx, 0, n)
        by = chip_rows(name, qy, n, n)
        remote(bx, bx, i, ny).start()
        remote(by, by, i, nx).start()
        ag_wait_sent(i, n, name)

    def ag_last(name):
        wait_in(chip_rows(name, qd, 0, span(name)), ag[name][0])
        if name[0] != "d":
            wait_in(block(name, my, rows_dev), local_i[name])

    flip("q")
    ag_own("q")
    g_core = send(gains.at[0], gains.at[1], part)
    flip("o")
    ag_partner("q")
    ag_own("o")
    keep("q")
    keep("o")
    flip("u0")
    flip("u1")
    for m in range(2):
        for core in range(2):
            to_chip(seg.at[m], r["segs"].at[z], seg_i + z, seg_i + 2 * m + core, 2 * m + c, core)
    ag_partner("o")
    keep("u0")
    keep("u1")
    pltpu.make_async_copy(wdn, rows(W["d"], ffb * q, ffb), rsem.at[local_d]).start()

    g_core.wait_recv()
    gains[2] = gains[0] + gains[1]
    g_in = [send(gains.at[2], gains.at[3 + i], dev) for i, dev in enumerate((nx, ny, nd))]
    ag_second("q")
    ag_first("u0")
    ag_first("u1")
    for copy in g_in:
        copy.wait_recv()
    g_all = jnp.where(x == 0, gains[2], gains[3]) + jnp.where(x == 0, gains[3], gains[2])
    g_all = g_all + (gains[4] + gains[5])
    gains[6] = g_all
    gain_one = gains[6][:, :width]
    gain_two = gains[6][:, width:]

    segs, segc, mask = r["segs"], r["segc"], r["mask"]
    for b in range(4):
        wait_in(segs.at[b], seg_i + b)
    for b in range(4):
        tile = jnp.broadcast_to(segs[b].astype(F32), (LANES, quarter))
        segc[pl.ds(quarter * b, quarter), :] = jnp.transpose(tile)
    base = []
    at = 0
    for b in range(4):
        k0 = max(0, b - 2)
        base.append((at, k0, (b - k0 + 1) * quarter))
        for kb in range(k0, b + 1):
            col = segc[pl.ds(quarter * kb, quarter), :]
            same = jnp.concatenate([col] * (quarter // LANES), axis=1) == segs[b].astype(F32)
            if kb == b:
                shape = (quarter, quarter)
                same = same & (
                    lax.broadcasted_iota(jnp.int32, shape, 0)
                    <= lax.broadcasted_iota(jnp.int32, shape, 1)
                )
            mask[pl.ds(at, quarter), :] = jnp.where(same, 1.0, 0.0)
            at += quarter

    xb, normed = r["xb"], r["normed"]
    n_copies = []
    for k in range(2):
        wait_in(rows(xb, quarter * k, quarter), x_i + k)
        if k == 1:
            for m in range(2):
                dst = rows(r["cb"], quarter * z, quarter)
                to_chip(cot.at[m], dst, c_i + zk, c_i + m, 2 * m + c, zh)
        cen, rstd = row_stats(xb[pl.ds(quarter * k, quarter), :].astype(F32))
        normed[pl.ds(own0 + quarter * k, quarter), :] = (cen * rstd * gain_one).astype(BF)
        mine = rows(normed, own0 + quarter * k, quarter)
        n_copies.append(send(mine, mine, part))

    ag_last("q")
    qkv = r["qkv"]

    def qkv_rows(first):
        def step(k, _):
            ts = pl.ds(pl.multiple_of(first + quarter * k, quarter), quarter)
            qkv[ts, :] = nn(normed[ts, :], W["q"][...]).astype(BF)
            return 0

        lax.fori_loop(0, 2, step, 0)

    qkv_rows(own0)
    for copy in n_copies:
        copy.wait_recv()
    qkv_rows(oth0)
    ag_second("o")
    ag_second("u0")
    attended, lev = r["attended"], r["lev"]
    lane = lax.broadcasted_iota(jnp.int32, (1, LANES), 1)
    head_lane = [jnp.where(lane < LANES // 2, 1.0, 0.0), jnp.where(lane < LANES // 2, 0.0, 1.0)]
    head_bf = [v.astype(BF) for v in head_lane]
    scale = HEAD_DIM ** (-0.5)

    def attend(p):
        for b in range(4):
            at, k0, n = base[b]
            qs = pl.ds(quarter * b, quarter)
            ks = pl.ds(quarter * k0, n)
            query = qkv[qs, dcol(p * LANES, LANES)] * jnp.asarray(scale, BF)
            key = qkv[ks, dcol(hcols + p * LANES, LANES)]
            value = qkv[ks, dcol(2 * hcols + p * LANES, LANES)]
            allowed = mask[pl.ds(at, n), :]
            total_out = None
            for h in range(2):
                sm = nt(key, query * head_bf[h]) * allowed
                mag = jnp.abs(sm)
                top = jnp.max(mag, axis=0, keepdims=True)
                raw = jnp.exp(mag - top)
                low = jnp.exp(-top)
                total = jnp.sum(raw * allowed, axis=0, keepdims=True)
                sign = jnp.clip(sm * HUGE, -1.0, 1.0)
                signed = (sign * (raw - low) * (1.0 / total)).astype(BF)
                lev[2 * p + h, :, qs] = top + jnp.log(total)
                out = tn(signed, value * head_bf[h])
                total_out = out if total_out is None else total_out + out
            attended[qs, dcol(c * hcols + p * LANES, LANES)] = total_out.astype(BF)
            if p == 1 and b == 1:
                ag_second("u1")
                ag_first("d0")
                ag_first("d1")

    att_i = sems(pairs)

    def att_copy(p):
        cols = attended.at[:, dcol(c * hcols + p * LANES, LANES)]
        return remote(cols, cols, att_i + p, part)

    for p in range(pairs):
        attend(p)
        att_copy(p).start()
        ends.append(att_copy(p).wait_send)
        if p == 0:
            ag_last("o")
            half_o = W["o"].at[:, dcol(c * hcols, hcols)]
            o_copy = send(half_o, half_o, part)
    o_copy.wait_recv()
    for p in range(pairs):
        att_copy(p).wait_recv()

    middle, n2 = r["middle"], r["n2"]
    n2_copies = []
    for k in range(2):
        ts = pl.ds(own0 + quarter * k, quarter)
        ls = pl.ds(quarter * k, quarter)
        mid_v = xb[ls, :].astype(F32) + nn(attended[ts, :], W["o"][...])
        middle[ls, :] = mid_v
        cen, rstd = row_stats(mid_v)
        n2[ts, :] = (cen * rstd * gain_two).astype(BF)
        mine = rows(n2, own0 + quarter * k, quarter)
        n2_copies.append(send(mine, mine, part))

    cb = r["cb"]
    c_copies = []
    for k in range(2):
        mine = rows(cb, own0 + quarter * k, quarter)
        wait_in(mine, c_i + k)
        c_copies.append(send(mine, mine, part))

    active, du = r["active"], r["du"]
    ft = 256
    nft = half_u // ft

    def up_rows(first, col):
        def step(i, _):
            ts = pl.ds(first + quarter * lax.div(i, nft), quarter)
            cols = dcol(col + ft * lax.rem(i, nft), ft)
            u = nn(n2[ts, :], W["u"][:, cols])
            u2 = u * u
            t = jnp.tanh(GELU_K * (u + GELU_C * u * u2))
            active[ts, cols] = (0.5 * u * (1.0 + t)).astype(BF)
            slope = 0.5 * (1.0 + t) + 0.5 * u * (1.0 - t * t) * (
                GELU_K * (1.0 + 3.0 * GELU_C * u2)
            )
            du[ts, cols] = slope.astype(BF)
            return 0

        lax.fori_loop(0, 2 * nft, step, 0)

    ag_last("u0")
    up_rows(own0, 0)
    for copy in n2_copies:
        copy.wait_recv()
    ag_last("u1")
    up_rows(own0, half_u)
    ag_second("d0")
    up_rows(oth0, 0)
    up_rows(oth0, half_u)
    ag_second("d1")

    def reduce_unit(name, ref, stride, off, n, cols, place):
        h2 = n // 2
        r1, r2, r3, r4 = (r[name + k] for k in ("1", "2", "3", "4"))
        fin = r3
        i1, i2, i3, i4 = sems(), sems(), sems(), sems()

        def at_rows(qq, first, count):
            return pl.ds(pl.multiple_of(qq * stride + off + first, 16), count), cols

        def q_of(yy, xx):
            return 2 * yy + xx

        def first():
            for k in range(2):
                remote(ref.at[at_rows(q_of(k, 1 - x), 0, h2)], r1.at[k], i1, nx).start()
                remote(ref.at[at_rows(q_of(1 - y, k), h2, h2)], r1.at[2 + k], i1, ny).start()
            ends.append(lambda: remote(r1, r1, i1, nx).wait_send())

        def second():
            wait_in(r1, i1)
            ra = at_rows(q_of(1 - y, x), 0, h2)
            ref[ra] = (ref[ra].astype(F32) + r1[1 - y].astype(F32)).astype(BF)
            remote(ref.at[ra], r2.at[0], i2, ny).start()
            rb = at_rows(q_of(y, 1 - x), h2, h2)
            ref[rb] = (ref[rb].astype(F32) + r1[3 - x].astype(F32)).astype(BF)
            remote(ref.at[rb], r2.at[1], i2, nx).start()
            ends.append(lambda: remote(r2, r2, i2, nx).wait_send())

        own = at_rows(q, 0, n)

        def third():
            wait_in(r2, i2)
            ra = at_rows(q, 0, h2)
            ref[ra] = (
                ref[ra].astype(F32) + r1[y].astype(F32) + r2[0].astype(F32)
            ).astype(BF)
            rb = at_rows(q, h2, h2)
            ref[rb] = (
                ref[rb].astype(F32) + r1[2 + x].astype(F32) + r2[1].astype(F32)
            ).astype(BF)

            @pl.when(edge)
            def _():
                remote(ref.at[own], r3, i3, zp).start()

        def fourth():
            @pl.when(mid)
            def _():
                wait_in(r3, i3)
                ref[own] = (ref[own].astype(F32) + r3[...].astype(F32)).astype(BF)
                remote(ref.at[own], r4, i4, zm).start()

        def fifth():
            @pl.when(mid)
            def _():
                wait_in(r4, i4)
                fin[...] = (ref[own].astype(F32) + r4[...].astype(F32)).astype(BF)
                remote(fin, fin, i3, zp).start()

        def last():
            @pl.when(edge)
            def _():
                wait_in(fin, i3)

            place(fin)

        def end():
            remote(ref.at[own], r3, i3, zp).wait_send()

            @pl.when(mid)
            def _():
                remote(ref.at[own], r4, i4, zm).wait_send()

        ends.append(end)
        return first, second, third, fourth, fifth, last

    waits = []

    def put(src, dst):
        i = sems()
        copy = pltpu.make_async_copy(src, dst, rsem.at[i])
        copy.start()
        waits.append(copy.wait)

    def by_core(fin, cuts, out):
        i_mine, i_his = sems(), sems()
        mine = pl.ds(pl.multiple_of(c * rows_dev, 32), rows_dev)
        his = pl.ds(pl.multiple_of((1 - c) * rows_dev, 32), rows_dev)
        for src_col, dst_col, n in cuts:
            src, dst = fin.at[his, pl.ds(src_col, n)], out.at[:, dcol(dst_col, n)]
            remote(src, dst, i_his, part).start()
            pltpu.make_async_copy(fin.at[mine, pl.ds(src_col, n)], dst, rsem.at[i_mine]).start()
        whole = fin.at[mine]
        waits.append(lambda: wait_in(whole, i_mine))
        waits.append(lambda: wait_in(whole, i_his))
        ends.append(lambda: remote(whole, whole, i_his, part).wait_send())

    def place_d(i, n):
        return lambda fin: put(fin, r["o_down"].at[pl.ds(n * i, n), :])

    def place_u(j):
        return lambda fin: by_core(fin, [(0, (2 * j + c) * ffb, ffb)], r["o_up"])

    def place_o(fin):
        by_core(fin, [(0, c * hcols, hcols)], r["o_out"])

    def place_q(p):
        cuts = [(t * LANES, t * width + c * hcols + p * LANES, LANES) for t in range(3)]
        return lambda fin: by_core(fin, cuts, r["o_qkv"])

    red = {}
    dn_rows = ffb // 4
    for i in range(4):
        name = "d%d" % i
        red[name] = reduce_unit(
            name, r["g_d"], ffb, dn_rows * i, dn_rows, slice(None), place_d(i, dn_rows)
        )
    for j in range(4):
        name = "u%d" % j
        red[name] = reduce_unit(
            name, r["g_u"], rows_chip, 0, rows_chip, pl.ds(ffb * j, ffb), place_u(j)
        )
    red["o"] = reduce_unit("o", r["g_o"], rows_chip, 0, rows_chip, slice(None), place_o)
    units = list(red)
    units += ["q%d" % p for p in range(pairs)]
    for p in range(pairs):
        name = "q%d" % p
        red[name] = reduce_unit(
            name, r["g_q"].at[p], rows_chip, 0, rows_chip, slice(None), place_q(p)
        )

    turn = iter(SCHEDULE)

    def stages():
        for at in next(turn):
            if at < 6 * len(units):
                red[units[at // 6]][at % 6]()
            else:
                tokens_out(at - 6 * len(units))

    xs, xr, mixacc = r["xs"], r["xr"], r["mixacc"]

    def down(blk, first, into, fresh):
        w_rows = pl.ds(pl.multiple_of(ffb * blk, LANES), ffb)
        for k in range(2):
            ls = pl.ds(quarter * k, quarter)
            out = nn(active[pl.ds(first + quarter * k, quarter), dcol(ffb * blk, ffb)], W["d"][w_rows, :])
            into[ls, :] = out if fresh else into[ls, :] + out

    for copy in c_copies:
        copy.wait_recv()
    gt = 256

    def grad_down_step(i, _):
        cols = dcol(gt * i, gt)
        r["g_d"][pl.ds(pl.multiple_of(gt * i, gt), gt), :] = tn(active[:, cols], cb[...]).astype(BF)
        return 0

    lax.fori_loop(0, ffh // gt, grad_down_step, 0)
    wait_in(rows(W["d"], ffb * q, ffb), local_d)
    stages()

    for i, blk in enumerate((q, qx, qy)):
        down(blk, oth0, xs.at[1], i == 0)
    stages()
    ag_last("d0")
    ag_last("d1")
    down(qd, oth0, xs.at[1], False)
    mix_copies = [
        send(xs.at[1, pl.ds(quarter * k, quarter), :], xr.at[1, pl.ds(quarter * k, quarter), :], part)
        for k in range(2)
    ]
    for k in range(2):
        ls = pl.ds(quarter * k, quarter)
        mixacc[ls, :] = nn(active[pl.ds(own0 + quarter * k, quarter), :], W["d"][...])

    def from_chip(buf, out, i0, k, first, n, last):
        zd = 2 * c + k
        src = buf.at[pl.ds(quarter * k + first, n), :]
        is_self = (zd == z) & (zk == c)
        dev = (zd, s - c + zk)
        dst = out.at[zh, pl.ds(first, n), :]

        @pl.when(is_self)
        def _():
            pltpu.make_async_copy(src, dst, rsem.at[i0 + zh]).start()

        @pl.when(jnp.logical_not(is_self))
        def _():
            remote(src, dst, i0 + zh, dev, i0 + k).start()

        def end():
            @pl.when(jnp.logical_not(is_self))
            def _():
                whole = buf.at[pl.ds(quarter * k, quarter), :]
                remote(whole, out.at[zh], i0 + zh, dev, i0 + k).wait_send()

        if last:
            ends.append(end)
            waits.append(functools.partial(wait_in, out.at[k], i0 + k))

    mo_i, to_i = sems(2), sems(2)
    mixb = r["mixb"]
    for k in range(2):
        ls = pl.ds(quarter * k, quarter)
        mix_copies[k].wait_recv()
        mixb[ls, :] = (middle[ls, :] + mixacc[ls, :] + xr[1, ls, :]).astype(BF)

    def tokens_out(at):
        if at < 2:
            from_chip(mixb, r["o_mixed"], mo_i, at, 0, quarter, True)
        else:
            piece, n = at - 2, quarter // 4
            from_chip(r["gtb"], r["o_gt"], to_i, piece // 4, piece % 4 * n, n, piece % 4 == 3)

    stages()

    fd = 512

    for k in range(4):

        def d_up_step(i, _):
            ts = pl.ds(quarter * k, quarter)
            cols = dcol(fd * i, fd)
            da = nt(cb[ts, :], W["d"][pl.ds(pl.multiple_of(fd * i, LANES), fd), :])
            du[ts, cols] = (da * du[ts, cols].astype(F32)).astype(BF)
            return 0

        lax.fori_loop(0, ffh // fd, d_up_step, 0)
        stages()

    def exchange(n, product_of):
        copies = []
        for k in range(2):
            ls = pl.ds(quarter * k, quarter)
            xs[n % 2, ls, :] = product_of(pl.ds(oth0 + quarter * k, quarter))
            copies.append(send(xs.at[n % 2, ls, :], xr.at[n % 2, ls, :], part))
        return copies

    dn2_copies = exchange(0, lambda ts: nt(du[ts, :], W["u"][...]))
    stages()
    dbr, gsum = r["dbr"], r["gsum"]
    gain_acc = jnp.zeros((1, width), F32)
    db_copies = []
    for k in range(2):
        ts = pl.ds(own0 + quarter * k, quarter)
        ls = pl.ds(quarter * k, quarter)
        dn = nt(du[ts, :], W["u"][...])
        dn2_copies[k].wait_recv()
        dn = dn + xr[0, ls, :]
        cen, rstd = row_stats(middle[ls, :])
        n = cen * rstd
        gain_acc = gain_acc + jnp.sum(dn * n, axis=0, keepdims=True)
        dmid = cb[ts, :].astype(F32) + norm_back(dn, n, rstd, gain_two)
        mixacc[ls, :] = dmid
        dbr[ts, :] = dmid.astype(BF)
        mine = rows(dbr, own0 + quarter * k, quarter)
        db_copies.append(send(mine, mine, part))
        stages()
    gsum[0, :, width:] = gain_acc

    for j in range(2):

        def grad_up_step(i, _):
            cols = dcol(gt * i, gt)
            out = tn(n2[:, cols], du[:, pl.ds(half_u * j, half_u)]).astype(BF)
            r["g_u"][pl.ds(pl.multiple_of(gt * i, gt), gt), pl.ds(half_u * j, half_u)] = out
            return 0

        lax.fori_loop(0, width // gt, grad_up_step, 0)
        stages()

    for copy in db_copies:
        copy.wait_recv()
    datt = r["datt"]

    def datt_step(k, _):
        ts = pl.ds(pl.multiple_of(quarter * k, quarter), quarter)
        w_rows = W["o"][pl.ds(pl.multiple_of(c * hcols, LANES), hcols), :]
        datt[ts, :] = nt(dbr[ts, :], w_rows).astype(BF)
        return 0

    lax.fori_loop(0, 4, datt_step, 0)
    stages()

    dk, dv = r["dk"], r["dv"]
    sel = (
        lax.broadcasted_iota(jnp.int32, (8, LANES), 0)
        == lax.div(lax.broadcasted_iota(jnp.int32, (8, LANES), 1), LANES // 2)
    ).astype(F32)

    def attend_back(p):
        dk[...] = jnp.zeros_like(dk)
        dv[...] = jnp.zeros_like(dv)
        for b in range(4):
            at, k0, n = base[b]
            qs = pl.ds(quarter * b, quarter)
            ks = pl.ds(quarter * k0, n)
            query = qkv[qs, dcol(p * LANES, LANES)] * jnp.asarray(scale, BF)
            key = qkv[ks, dcol(hcols + p * LANES, LANES)]
            value = qkv[ks, dcol(2 * hcols + p * LANES, LANES)]
            d_att = datt[qs, dcol(p * LANES, LANES)]
            att = attended[qs, dcol(c * hcols + p * LANES, LANES)]
            delta = nt(sel, d_att.astype(F32) * att.astype(F32), lax.Precision.HIGHEST)
            allowed = mask[pl.ds(at, n), :]
            d_query = None
            for h in range(2):
                q_h = query * head_bf[h]
                d_h = d_att * head_bf[h]
                sm = nt(key, q_h) * allowed
                mag = jnp.abs(sm)
                level = lev[2 * p + h, :, qs]
                prob = jnp.exp(mag - level)
                low = jnp.exp(-level)
                sign = jnp.clip(sm * HUGE, -1.0, 1.0)
                weight = (sign * (prob - low)).astype(BF)
                d_signed = nt(value, d_h)
                d_score = (prob * allowed * (d_signed - sign * delta[h : h + 1, :])).astype(BF)
                dv[ks, :] += nn(weight, d_h)
                dk[ks, :] += nn(d_score, q_h)
                out = tn(d_score, key * head_bf[h])
                d_query = out if d_query is None else d_query + out
            qkv[qs, dcol(p * LANES, LANES)] = (d_query * scale).astype(BF)
            stages()
        qkv[:, dcol(hcols + p * LANES, LANES)] = dk[...].astype(BF)
        qkv[:, dcol(2 * hcols + p * LANES, LANES)] = dv[...].astype(BF)

    def grad_qkv(p):
        def step(i, _):
            cols = dcol(gt * i, gt)
            d_pair = jnp.concatenate(
                [qkv[:, dcol(t * hcols + p * LANES, LANES)] for t in range(3)], axis=1
            )
            out = tn(normed[:, cols], d_pair).astype(BF)
            r["g_q"][p, pl.ds(pl.multiple_of(gt * i, gt), gt), :] = out
            return 0

        lax.fori_loop(0, width // gt, step, 0)

    def grad_out_step(i, _):
        cols = dcol(gt * i, gt)
        out = tn(attended[:, cols], dbr[:, dcol(c * hcols, hcols)]).astype(BF)
        r["g_o"][pl.ds(pl.multiple_of(gt * i, gt), gt), :] = out
        return 0

    lax.fori_loop(0, width // gt, grad_out_step, 0)
    stages()
    attend_back(0)
    grad_qkv(0)
    stages()
    attend_back(1)
    grad_qkv(1)
    stages()
    attend_back(2)

    for copy in dn2_copies:
        copy.wait_send()
        ends.remove(copy.wait_send)
    dn1_copies = exchange(2, lambda ts: nt(qkv[ts, :], W["q"][...]))
    stages()
    grad_qkv(2)
    stages()
    gtb = r["gtb"]
    gain_acc = jnp.zeros((1, width), F32)
    for k in range(2):
        ts = pl.ds(own0 + quarter * k, quarter)
        ls = pl.ds(quarter * k, quarter)
        dn = nt(qkv[ts, :], W["q"][...])
        dn1_copies[k].wait_recv()
        dn = dn + xr[0, ls, :]
        cen, rstd = row_stats(xb[ls, :].astype(F32))
        n = cen * rstd
        gain_acc = gain_acc + jnp.sum(dn * n, axis=0, keepdims=True)
        gtb[ls, :] = (mixacc[ls, :] + norm_back(dn, n, rstd, gain_one)).astype(BF)
        stages()
    gsum[0, :, :width] = gain_acc

    g3, g4, g5 = sems(), sems(), sems()
    g_copy = send(gsum.at[0], gsum.at[1], part)
    stages()

    g_copy.wait_recv()
    gsum[2] = gsum[0] + gsum[1]
    g_copy = send(gsum.at[2], gsum.at[3], nx)
    stages()
    g_copy.wait_recv()
    gsum[4] = gsum[2] + gsum[3]
    g_copy = send(gsum.at[4], gsum.at[5], ny)
    stages()
    g_copy.wait_recv()
    gsum[6] = gsum[4] + gsum[5]

    @pl.when(edge)
    def _():
        remote(gsum.at[6], gsum.at[7], g3, zp).start()

    stages()

    @pl.when(mid)
    def _():
        remote(gsum.at[6], gsum.at[7], g3, zp).wait_recv()
        gsum[8] = gsum[6] + gsum[7]
        remote(gsum.at[8], gsum.at[9], g4, zm).start()

    stages()

    @pl.when(mid)
    def _():
        remote(gsum.at[8], gsum.at[9], g4, zm).wait_recv()
        gsum[10] = gsum[8] + gsum[9]
        remote(gsum.at[10], gsum.at[10], g5, zp).start()

    stages()

    @pl.when(mid)
    def _():
        remote(gsum.at[8], gsum.at[9], g4, zm).wait_send()
        remote(gsum.at[10], gsum.at[10], g5, zp).wait_send()

    @pl.when(edge)
    def _():
        remote(gsum.at[10], gsum.at[10], g5, zp).wait_recv()
        remote(gsum.at[6], gsum.at[7], g3, zp).wait_send()

    pick = (
        lax.broadcasted_iota(jnp.int32, (width, LANES), 0)
        == lax.broadcasted_iota(jnp.int32, (width, LANES), 1) + rows_dev * s
    ).astype(F32)
    for k in range(2):
        vec = jnp.broadcast_to(gsum[10][:, width * k : width * (k + 1)], (8, width))
        r["o_gains"][k : k + 1, :] = nn(vec, pick, lax.Precision.HIGHEST)[0:1, :rows_dev]
    for wait in waits:
        wait()
    for end in ends:
        end()
    assert used[0] <= N_SEMS, used[0]


def per_device_fast(tokens, segments, w_qkv, w_out, w_up, w_down, gain_one, gain_two, cotangent):
    micro, _, quarter, width = tokens.shape
    rows_dev = w_qkv.shape[0]
    ff = w_up.shape[1]
    ffb = w_down.shape[0]
    half, length = 2 * quarter, 4 * quarter
    hcols, ffh, rows_chip = width // 2, ff // 2, 2 * rows_dev
    pairs = hcols // LANES
    pcols = 3 * LANES
    scratch = {}

    def vm(name, shape, dtype=BF):
        scratch[name] = pltpu.VMEM(shape, dtype)

    vm("w_q", (width, pairs * pcols))
    vm("w_o", (width, width))
    vm("w_u", (width, ffh))
    vm("w_d", (ffh, width))
    vm("segs", (4, 1, quarter), jnp.int32)
    vm("segc", (length, LANES), F32)
    vm("mask", (9 * quarter, quarter), F32)
    vm("xb", (half, width))
    vm("cb", (length, width))
    vm("gains", (7, 1, 2 * width), F32)
    vm("gsum", (11, 1, 2 * width), F32)
    vm("normed", (length, width))
    vm("qkv", (length, pairs * pcols))
    vm("lev", (2 * pairs, 1, length), F32)
    vm("attended", (length, width))
    vm("middle", (half, width), F32)
    vm("n2", (length, width))
    vm("active", (length, ffh))
    vm("du", (length, ffh))
    vm("xs", (2, half, width), F32)
    vm("xr", (2, half, width), F32)
    vm("mixb", (half, width))
    vm("mixacc", (half, width), F32)
    vm("gtb", (half, width))
    vm("dbr", (length, width))
    vm("datt", (length, hcols))
    vm("dk", (length, LANES), F32)
    vm("dv", (length, LANES), F32)
    vm("g_d", (ffh, width))
    vm("g_u", (width, ffh))
    vm("g_o", (width, hcols))
    vm("g_q", (pairs, width, pcols))
    pieces = [("d%d" % i, ffb // 4, width) for i in range(4)]
    pieces += [("u%d" % j, rows_chip, ffb) for j in range(4)]
    pieces += [("o", rows_chip, hcols)]
    pieces += [("q%d" % p, rows_chip, pcols) for p in range(pairs)]
    for name, blk, cols in pieces:
        vm(name + "1", (4, blk // 2, cols))
        vm(name + "2", (2, blk // 2, cols))
        vm(name + "3", (blk, cols))
        vm(name + "4", (blk, cols))
    scratch["ssem"] = pltpu.SemaphoreType.DMA((N_SEMS,))
    scratch["rsem"] = pltpu.SemaphoreType.DMA((N_SEMS,))
    outs = {
        "o_mixed": ((micro, quarter, width), BF),
        "o_gt": ((micro, quarter, width), BF),
        "o_qkv": ((rows_dev, 3 * width), BF),
        "o_out": ((rows_dev, width), BF),
        "o_up": ((rows_dev, ff), BF),
        "o_down": ((ffb, width), BF),
        "o_gains": ((2, rows_dev), F32),
    }
    ins = ["tok", "seg", "wqkv", "wout", "wup", "wdn", "g1", "g2", "cot"]
    names = ins + list(outs) + list(scratch)
    hbm = pl.BlockSpec(memory_space=pl.ANY)
    vmem = pl.BlockSpec(memory_space=pltpu.VMEM)
    tokens_all = 2 * half
    flops = 6 * half * (width * (4 * width + 2 * ff)) + 14 * 9 * 6 * quarter * quarter * 128
    got = pl.pallas_call(
        functools.partial(layer_kernel, names),
        out_shape=[jax.ShapeDtypeStruct(*v) for v in outs.values()],
        in_specs=[vmem if k in ("g1", "g2") else hbm for k in ins],
        out_specs=[vmem if k == "o_gains" else hbm for k in outs],
        scratch_shapes=list(scratch.values()),
        compiler_params=pltpu.CompilerParams(
            collective_id=0, has_side_effects=True, vmem_limit_bytes=VMEM_LIMIT
        ),
        cost_estimate=pl.CostEstimate(
            flops=flops, bytes_accessed=20 * tokens_all * width, transcendentals=0
        ),
    )(
        tokens[:, 0],
        segments.reshape(micro, 1, quarter),
        w_qkv,
        w_out,
        w_up,
        w_down,
        gain_one[None],
        gain_two[None],
        cotangent[:, 0],
    )
    mixed, grad_tokens, g_qkv, g_out, g_up, g_down, g_gains = got
    return (
        mixed[:, None],
        grad_tokens.astype(F32)[:, None],
        g_qkv.astype(F32),
        g_out.astype(F32),
        g_up.astype(F32),
        g_down.astype(F32),
        g_gains[0],
        g_gains[1],
    )


VMEM_LIMIT = 62 * 1024 * 1024


def solution(mesh):
    placed = (
        P(None, "shard", "seq", None),
        P(None, "shard", "seq"),
        P("shard", None),
        P("shard", None),
        P("shard", None),
        P("shard", None),
        P("shard"),
        P("shard"),
        P(None, "shard", "seq", None),
    )
    chip_sized = mesh.shape["seq"] == 4 and mesh.shape["shard"] == 8
    return jax.shard_map(
        per_device_fast if chip_sized else per_device,
        mesh=mesh,
        in_specs=placed,
        out_specs=(
            P(None, "shard", "seq", None),
            P(None, "shard", "seq", None),
            P("shard", None),
            P("shard", None),
            P("shard", None),
            P("shard", None),
            P("shard"),
            P("shard"),
        ),
        check_vma=False,
    )
```
